32 devices in a mesh: dp: 8 (over z, y), tensor: 4 (over x, core).
Axes of the slice: x: 2, y: 2, z: 4, core: 2. Of those that a mesh axis runs over, the one named last changes fastest.
Arguments:
- tokens: bfloat16 [16384, 768], P('dp'), may hold values from -6 to 6
- documents: int32 [16384], P('dp'), may hold values from 0 to 63, never falling along the last dimension, each value on 1 to 1024 neighbouring positions
- attn_gain: float32 [768], replicated, may hold values from 0.5 to 1.5
- qkv_weight: bfloat16 [768, 3, 768], P(None, None, 'tensor'), may hold values from -0.21875 to 0.21875
- out_weight: bfloat16 [768, 768], P('tensor'), may hold values from -1.75 to 1.75
- mlp_gain: float32 [768], replicated, may hold values from 0.5 to 1.5
- up_weight: bfloat16 [768, 3072], P(None, 'tensor'), may hold values from -0.21875 to 0.21875
- down_weight: bfloat16 [3072, 768], P('tensor'), may hold values from -0.15625 to 0.15625
- cotangent: bfloat16 [16384, 768], P('dp'), may hold values from -6 to 6
Outputs:
- block_out: bfloat16 [16384, 768], P('dp')
- input_grad: float32 [16384, 768], P('dp')
- attn_gain_grad: float32 [768], P('dp')
- qkv_grad: float32 [768, 3, 768], P('dp', None, 'tensor')
- out_grad: float32 [768, 768], P('tensor', 'dp')
- mlp_gain_grad: float32 [768], P('dp')
- up_grad: float32 [768, 3072], P('dp', 'tensor')
- down_grad: float32 [3072, 768], P('tensor', 'dp')
The draws below stay inside these ranges and needn't reach their ends.
Inputs may be any that keep to these rules, and one draw needn't show every extreme that they name: `documents`: document numbers never fall along the rows; a document holds 1 to 1024 rows, and one holds exactly 1024.
All inputs are finite; a program needn't handle non-finite values.
Results may differ from the reference program's by a relative error of at most 0.018.
Values may be sent and summed in bfloat16 or wider, within the bound.
No kernel may reach another device: no remote copies, remote signals or barrier semaphores. Data moves between devices by JAX's collectives and lax.ppermute only.
A program may use at most 128 MiB of HBM per device.

```python
import math
import jax
import jax.numpy as jnp
import numpy as np
from jax import lax

D = 768
HEADS = 12
HEAD = 64
FF = 3072
SEQ = 1024
TOK_DEV = 2048
TOKENS = 16384
N_DP = 8
N_TENSOR = 4


def spiked(entries, stream_key, source, target, parts, factor):
    def block_of(axis_at):
        return (jnp.arange(entries.shape[axis_at]) // (entries.shape[axis_at] // parts)).reshape((-1,) + (1,) * (entries.ndim - 1 - axis_at))

    near = jax.random.permutation(stream_key, parts)[block_of(target)]
    far = (block_of(target) + parts // 2) % parts
    return jnp.where((block_of(source) == near) | (block_of(source) == far), factor * entries, entries)


def block_scale(stream_key, extent, shards, low, largest):
    loudness = 1.0
    for position, blocks in shards:
        draws = jax.random.uniform(jax.random.fold_in(jax.random.fold_in(stream_key, 6), position), (blocks,), jnp.float32, low / len(shards), largest / len(shards))
        loudness = loudness * jnp.repeat(jnp.exp(draws), extent[position] // blocks).reshape((-1,) + (1,) * (len(extent) - 1 - position))
    return loudness


def split_up(amount, total, reach, skew):
    portions = [(1 << 20) // math.isqrt(grade ** skew) + 1 for grade in range(2, amount + 1)]
    rest, counts = total - reach - (amount - 1), [1] * (amount - 1)
    while rest > 0:
        movable = [i for i in range(amount - 1) if counts[i] < reach]
        pool, budget = sum([portions[i] for i in movable]), rest
        for i in movable:
            extra = min(reach - counts[i], max(1, budget * portions[i] // pool), rest)
            counts[i] = counts[i] + extra
            rest = rest - extra
    return np.array([reach] + counts)


def ragged(key, count, total, bound, slope):
    if count == 2:
        one = jax.random.randint(key, (), max(1, total - bound), min(bound, total - 1) + 1)
        return jnp.stack([one, total - one])
    sizes = jnp.asarray(split_up(count, total, bound, slope), jnp.int32)
    pairs = (count - 1) // 2
    giver, receiver = sizes[1:1 + 2 * pairs:2], sizes[2:2 + 2 * pairs:2]
    room = jnp.minimum(giver - 1, bound - receiver)
    shifted = jax.random.randint(jax.random.fold_in(key, 1), (pairs,), 0, 1 << 20) % (room + 1)
    sizes = sizes.at[1:1 + 2 * pairs:2].set(giver - shifted).at[2:2 + 2 * pairs:2].set(receiver + shifted)
    return sizes[jax.random.permutation(jax.random.fold_in(key, 2), count)]


def scatter_about(rng, dims, width, limit, cuts=(), dtype=jnp.bfloat16):
    factor_of = block_scale(rng, dims, cuts, -0.22, 0.18) if cuts else 1.0
    entries = jax.random.normal(rng, dims, jnp.float32) * width * factor_of
    return jnp.minimum(jnp.maximum(entries, -limit), limit).astype(dtype)


def noise_with(key, dims, width, limit, cuts, heavy, kind=jnp.bfloat16):
    array = width * jax.random.normal(key, dims, jnp.float32)
    if cuts:
        array = array * block_scale(key, dims, cuts, -0.22, 0.18)
    return jnp.clip(spiked(array, jax.random.fold_in(key, 3), *heavy), -limit, limit).astype(kind)


def setup_inputs(seed: int = 0) -> dict:
    key_of = jax.random.split(jax.random.key(seed), 10)
    tokens = scatter_about(key_of[0], (TOKENS, D), 1.0, 6.0, ((0, 8),))
    documents = jnp.searchsorted(jnp.cumsum(ragged(key_of[1], 4 * TOKENS // SEQ, TOKENS, SEQ, 2)), jnp.arange(TOKENS), side="right").astype(jnp.int32)
    attn_gain = jnp.clip(1.0 + 0.1 * jax.random.normal(key_of[2], (D,), jnp.float32), 0.5, 1.5)
    qkv_weight = scatter_about(key_of[3], (D, 3, D), D ** -0.5, 0.21875, ((2, 4),))
    out_weight = scatter_about(key_of[4], (D, D), (D // 64) ** -0.5, 1.75, ((0, 4),))
    mlp_gain = jnp.clip(1.0 + 0.1 * jax.random.normal(key_of[5], (D,), jnp.float32), 0.5, 1.5)
    up_weight = scatter_about(key_of[6], (D, FF), D ** -0.5, 0.21875, ((1, 4),))
    down_weight = scatter_about(key_of[7], (FF, D), (FF // 2) ** -0.5, 0.15625, ((0, 4),))
    cotangent = noise_with(key_of[8], (TOKENS, D), 1.0, 6.0, ((0, 8),), (0, 1, 8, 2.0))
    return {"tokens": tokens, "documents": documents, "attn_gain": attn_gain, "qkv_weight": qkv_weight, "out_weight": out_weight, "mlp_gain": mlp_gain, "up_weight": up_weight, "down_weight": down_weight, "cotangent": cotangent}


@jax.custom_vjp
def low(v):
    return lax.optimization_barrier(v.astype(jnp.bfloat16)).astype(jnp.float32)

@jax.custom_vjp
def low_back(v):
    return v

def low_keep(v):
    return (low(v), None)

def low_pass(kept, grad):
    return (grad,)

def back_keep(v):
    return (v, None)

def back_low(kept, grad):
    return (low(grad),)
low.defvjp(low_keep, low_pass)
low_back.defvjp(back_keep, back_low)
highest = lax.Precision.HIGHEST

def layer_norm(inputs, gain):
    average = lax.optimization_barrier(jnp.mean(inputs, -1, keepdims=True))
    centered = inputs - average
    variance = lax.optimization_barrier(jnp.mean(centered * centered, -1, keepdims=True))
    return centered * lax.rsqrt(variance + 1e-05) * gain

def attend(pieces):
    queries, key_rows, values, doc_row = pieces
    scores = jnp.einsum('qhe,khe->hqk', queries, key_rows, precision=highest) * 0.125
    scores = low_back(scores)
    positions = jnp.arange(SEQ)
    allowed = (doc_row[:, None] == doc_row[None, :]) & (positions[None, :] <= positions[:, None])
    scores = jnp.where(allowed[None], scores, -jnp.inf)
    row_max = lax.optimization_barrier(jnp.max(scores, -1, keepdims=True))
    exponent = jnp.exp(scores - row_max)
    weights = exponent / lax.optimization_barrier(jnp.sum(exponent, -1, keepdims=True))
    return jnp.einsum('hqk,khe->qhe', low(weights), values, precision=highest)

def block_forward(inputs, doc_rows, attn_gain, qkv_weight, out_weight, mlp_gain, up_weight, down_weight):
    row_count = inputs.shape[0]
    seq_count = row_count // SEQ
    attn_in = low(layer_norm(inputs, attn_gain))
    projected = jnp.einsum('td,dpc->tpc', attn_in, qkv_weight, precision=highest)
    projected = low_back(low(projected))
    shaped = projected.reshape(seq_count, SEQ, 3, HEADS, HEAD)
    attended = lax.map(jax.checkpoint(attend), (shaped[:, :, 0], shaped[:, :, 1], shaped[:, :, 2], doc_rows.reshape(seq_count, SEQ)))
    attended = low_back(low(attended.reshape(row_count, D)))
    group_width = D // N_TENSOR
    partial_value = jnp.einsum('tgc,gcd->tgd', attended.reshape(row_count, N_TENSOR, group_width), out_weight.reshape(N_TENSOR, group_width, D), precision=highest)
    hidden = inputs + lax.optimization_barrier(jnp.sum(low_back(low(partial_value)), 1))
    mlp_in = low(layer_norm(hidden, mlp_gain))
    up_proj = low_back(jnp.dot(mlp_in, up_weight, precision=highest))
    activated = low(jax.nn.gelu(up_proj, approximate=True))
    unit_width = FF // N_TENSOR
    partial_two = jnp.einsum('tgf,gfd->tgd', activated.reshape(row_count, N_TENSOR, unit_width), down_weight.reshape(N_TENSOR, unit_width, D), precision=highest)
    return hidden + lax.optimization_barrier(jnp.sum(low_back(low(partial_two)), 1))

def reference(tokens, documents, attn_gain, qkv_weight, out_weight, mlp_gain, up_weight, down_weight, cotangent):
    params = (attn_gain, qkv_weight.astype(jnp.float32), out_weight.astype(jnp.float32), mlp_gain, up_weight.astype(jnp.float32), down_weight.astype(jnp.float32))

    def advance(running, pieces):
        token_rows, doc_rows, grad_rows = pieces

        def forward(inputs, *weights):
            return block_forward(inputs, doc_rows, *weights)
        result, pullback = jax.vjp(forward, token_rows.astype(jnp.float32), *params)
        gradients = pullback(grad_rows.astype(jnp.float32))
        running = tuple((before + gradient for before, gradient in zip(running, gradients[1:])))
        return (running, (result.astype(jnp.bfloat16), gradients[0]))
    zeros = tuple((jnp.zeros(parameter.shape, jnp.float32) for parameter in params))
    running, outputs = lax.scan(advance, zeros, (tokens.reshape(N_DP, TOK_DEV, D), documents.reshape(N_DP, TOK_DEV), cotangent.reshape(N_DP, TOK_DEV, D)))
    block_out = outputs[0].reshape(TOKENS, D)
    input_grad = outputs[1].reshape(TOKENS, D)
    return (block_out, input_grad, running[0], running[1], running[2], running[3], running[4], running[5])
```

```python
import functools
import math

import jax
import jax.numpy as jnp
from jax import lax
from jax.experimental import pallas as pl
from jax.experimental.pallas import tpu as pltpu
from jax.sharding import PartitionSpec as P

HEAD = 64
SEQ = 1024
BLK = 256
NBLK = SEQ // BLK
EPS = 1e-05
VMEM_BYTES = 56 * 1024 * 1024
F32 = jnp.float32
BF16 = jnp.bfloat16
C0 = math.sqrt(2.0 / math.pi)
C1 = 0.044715
NEG = -1e30

NN = (((1,), (0,)), ((), ()))
NT = (((1,), (1,)), ((), ()))
TN = (((0,), (0,)), ((), ()))


def mm(a, b, dims):
    return lax.dot_general(a, b, dims, preferred_element_type=F32)


def normed(rows):
    centered = rows - jnp.mean(rows, -1, keepdims=True)
    inverse = lax.rsqrt(jnp.mean(centered * centered, -1, keepdims=True) + EPS)
    return centered * inverse, inverse


def norm_back(grad_rows, unit, inverse, gain):
    scaled = grad_rows * gain
    first = jnp.mean(scaled, -1, keepdims=True)
    second = jnp.mean(scaled * unit, -1, keepdims=True)
    return inverse * (scaled - first - unit * second)


def head_mask(rows, width, h):
    lane = lax.broadcasted_iota(jnp.int32, (rows, width), 1)
    return (lane >= h * HEAD) & (lane < (h + 1) * HEAD)


def doc_columns(docs_ref, base):
    row = docs_ref[0, :, base : base + BLK]
    column = jnp.transpose(jnp.broadcast_to(row, (128, BLK)))
    return jnp.concatenate([column] * (BLK // 128), 1)


def flipped(index, bits):
    return sum(((index >> b) & 1) << (bits - 1 - b) for b in range(bits))


def put_pieces(out_ref, me, grad, lane=0):
    pieces, rows, _ = out_ref.shape
    width = grad.shape[1]
    for p in range(pieces):
        out_ref[flipped(p, pieces.bit_length() - 1) ^ me, :, lane : lane + width] = grad[p * rows : (p + 1) * rows].astype(BF16)


def forward_block(q_ref, k_ref, v_ref, docs_ref, lse_ref, qb):
    heads = q_ref.shape[1] // HEAD
    width = q_ref.shape[1]
    base = qb * BLK
    queries = q_ref[base : base + BLK] * jnp.asarray(0.125, BF16)
    docs_q = doc_columns(docs_ref, base)
    at_row = lax.broadcasted_iota(jnp.int32, (BLK, BLK), 0)
    at_col = lax.broadcasted_iota(jnp.int32, (BLK, BLK), 1)
    total = jnp.zeros((BLK, width), F32)
    for h in range(heads):
        mask = head_mask(BLK, width, h)
        q_h = jnp.where(mask, queries, jnp.zeros_like(queries))
        scores = []
        for kb in range(qb + 1):
            keys = slice(kb * BLK, (kb + 1) * BLK)
            s = mm(q_h, k_ref[keys], NT)
            allowed = docs_q == docs_ref[0, :, keys]
            if kb == qb:
                allowed = allowed & (at_col <= at_row)
            scores.append(jnp.where(allowed, s, NEG))
        top = functools.reduce(jnp.maximum, scores)
        row_max = jnp.max(top, -1, keepdims=True)
        out = jnp.zeros((BLK, width), F32)
        sums = jnp.zeros((BLK, BLK), F32)
        for kb in range(qb + 1):
            e = jnp.exp(scores[kb] - row_max)
            sums = sums + e
            out = out + mm(e.astype(BF16), v_ref[kb * BLK : (kb + 1) * BLK], NN)
        row_sum = jnp.sum(sums, -1, keepdims=True)
        total = jnp.where(mask, out / row_sum, total)
        lse = row_max + jnp.log(row_sum)
        lse_ref[h : h + 1, base : base + BLK] = jnp.transpose(jnp.broadcast_to(lse, (BLK, 128)))[:1]
    return total.astype(BF16)


def first_kernel(s_ref, x_ref, gain_ref, w_ref, docs_ref, n_ref, q_ref, k_ref, v_ref, att_ref, lse_ref):
    for qb in range(NBLK):
        rows = slice(qb * BLK, (qb + 1) * BLK)
        unit, _ = normed(x_ref[rows].astype(F32))
        n = (unit * gain_ref[...]).astype(BF16)
        n_ref[rows] = n
        for i, ref in enumerate((q_ref, k_ref, v_ref)):
            ref[rows] = mm(n, w_ref[i], NT).astype(BF16)
        att_ref[rows] = forward_block(q_ref, k_ref, v_ref, docs_ref, lse_ref, qb)


def second_kernel(
    s_ref, n_ref, w_ref, docs_ref, att_one_ref, wo_one_ref, wo_ref, q_ref, k_ref, v_ref, att_ref, lse_ref, sum_ref
):
    for qb in range(NBLK):
        rows = slice(qb * BLK, (qb + 1) * BLK)
        n = n_ref[rows]
        for i, ref in enumerate((q_ref, k_ref, v_ref)):
            ref[rows] = mm(n, w_ref[i], NT).astype(BF16)
        att = forward_block(q_ref, k_ref, v_ref, docs_ref, lse_ref, qb)
        att_ref[rows] = att
        total = mm(att_one_ref[rows], wo_one_ref[...], NN) + mm(att, wo_ref[...], NN)
        sum_ref[rows] = total.astype(BF16)


def gelu_pair(u):
    square = u * u
    th = jnp.tanh(u * (C0 + (C0 * C1) * square))
    half = 0.5 * u
    act = half + half * th
    slope = 0.5 + 0.5 * th + half * (1.0 - th * th) * (C0 + (3.0 * C0 * C1) * square)
    return act, slope


def mlp_rows(mlp_in, cot, up_ref, down_ref, down_acc, up_acc):
    act, slope = gelu_pair(mm(mlp_in, up_ref[...], NN))
    act = act.astype(BF16)
    act_grad = mm(cot, down_ref[...], NT)
    up_in = (act_grad * slope).astype(BF16)
    out = mm(act, down_ref[...], NN)
    back = mm(up_in, up_ref[...], NT)
    down_acc[...] += mm(cot, act, TN)
    up_acc[...] += mm(mlp_in, up_in, TN)
    return out, back


def mlp_first_kernel(
    s_ref, me_ref, x_ref, a_ref, b_ref, gain_ref, cot_ref, up_ref, down_ref,
    hidden_ref, in_ref, out_ref, back_ref, down_grad_ref, up_grad_ref, down_acc, up_acc,
):
    step = pl.program_id(0)

    @pl.when(step == 0)
    def _():
        down_acc[...] = jnp.zeros_like(down_acc)
        up_acc[...] = jnp.zeros_like(up_acc)

    hidden = x_ref[...].astype(F32) + (a_ref[...].astype(F32) + b_ref[...].astype(F32))
    hidden_ref[...] = hidden
    unit, _ = normed(hidden)
    mlp_in = (unit * gain_ref[...]).astype(BF16)
    in_ref[...] = mlp_in
    out, back = mlp_rows(mlp_in, cot_ref[...], up_ref, down_ref, down_acc, up_acc)
    out_ref[...] = out
    back_ref[...] = back

    @pl.when(step == NBLK - 1)
    def _():
        put_pieces(down_grad_ref, me_ref[0], down_acc)
        put_pieces(up_grad_ref, me_ref[0], up_acc)


def mlp_second_kernel(
    s_ref, me_ref, in_ref, out_one_ref, back_one_ref, cot_ref, up_ref, down_ref,
    out_ref, back_ref, down_grad_ref, up_grad_ref, down_acc, up_acc,
):
    step = pl.program_id(0)

    @pl.when(step == 0)
    def _():
        down_acc[...] = jnp.zeros_like(down_acc)
        up_acc[...] = jnp.zeros_like(up_acc)

    out, back = mlp_rows(in_ref[...], cot_ref[...], up_ref, down_ref, down_acc, up_acc)
    out_ref[...] = (out_one_ref[...] + out).astype(BF16)
    back_ref[...] = (back_one_ref[...] + back).astype(BF16)

    @pl.when(step == NBLK - 1)
    def _():
        put_pieces(down_grad_ref, me_ref[0], down_acc)
        put_pieces(up_grad_ref, me_ref[0], up_acc)


def middle_kernel(
    s_ref, me_ref, hidden_ref, a_ref, b_ref, cot_ref, gain_ref, wo_one_ref, wo_two_ref, att_one_ref, att_two_ref,
    grad_ref, da_one_ref, da_two_ref, go_one_ref, go_two_ref, acc_one, acc_two,
):
    step = pl.program_id(0)

    @pl.when(step == 0)
    def _():
        acc_one[...] = jnp.zeros_like(acc_one)
        acc_two[...] = jnp.zeros_like(acc_two)

    unit, inverse = normed(hidden_ref[...])
    grad = a_ref[...].astype(F32) + b_ref[...].astype(F32)
    hidden_grad = cot_ref[...].astype(F32) + norm_back(grad, unit, inverse, gain_ref[...])
    grad_ref[...] = hidden_grad
    low = hidden_grad.astype(BF16)
    da_one_ref[...] = mm(low, wo_one_ref[...], NT).astype(BF16)
    da_two_ref[...] = mm(low, wo_two_ref[...], NT).astype(BF16)
    acc_one[...] += mm(low, att_one_ref[...], TN)
    acc_two[...] += mm(low, att_two_ref[...], TN)

    @pl.when(step == NBLK - 1)
    def _():
        put_pieces(go_one_ref, me_ref[0], acc_one)
        put_pieces(go_two_ref, me_ref[0], acc_two)


def attend_back(
    add_first, s_ref, me_ref, q_ref, k_ref, v_ref, att_ref, da_ref, lse_ref, docs_ref, n_ref, w_ref, go_ref, *rest
):
    if add_first:
        before_ref, sum_ref, grad_ref, dq_acc, dk_ref, dv_ref = rest
    else:
        sum_ref, grad_ref, dq_acc, dk_ref, dv_ref = rest
    width = q_ref.shape[1]
    heads = width // HEAD
    eighth = jnp.asarray(0.125, BF16)
    prod = da_ref[...].astype(F32) * att_ref[...].astype(F32)
    pick_lane = lax.broadcasted_iota(jnp.int32, (8, width), 1)
    pick_row = lax.broadcasted_iota(jnp.int32, (8, width), 0)
    pick = jnp.where((pick_lane >= pick_row * HEAD) & (pick_lane < (pick_row + 1) * HEAD), 1.0, 0.0).astype(F32)
    inner = lax.dot_general(pick, prod, NT, precision=lax.Precision.HIGHEST, preferred_element_type=F32)
    at_row = lax.broadcasted_iota(jnp.int32, (BLK, BLK), 0)
    at_col = lax.broadcasted_iota(jnp.int32, (BLK, BLK), 1)
    dq_acc[...] = jnp.zeros_like(dq_acc)
    masks = [head_mask(BLK, width, h) for h in range(heads)]

    def only(block, h):
        return jnp.where(masks[h], block, jnp.zeros_like(block))

    for kb in range(NBLK):
        keys = slice(kb * BLK, (kb + 1) * BLK)
        k_blk = k_ref[keys]
        v_blk = v_ref[keys]
        k_scaled = k_blk * eighth
        docs_k = doc_columns(docs_ref, kb * BLK)
        dk = jnp.zeros((BLK, width), F32)
        dv = jnp.zeros((BLK, width), F32)
        for qb in range(kb, NBLK):
            queries = slice(qb * BLK, (qb + 1) * BLK)
            q_blk = q_ref[queries] * eighth
            da_blk = da_ref[queries]
            allowed = docs_k == docs_ref[0, :, queries]
            if kb == qb:
                allowed = allowed & (at_row <= at_col)
            dq = jnp.zeros((BLK, width), F32)
            for h in range(heads):
                q_h = only(q_blk, h)
                da_h = only(da_blk, h)
                s = jnp.where(allowed, mm(k_blk, q_h, NT) - lse_ref[h : h + 1, queries], NEG)
                p = jnp.exp(s)
                dp = mm(v_blk, da_h, NT)
                ds = (p * (dp - inner[h : h + 1, queries])).astype(BF16)
                dv = dv + mm(p.astype(BF16), da_h, NN)
                dk = dk + mm(ds, q_h, NN)
                dq = dq + mm(ds, only(k_scaled, h), TN)
            dq_acc[queries] += dq
        dk_ref[keys] = dk.astype(BF16)
        dv_ref[keys] = dv.astype(BF16)

    n = n_ref[...]
    put_pieces(grad_ref, me_ref[0], mm(n, dq_acc[...].astype(BF16), TN), 0)
    put_pieces(grad_ref, me_ref[0], mm(n, dk_ref[...], TN), width)
    put_pieces(grad_ref, me_ref[0], mm(n, dv_ref[...], TN), 2 * width)
    pieces = grad_ref.shape[0]
    for p in range(pieces):
        grad_ref[p, :, 3 * width :] = go_ref[p]
    for qb in range(NBLK):
        rows = slice(qb * BLK, (qb + 1) * BLK)
        total = mm(dq_acc[rows].astype(BF16), w_ref[0], NN)
        total = total + mm(dk_ref[rows], w_ref[1], NN)
        total = total + mm(dv_ref[rows], w_ref[2], NN)
        if add_first:
            sum_ref[rows] = (before_ref[rows] + total).astype(BF16)
        else:
            sum_ref[rows] = total


def last_kernel(s_ref, x_ref, gain_ref, grad_ref, a_ref, b_ref, out_ref, low_ref):
    unit, inverse = normed(x_ref[...].astype(F32))
    grad = a_ref[...].astype(F32) + b_ref[...].astype(F32)
    out = grad_ref[...] + norm_back(grad, unit, inverse, gain_ref[...])
    out_ref[...] = out
    low_ref[...] = out.astype(BF16)


def block_kernel(s_ref, hidden_ref, a_ref, b_ref, out_ref):
    out_ref[...] = (hidden_ref[...] + (a_ref[...].astype(F32) + b_ref[...].astype(F32))).astype(BF16)


def place_kernel(s_ref, c_ref, own_ref, one_ref, two_ref, out_ref):
    step = pl.program_id(0)
    half = step % 2

    @pl.when(step // 2 == s_ref[0])
    def _():
        out_ref[...] = own_ref[...].astype(out_ref.dtype)

    @pl.when((step // 2 != s_ref[0]) & (half == c_ref[0]))
    def _():
        out_ref[...] = one_ref[...].astype(out_ref.dtype)

    @pl.when((step // 2 != s_ref[0]) & (half != c_ref[0]))
    def _():
        out_ref[...] = two_ref[...].astype(out_ref.dtype)


def whole(shape):
    return pl.BlockSpec(shape, lambda *_: (0,) * len(shape))


def rows_of(width):
    return pl.BlockSpec((BLK, width), lambda i, *_: (i, 0))


def rows_at_s(width):
    return pl.BlockSpec((BLK, width), lambda i, s_ref, *_: (s_ref[0] * NBLK + i, 0))


def sds(shape, dtype):
    return jax.ShapeDtypeStruct(shape, dtype)


def call(kernel, scalars, grid, in_specs, out_specs, out_shape, args, name, flops, scratch=()):
    moved = sum(a.size * a.dtype.itemsize for a in args) + sum(
        math.prod(o.shape) * jnp.dtype(o.dtype).itemsize for o in out_shape
    )
    return pl.pallas_call(
        kernel,
        out_shape=out_shape,
        grid_spec=pltpu.PrefetchScalarGridSpec(
            num_scalar_prefetch=len(scalars),
            grid=grid,
            in_specs=in_specs,
            out_specs=out_specs,
            scratch_shapes=list(scratch),
        ),
        compiler_params=pltpu.CompilerParams(vmem_limit_bytes=VMEM_BYTES),
        cost_estimate=pl.CostEstimate(flops=int(flops), bytes_accessed=int(moved), transcendentals=0),
        name=name,
    )(*scalars, *args)


def on_device(
    tokens, documents, attn_gain, qkv_weight, out_weight, mlp_gain, up_weight, down_weight, cotangent, *, n_dp, n_tensor
):
    d = tokens.shape[1]
    width = qkv_weight.shape[2]
    units = up_weight.shape[1]
    heads = width // HEAD
    piece = d // n_dp
    t = lax.axis_index("tensor")
    me = lax.axis_index("dp").astype(jnp.int32)
    s = (t // 2).astype(jnp.int32)
    c = (t % 2).astype(jnp.int32)
    bits = n_dp.bit_length() - 1
    s1, me1, c1 = s.reshape(1), flipped(me, bits).reshape(1), c.reshape(1)
    across = [(i, i ^ 2) for i in range(n_tensor)]
    inside = [(i, i ^ 1) for i in range(n_tensor)]

    def over_x(v):
        return lax.ppermute(v, "tensor", across)

    def over_core(v):
        return lax.ppermute(v, "tensor", inside)

    w_one = jnp.transpose(qkv_weight, (1, 2, 0))
    w_two = over_x(w_one)
    wo_one = out_weight
    wo_two = over_x(wo_one)
    up_one = up_weight
    up_two = over_x(up_one)
    down_one = down_weight
    down_two = over_x(down_one)

    docs = documents.astype(F32).reshape(tokens.shape[0] // SEQ, 1, SEQ)
    docs_spec = pl.BlockSpec((1, 1, SEQ), lambda i, s_ref, *_: (s_ref[0], 0, 0))
    gain_one = attn_gain.reshape(1, d)
    gain_two = mlp_gain.reshape(1, d)
    seq_spec = pl.BlockSpec((SEQ, d), lambda i, s_ref, *_: (s_ref[0], 0))
    full_spec = whole((SEQ, d))
    head_spec = whole((SEQ, width))
    head_out = sds((SEQ, width), BF16)
    lse_out = sds((8, SEQ), F32)
    w_spec = whole((3, width, d))
    wo_spec = whole((width, d))
    one_step = (1,)
    attn_flops = 2 * heads * 2 * SEQ * SEQ * HEAD
    qkv_flops = 2 * SEQ * d * 3 * width

    n, q_one, k_one, v_one, att_one, lse_one = call(
        first_kernel, (s1,), one_step,
        [seq_spec, whole((1, d)), w_spec, docs_spec],
        [full_spec, head_spec, head_spec, head_spec, head_spec, whole((8, SEQ))],
        [sds((SEQ, d), BF16), head_out, head_out, head_out, head_out, lse_out],
        (tokens, gain_one, w_one, docs), "attend_own", qkv_flops + attn_flops,
    )
    q_two, k_two, v_two, att_two, lse_two, attn_sum = call(
        second_kernel, (s1,), one_step,
        [full_spec, w_spec, docs_spec, head_spec, wo_spec, wo_spec],
        [head_spec, head_spec, head_spec, head_spec, whole((8, SEQ)), full_spec],
        [head_out, head_out, head_out, head_out, lse_out, sds((SEQ, d), BF16)],
        (n, w_two, docs, att_one, wo_one, wo_two), "attend_other", qkv_flops + attn_flops,
    )
    attn_recv = over_core(attn_sum)

    rows = rows_of(d)
    x_rows = rows_at_s(d)
    gain_spec = whole((1, d))
    square = whole((d, units))
    square_t = whole((units, d))
    pieces = n_dp
    grad_spec = whole((pieces, piece, units))
    grad_out = sds((pieces, piece, units), BF16)
    accs = [pltpu.VMEM((d, units), F32), pltpu.VMEM((d, units), F32)]
    mlp_flops = 7 * 2 * SEQ * d * units
    hidden, mlp_in, out_one, back_one, down_grad_one, up_grad_one = call(
        mlp_first_kernel, (s1, me1), (NBLK,),
        [x_rows, rows, rows, gain_spec, x_rows, square, square_t],
        [rows, rows, rows, rows, grad_spec, grad_spec],
        [sds((SEQ, d), F32), sds((SEQ, d), BF16), sds((SEQ, d), F32), sds((SEQ, d), F32), grad_out, grad_out],
        (tokens, attn_sum, attn_recv, gain_two, cotangent, up_one, down_one), "mlp_own", mlp_flops, accs,
    )
    mlp_sum, back_sum, down_grad_two, up_grad_two = call(
        mlp_second_kernel, (s1, me1), (NBLK,),
        [rows, rows, rows, x_rows, square, square_t],
        [rows, rows, grad_spec, grad_spec],
        [sds((SEQ, d), BF16), sds((SEQ, d), BF16), grad_out, grad_out],
        (mlp_in, out_one, back_one, cotangent, up_two, down_two), "mlp_other", mlp_flops, accs,
    )
    back_recv = over_core(back_sum)
    mlp_recv = over_core(mlp_sum)

    head_rows = rows_of(width)
    go_spec = whole((pieces, piece, width))
    go_out = sds((pieces, piece, width), BF16)
    hidden_grad, da_one, da_two, go_one, go_two = call(
        middle_kernel, (s1, me1), (NBLK,),
        [rows, rows, rows, x_rows, gain_spec, wo_spec, wo_spec, head_rows, head_rows],
        [rows, head_rows, head_rows, go_spec, go_spec],
        [sds((SEQ, d), F32), head_out, head_out, go_out, go_out],
        (hidden, back_sum, back_recv, cotangent, gain_two, wo_one, wo_two, att_one, att_two), "middle",
        4 * 2 * SEQ * d * width,
        [pltpu.VMEM((d, width), F32), pltpu.VMEM((d, width), F32)],
    )

    qkv_spec = whole((pieces, piece, 4 * width))
    qkv_out = sds((pieces, piece, 4 * width), BF16)
    back_specs = [head_spec] * 5 + [whole((8, SEQ)), docs_spec, full_spec, w_spec, go_spec]
    back_scratch = [pltpu.VMEM((SEQ, width), F32), pltpu.VMEM((SEQ, width), BF16), pltpu.VMEM((SEQ, width), BF16)]
    back_flops = 2 * qkv_flops + 5 * attn_flops // 2
    in_one, qkv_grad_two = call(
        functools.partial(attend_back, False), (s1, me1), one_step, back_specs, [full_spec, qkv_spec],
        [sds((SEQ, d), F32), qkv_out],
        (q_two, k_two, v_two, att_two, da_two, lse_two, docs, n, w_two, go_two), "attend_back_other",
        back_flops, back_scratch,
    )
    in_sum, qkv_grad_one = call(
        functools.partial(attend_back, True), (s1, me1), one_step, back_specs + [full_spec], [full_spec, qkv_spec],
        [sds((SEQ, d), BF16), qkv_out],
        (q_one, k_one, v_one, att_one, da_one, lse_one, docs, n, w_one, go_one, in_one), "attend_back_own",
        back_flops, back_scratch,
    )
    in_recv = over_core(in_sum)

    input_own, input_low = call(
        last_kernel, (s1,), (NBLK,),
        [x_rows, gain_spec, rows, rows, rows], [rows, rows],
        [sds((SEQ, d), F32), sds((SEQ, d), BF16)],
        (tokens, gain_one, hidden_grad, in_sum, in_recv), "norm_back", 0,
    )
    (block_own,) = call(
        block_kernel, (s1,), (NBLK,), [rows] * 3, [rows], [sds((SEQ, d), BF16)],
        (hidden, mlp_sum, mlp_recv), "block_out", 0,
    )

    def place(own, low, dtype):
        half = lax.dynamic_slice_in_dim(low, c * (SEQ // 2), SEQ // 2, 0)
        one = over_x(half)
        two = over_core(one)
        half_rows = SEQ // 2
        (out,) = call(
            place_kernel, (s1, c1), (4,),
            [pl.BlockSpec((half_rows, d), lambda i, *_: (i % 2, 0)), whole((half_rows, d)), whole((half_rows, d))],
            [pl.BlockSpec((half_rows, d), lambda i, *_: (i, 0))], [sds((2 * SEQ, d), dtype)],
            (own, one, two), "place", 0,
        )
        return out

    block_out = place(block_own, block_own, BF16)
    input_grad = place(input_own, input_low, F32)

    def reduce(one, two):
        total = one.astype(F32) + over_x(two).astype(F32)
        for bit in range(bits):
            count = n_dp >> (bit + 1)
            send = total[count:].astype(BF16)
            recv = lax.ppermute(send, "dp", [(i, i ^ (1 << bit)) for i in range(n_dp)])
            total = total[:count] + recv.astype(F32)
        return total[0]

    down_part = reduce(down_grad_one, down_grad_two)
    up_part = reduce(up_grad_one, up_grad_two)
    last_part = reduce(qkv_grad_one, qkv_grad_two)
    qkv_flat = last_part[:, : 3 * width]
    qkv_part = qkv_flat.reshape(piece, 3, width)
    out_part = last_part[:, 3 * width :].T

    start = me * piece
    w_mine = lax.dynamic_slice_in_dim(qkv_weight, start, piece, 0).reshape(piece, 3 * width).astype(F32)
    up_mine = lax.dynamic_slice_in_dim(up_weight, start, piece, 0).astype(F32)
    gains = jnp.stack([jnp.sum(w_mine * qkv_flat, 1), jnp.sum(up_mine * up_part, 1)])
    gains = gains + over_core(gains)
    gains = gains + over_x(gains)
    attn_gain_part = gains[0] / lax.dynamic_slice_in_dim(attn_gain, start, piece, 0)
    mlp_gain_part = gains[1] / lax.dynamic_slice_in_dim(mlp_gain, start, piece, 0)
    return (block_out, input_grad, attn_gain_part, qkv_part, out_part, mlp_gain_part, up_part, down_part.T)


def solution(mesh):
    in_specs = (
        P("dp", None),
        P("dp"),
        P(),
        P(None, None, "tensor"),
        P("tensor", None),
        P(),
        P(None, "tensor"),
        P("tensor", None),
        P("dp", None),
    )
    out_specs = (
        P("dp", None),
        P("dp", None),
        P("dp"),
        P("dp", None, "tensor"),
        P("tensor", "dp"),
        P("dp"),
        P("dp", "tensor"),
        P("tensor", "dp"),
    )
    body = functools.partial(on_device, n_dp=mesh.shape["dp"], n_tensor=mesh.shape["tensor"])
    return jax.shard_map(body, mesh=mesh, in_specs=in_specs, out_specs=out_specs, check_vma=False)
```

```python
import functools
import math

import jax
import jax.numpy as jnp
from jax import lax
from jax.experimental import pallas as pl
from jax.experimental.pallas import tpu as pltpu
from jax.sharding import PartitionSpec as P

HEAD = 64
SEQ = 1024
BLK = 256
NBLK = SEQ // BLK
EPS = 1e-05
VMEM_BYTES = 14 * 1024 * 1024
F32 = jnp.float32
BF16 = jnp.bfloat16
C0 = math.sqrt(2.0 / math.pi)
C1 = 0.044715
NEG = -1e30

NN = (((1,), (0,)), ((), ()))
NT = (((1,), (1,)), ((), ()))
TN = (((0,), (0,)), ((), ()))


def mm(a, b, dims):
    return lax.dot_general(a, b, dims, preferred_element_type=F32)


def normed(rows):
    centered = rows - jnp.mean(rows, -1, keepdims=True)
    inverse = lax.rsqrt(jnp.mean(centered * centered, -1, keepdims=True) + EPS)
    return centered * inverse, inverse


def norm_back(grad_rows, unit, inverse, gain):
    scaled = grad_rows * gain
    first = jnp.mean(scaled, -1, keepdims=True)
    second = jnp.mean(scaled * unit, -1, keepdims=True)
    return inverse * (scaled - first - unit * second)


def head_mask(rows, width, h):
    lane = lax.broadcasted_iota(jnp.int32, (rows, width), 1)
    return (lane >= h * HEAD) & (lane < (h + 1) * HEAD)


def mapped(index, order):
    bits = len(order)
    return sum(((index >> b) & 1) << (bits - 1 - i) for i, b in enumerate(order))


def put_pieces(all_ref, me, grad, order, base=0, lane=0):
    rows = all_ref.shape[1]
    width = grad.shape[1]
    for p in range(grad.shape[0] // rows):
        place = mapped(p + base // rows, order) ^ me
        all_ref[place, :, lane : lane + width] = grad[p * rows : (p + 1) * rows].astype(BF16)


def block(i):
    return slice(i * BLK, (i + 1) * BLK)


def send_out(pairs, sems, base=0):
    copies = [pltpu.make_async_copy(src, dst, sems.at[base + i]) for i, (src, dst) in enumerate(pairs)]
    for one in copies:
        one.start()
    return copies


def wait_all(copies):
    for one in copies:
        one.wait()


def pieces_out(all_ref, refs):
    count = refs[0].shape[0]
    return [(all_ref.at[i * count : (i + 1) * count], ref) for i, ref in enumerate(refs)]


def quarters_in(whole_ref, color, pieces):
    rows = pieces[0].shape[0]
    at = [2 * color, 2 * color + 1, 2 * (1 - color), 2 * (1 - color) + 1]
    return [(ref, whole_ref.at[pl.ds(pl.multiple_of(i * rows, 16), rows)]) for i, ref in zip(at, pieces)]


def forward_scores(q_ref, k_ref, qb, h):
    width = q_ref.shape[1]
    rows = slice(qb * BLK, (qb + 1) * BLK)
    queries = q_ref[rows] * jnp.asarray(0.125, BF16)
    q_h = jnp.where(head_mask(BLK, width, h), queries, jnp.zeros_like(queries))
    return mm(q_h, k_ref[: (qb + 1) * BLK], NT)


def forward_allowed(docs_ref, qb):
    base, end = qb * BLK, (qb + 1) * BLK
    column = jnp.transpose(jnp.broadcast_to(docs_ref[0, :, base:end], (128, BLK)))
    docs_q = jnp.concatenate([column] * (end // 128), 1)
    at_row = lax.broadcasted_iota(jnp.int32, (BLK, end), 0) + base
    at_col = lax.broadcasted_iota(jnp.int32, (BLK, end), 1)
    return (docs_q == docs_ref[0, :, :end]) & (at_col <= at_row)


def forward_attention(q_ref, k_ref, v_ref, docs_ref, lse_ref, att_ref, ahead=2):
    width = q_ref.shape[1]
    heads = width // HEAD
    items = [(qb, h) for qb in range(NBLK) for h in range(heads)]
    pending = [forward_scores(q_ref, k_ref, *items[i]) for i in range(ahead)]
    for i, (qb, h) in enumerate(items):
        rows = slice(qb * BLK, (qb + 1) * BLK)
        if i + ahead < len(items):
            pending.append(forward_scores(q_ref, k_ref, *items[i + ahead]))
        if h == 0:
            allowed = forward_allowed(docs_ref, qb)
            total = jnp.zeros((BLK, width), F32)
        s = jnp.where(allowed, pending.pop(0), NEG)
        row_max = jnp.max(s, -1, keepdims=True)
        e = jnp.exp(s - row_max)
        row_sum = jnp.sum(e, -1, keepdims=True)
        out = mm(e.astype(BF16), v_ref[: (qb + 1) * BLK], NN)
        total = jnp.where(head_mask(BLK, width, h), out / row_sum, total)
        lse = row_max + jnp.log(row_sum)
        lse_ref[h : h + 1, rows] = jnp.transpose(jnp.broadcast_to(lse, (BLK, 128)))[:1]
        if h == heads - 1:
            att_ref[rows] = total.astype(BF16)


def over_blocks(body):
    def step(i, carry):
        body(pl.ds(pl.multiple_of(i * BLK, BLK), BLK))
        return carry

    lax.fori_loop(0, NBLK, step, 0)


def project(n_ref, w_ref, refs):
    width = refs[0].shape[1]
    for i, ref in enumerate(refs):
        ref[...] = mm(n_ref[...], w_ref[i * width : (i + 1) * width], NT).astype(BF16)


def pick_kernel(color_ref, *refs):
    count = (len(refs) - 1) // 3
    sems = refs[-1]
    pairs = []
    for i in range(count):
        src = refs[i]
        rows = src.shape[0] // 4
        for j in range(2):
            at = pl.ds(pl.multiple_of((2 * color_ref[0] + j) * rows, 16), rows)
            pairs.append((src.at[at], refs[count + 2 * i + j]))
    wait_all(send_out(pairs, sems))


def first_kernel(
    s_ref, x_ref, gain_ref, w_ref, docs_ref,
    n_ref, att_ref, n_out, q_out, k_out, v_out, att_out, lse_ref, x_vmem, q_ref, k_ref, v_ref, sems,
):
    mine = pl.ds(pl.multiple_of(s_ref[0] * SEQ, SEQ), SEQ)
    wait_all(send_out([(x_ref.at[mine], x_vmem)], sems, 5))
    for i in range(NBLK):
        unit, _ = normed(x_vmem[block(i)].astype(F32))
        n_ref[block(i)] = (unit * gain_ref[...]).astype(BF16)
    project(n_ref, w_ref, (q_ref, k_ref, v_ref))
    copies = send_out([(n_ref, n_out), (q_ref, q_out), (k_ref, k_out), (v_ref, v_out)], sems)
    forward_attention(q_ref, k_ref, v_ref, docs_ref, lse_ref, att_ref)
    wait_all(copies + send_out([(att_ref, att_out)], sems, 4))


def second_kernel(
    color_ref, n_ref, wa_ref, wb_ref, wc_ref, wd_ref, oa_ref, ob_ref, oc_ref, od_ref, docs_ref, att_one_ref, wo_one_ref,
    w_out, wo_out, q_out, k_out, v_out, att_out, lse_ref, sum_out,
    w_ref, wo_ref, q_ref, k_ref, v_ref, att_ref, sum_ref, sems,
):
    color = color_ref[0]
    loads = send_out(quarters_in(w_ref, color, (wa_ref, wb_ref, wc_ref, wd_ref)), sems, 6)
    loads_wo = send_out(quarters_in(wo_ref, color, (oa_ref, ob_ref, oc_ref, od_ref)), sems, 10)
    wait_all(loads)
    project(n_ref, w_ref, (q_ref, k_ref, v_ref))
    wait_all(loads_wo)
    copies = send_out([(w_ref, w_out), (wo_ref, wo_out), (q_ref, q_out), (k_ref, k_out), (v_ref, v_out)], sems)
    forward_attention(q_ref, k_ref, v_ref, docs_ref, lse_ref, att_ref)
    copies += send_out([(att_ref, att_out)], sems, 5)
    for i in range(NBLK):
        total = mm(att_one_ref[block(i)], wo_one_ref[...], NN) + mm(att_ref[block(i)], wo_ref[...], NN)
        sum_ref[block(i)] = total.astype(BF16)
        copies += send_out([(sum_ref.at[block(i)], sum_out.at[block(i)])], sems, 14 + i)
    wait_all(copies)


def gelu_pair(u):
    square = u * u
    th = jnp.tanh(u * (C0 + (C0 * C1) * square))
    half = 0.5 * u
    act = half + half * th
    slope = 0.5 + 0.5 * th + half * (1.0 - th * th) * (C0 + (3.0 * C0 * C1) * square)
    return act, slope


def mlp_rows(rows, in_ref, cot, up_ref, down_ref, act_ref, back_in_ref):
    act, slope = gelu_pair(mm(in_ref[rows], up_ref[...], NN))
    act = act.astype(BF16)
    act_ref[rows] = act
    back_in = (mm(cot, down_ref[...], NT) * slope).astype(BF16)
    back_in_ref[rows] = back_in
    return mm(act, down_ref[...], NN), mm(back_in, up_ref[...], NT)


def mlp_grads(orders, me_refs, in_ref, cot_ref, act_ref, back_in_ref, down_refs, up_refs):
    wide = cot_ref.shape[1] // 2

    def one_half(j, carry):
        base = pl.multiple_of(j * wide, 128)
        lanes = pl.ds(base, wide)
        put_pieces(down_refs, me_refs[0][0], mm(cot_ref[:, lanes], act_ref[...], TN), orders[0], j * wide)
        put_pieces(up_refs, me_refs[1][0], mm(in_ref[:, lanes], back_in_ref[...], TN), orders[1], j * wide)
        return carry

    lax.fori_loop(0, 2, one_half, 0)


def mlp_first_kernel(
    orders, s_ref, me_down_ref, me_up_ref, x_any, cot_any, a_any, b_any, up_any, down_any, gain_ref,
    hidden_any, in_ref, out_ref, back_ref, down_keep, down_send, up_keep, up_send,
    x_ref, cot_ref, both_ref, up_ref, down_ref, hidden_ref, act_ref, back_in_ref, down_all, up_all, sems,
):
    at = [pl.ds(pl.multiple_of(s_ref[0] * SEQ + i * BLK, BLK), BLK) for i in range(NBLK)]
    loads = []
    for i in range(NBLK):
        rows = block(i)
        pairs = [(x_any.at[at[i]], x_ref.at[rows])]
        pairs += [(src.at[rows], both_ref.at[j, rows]) for j, src in enumerate((a_any, b_any))]
        loads.append(send_out(pairs, sems, 3 * i))
    mine = pl.ds(pl.multiple_of(s_ref[0] * SEQ, SEQ), SEQ)
    loads_more = send_out([(up_any, up_ref), (cot_any.at[mine], cot_ref), (down_any, down_ref)], sems, 3 * NBLK)
    copies = []
    for i in range(NBLK):
        wait_all(loads[i])
        rows = block(i)
        hidden = x_ref[rows].astype(F32) + (both_ref[0, rows].astype(F32) + both_ref[1, rows].astype(F32))
        hidden_ref[rows] = hidden
        copies += send_out([(hidden_ref.at[rows], hidden_any.at[rows])], sems, 3 * NBLK + 3 + i)
        unit, _ = normed(hidden)
        in_ref[rows] = (unit * gain_ref[...]).astype(BF16)
    wait_all(loads_more)

    def one_block(rows):
        out, back = mlp_rows(rows, in_ref, cot_ref[rows], up_ref, down_ref, act_ref, back_in_ref)
        out_ref[rows] = out.astype(BF16)
        back_ref[rows] = back.astype(BF16)

    over_blocks(one_block)
    mlp_grads(orders, (me_down_ref, me_up_ref), in_ref, cot_ref, act_ref, back_in_ref, down_all, up_all)
    pairs = pieces_out(down_all, (down_keep, down_send)) + pieces_out(up_all, (up_keep, up_send))
    wait_all(copies + send_out(pairs, sems, 4 * NBLK + 3))


def mlp_second_kernel(
    orders, s_ref, me_down_ref, me_up_ref, color_ref, in_ref, out_one_ref, back_one_ref, cot_any,
    ua_ref, ub_ref, uc_ref, ud_ref, da_ref, db_ref, dc_ref, dd_ref,
    out_any, both_any, down_keep, down_send, up_keep, up_send,
    cot_ref, up_ref, down_ref, out_ref, back_ref, act_ref, back_in_ref, down_all, up_all, sems,
):
    color = color_ref[0]
    mine = pl.ds(pl.multiple_of(s_ref[0] * SEQ, SEQ), SEQ)
    loads = send_out(quarters_in(up_ref, color, (ua_ref, ub_ref, uc_ref, ud_ref)), sems)
    loads += send_out([(cot_any.at[mine], cot_ref)], sems, 4)
    loads += send_out(quarters_in(down_ref, color, (da_ref, db_ref, dc_ref, dd_ref)), sems, 5)
    wait_all(loads)

    def one_block(rows):
        out, back = mlp_rows(rows, in_ref, cot_ref[rows], up_ref, down_ref, act_ref, back_in_ref)
        out_ref[rows] = (out_one_ref[rows].astype(F32) + out).astype(BF16)
        back_ref[rows] = (back_one_ref[rows].astype(F32) + back).astype(BF16)

    over_blocks(one_block)
    copies = send_out([(back_ref, both_any.at[0]), (back_ref, both_any.at[1]), (out_ref, out_any)], sems, 9)
    mlp_grads(orders, (me_down_ref, me_up_ref), in_ref, cot_ref, act_ref, back_in_ref, down_all, up_all)
    pairs = pieces_out(down_all, (down_keep, down_send)) + pieces_out(up_all, (up_keep, up_send))
    wait_all(copies + send_out(pairs, sems, 12))


def middle_kernel(
    order, s_ref, me_ref, hidden_any, cot_any, both_any, wo_one_any, wo_two_any, att_one_any, att_two_any, gain_ref,
    grad_any, da_one_ref, da_two_ref, go_one_any, go_two_any,
    hidden_ref, cot_ref, both_ref, wo_one_ref, wo_two_ref, att_one_ref, att_two_ref, grad_ref, low_ref, go_one, go_two, sems,
):
    at = [pl.ds(pl.multiple_of(s_ref[0] * SEQ + i * BLK, BLK), BLK) for i in range(NBLK)]
    loads = []
    for i in range(NBLK):
        rows = block(i)
        pairs = [
            (hidden_any.at[rows], hidden_ref.at[rows]),
            (both_any.at[:, rows], both_ref.at[:, rows]),
            (cot_any.at[at[i]], cot_ref.at[rows]),
        ]
        loads.append(send_out(pairs, sems, 3 * i))
        if i == 0:
            loads_wo = send_out([(wo_one_any, wo_one_ref), (wo_two_any, wo_two_ref)], sems, 3 * NBLK)
    loads_att = send_out([(att_one_any, att_one_ref), (att_two_any, att_two_ref)], sems, 3 * NBLK + 2)
    copies = []
    for i in range(NBLK):
        rows = block(i)
        wait_all(loads[i])
        unit, inverse = normed(hidden_ref[rows])
        grad = both_ref[0, rows].astype(F32) + both_ref[1, rows].astype(F32)
        hidden_grad = cot_ref[rows].astype(F32) + norm_back(grad, unit, inverse, gain_ref[...])
        grad_ref[rows] = hidden_grad
        copies += send_out([(grad_ref.at[rows], grad_any.at[rows])], sems, 3 * NBLK + 4 + i)
        low = hidden_grad.astype(BF16)
        low_ref[rows] = low
        if i == 0:
            wait_all(loads_wo)
        da_one_ref[rows] = mm(low, wo_one_ref[...], NT).astype(BF16)
        da_two_ref[rows] = mm(low, wo_two_ref[...], NT).astype(BF16)
    wait_all(loads_att)
    put_pieces(go_one, me_ref[0], mm(low_ref[...], att_one_ref[...], TN), order)
    put_pieces(go_two, me_ref[0], mm(low_ref[...], att_two_ref[...], TN), order)
    wait_all(copies + send_out([(go_one, go_one_any), (go_two, go_two_any)], sems, 4 * NBLK + 4))


def attend_back(
    add_first, order, me_ref, q_ref, k_ref, v_ref, att_ref, da_ref, lse_ref, docs_ref, n_ref, w_ref, go_ref, *rest
):
    if add_first:
        before_ref, both_any = rest[:2]
    else:
        (sum_ref,) = rest[:1]
    *grad_refs, dq_ref, dk_ref, dv_ref, ds_ref, all_ref, low_ref, sems = rest[1 + add_first :]
    width = q_ref.shape[1]
    heads = width // HEAD
    eighth = jnp.asarray(0.125, BF16)
    prod = da_ref[...].astype(F32) * att_ref[...].astype(F32)
    pick_lane = lax.broadcasted_iota(jnp.int32, (8, width), 1)
    pick_row = lax.broadcasted_iota(jnp.int32, (8, width), 0)
    pick = jnp.where((pick_lane >= pick_row * HEAD) & (pick_lane < (pick_row + 1) * HEAD), 1.0, 0.0).astype(F32)
    inner = lax.dot_general(pick, prod, NT, precision=lax.Precision.HIGHEST, preferred_element_type=F32)
    for kb in range(NBLK):
        keys = slice(kb * BLK, (kb + 1) * BLK)
        start = kb * BLK
        count = SEQ - start
        column = jnp.transpose(jnp.broadcast_to(docs_ref[0, :, keys], (128, BLK)))
        docs_k = jnp.concatenate([column] * (count // 128), 1)
        at_row = lax.broadcasted_iota(jnp.int32, (BLK, count), 0)
        at_col = lax.broadcasted_iota(jnp.int32, (BLK, count), 1)
        allowed = (docs_k == docs_ref[0, :, start:]) & (at_row <= at_col)
        dk = jnp.zeros((BLK, width), F32)
        dv = jnp.zeros((BLK, width), F32)
        for h in range(heads):
            mask = head_mask(count, width, h)
            q_h = jnp.where(mask, q_ref[start:] * eighth, jnp.zeros((count, width), BF16))
            da_h = jnp.where(mask, da_ref[start:], jnp.zeros((count, width), BF16))
            s = mm(k_ref[keys], q_h, NT) - lse_ref[h : h + 1, start:]
            p = jnp.exp(jnp.where(allowed, s, NEG))
            dp = mm(v_ref[keys], da_h, NT)
            ds = (p * (dp - inner[h : h + 1, start:])).astype(BF16)
            ds_ref[h, keys, start:] = ds
            dv = dv + mm(p.astype(BF16), da_h, NN)
            dk = dk + mm(ds, q_h, NN)
        dk_ref[keys] = dk.astype(BF16)
        dv_ref[keys] = dv.astype(BF16)
    for qb in range(NBLK):
        rows = slice(qb * BLK, (qb + 1) * BLK)
        end = (qb + 1) * BLK
        dq = jnp.zeros((BLK, width), F32)
        for h in range(heads):
            k_h = jnp.where(head_mask(end, width, h), k_ref[:end] * eighth, jnp.zeros((end, width), BF16))
            dq = dq + mm(ds_ref[h, :end, rows], k_h, TN)
        dq_ref[rows] = dq.astype(BF16)
    n = n_ref[...]
    for i, ref in enumerate((dq_ref, dk_ref, dv_ref)):
        put_pieces(all_ref, me_ref[0], mm(n, ref[...], TN), order, 0, i * width)
    all_ref[:, :, 3 * width :] = go_ref[...]
    copies = send_out(pieces_out(all_ref, grad_refs), sems)
    for qb in range(NBLK):
        rows = slice(qb * BLK, (qb + 1) * BLK)
        total = mm(dq_ref[rows], w_ref[:width], NN)
        total = total + mm(dk_ref[rows], w_ref[width : 2 * width], NN)
        total = total + mm(dv_ref[rows], w_ref[2 * width :], NN)
        if add_first:
            low_ref[rows] = (before_ref[rows] + total).astype(BF16)
            to = [(low_ref.at[rows], both_any.at[j, rows]) for j in range(2)]
            copies += send_out(to, sems, 4 + 2 * qb)
        else:
            sum_ref[rows] = total
    wait_all(copies)


def last_kernel(
    s_ref, c_ref, x_any, both_any, grad_any, gain_ref, out_any, low_ref,
    x_ref, both_ref, grad_ref, out_ref, sems,
):
    at = [pl.ds(pl.multiple_of(s_ref[0] * SEQ + i * BLK, BLK), BLK) for i in range(NBLK)]
    loads = []
    for i in range(NBLK):
        rows = block(i)
        pairs = [
            (x_any.at[at[i]], x_ref.at[rows]),
            (both_any.at[:, rows], both_ref.at[:, rows]),
            (grad_any.at[rows], grad_ref.at[rows]),
        ]
        loads.append(send_out(pairs, sems, 3 * i))
    stores = []
    for i in range(NBLK):
        rows = block(i)
        wait_all(loads[i])
        unit, inverse = normed(x_ref[rows].astype(F32))
        grad = both_ref[0, rows].astype(F32) + both_ref[1, rows].astype(F32)
        out = grad_ref[rows] + norm_back(grad, unit, inverse, gain_ref[...])
        out_ref[rows] = out
        stores += send_out([(out_ref.at[rows], out_any.at[at[i]])], sems, 3 * NBLK + i)
    half = low_ref.shape[0]
    low_ref[...] = out_ref[pl.ds(pl.multiple_of(c_ref[0] * half, half), half)].astype(BF16)
    wait_all(stores)


def block_kernel(
    s_ref, c_ref, hidden_any, a_any, b_any, out_any, low_ref, hidden_ref, a_ref, b_ref, out_ref, sems
):
    loads, stores = [], []
    for i in range(NBLK):
        rows = block(i)
        pairs = [(src.at[rows], dst.at[rows]) for src, dst in ((hidden_any, hidden_ref), (a_any, a_ref), (b_any, b_ref))]
        loads.append(send_out(pairs, sems, 3 * i))
    for i in range(NBLK):
        rows = block(i)
        wait_all(loads[i])
        at = pl.ds(pl.multiple_of(s_ref[0] * SEQ + i * BLK, BLK), BLK)
        out_ref[rows] = (hidden_ref[rows] + (a_ref[rows].astype(F32) + b_ref[rows].astype(F32))).astype(BF16)
        stores += send_out([(out_ref.at[rows], out_any.at[at])], sems, 3 * NBLK + i)
    half = low_ref.shape[0]
    low_ref[...] = out_ref[pl.ds(pl.multiple_of(c_ref[0] * half, half), half)]
    wait_all(stores)


def fill_kernel(s_ref, both_ref, before_ref, out_ref):
    out_ref[...] = both_ref[pl.program_id(0)].astype(out_ref.dtype)


def add_kernel(plan, *refs):
    outs = refs[len(refs) - len(plan) :]
    for out, segments in zip(outs, plan):
        for place, count, lane, width, terms in segments:
            for j in range(count):
                total = None
                for index, first, start in terms:
                    term = refs[index][first + j, :, start : start + width].astype(F32)
                    total = term if total is None else total + term
                out[place + j, :, lane : lane + width] = total.astype(out.dtype)


VREF = pl.BlockSpec(memory_space=pltpu.VMEM)
SREF = pl.BlockSpec(memory_space=pltpu.SMEM)
ANYREF = pl.BlockSpec(memory_space=pl.ANY)


def vm(shape, dtype):
    return pltpu.VMEM(shape, dtype)


def far(shape, dtype):
    return pltpu.HBM(shape, dtype)


def sds(shape, dtype):
    return jax.ShapeDtypeStruct(shape, dtype)


def fast(v):
    return pltpu.with_memory_space_constraint(v, pltpu.VMEM)


class Free:
    def __init__(self, value):
        self.value = value


class Own(Free):
    pass


class Far(Own):
    pass


def call(
    kernel, scalars, args, outs, name, flops, scratch=(), in_specs=None, out_specs=None, grid=None, aliases=None, mib=14
):
    params = pltpu.CompilerParams(vmem_limit_bytes=mib * 1024 * 1024)
    cost = pl.CostEstimate(flops=int(flops), bytes_accessed=0, transcendentals=0)
    if grid is None:
        specs = [ANYREF if isinstance(a, Own) else VREF for a in args]
        args = [placed(a) for a in args]
        out_specs = [
            ANYREF if isinstance(o, Own) or getattr(o, "memory_space", None) == pltpu.HBM else VREF for o in outs
        ]
        outs = [o.value if isinstance(o, Own) else o for o in outs]
        return pl.pallas_call(
            kernel,
            out_shape=outs,
            in_specs=[SREF] * len(scalars) + specs,
            out_specs=out_specs,
            scratch_shapes=list(scratch),
            compiler_params=params,
            cost_estimate=cost,
            name=name,
        )(*scalars, *args)
    return pl.pallas_call(
        kernel,
        out_shape=outs,
        grid_spec=pltpu.PrefetchScalarGridSpec(
            num_scalar_prefetch=len(scalars),
            grid=grid,
            in_specs=[VREF] * len(args) if in_specs is None else in_specs,
            out_specs=out_specs,
            scratch_shapes=list(scratch),
        ),
        input_output_aliases=aliases or {},
        compiler_params=params,
        cost_estimate=cost,
        name=name,
    )(*scalars, *args)


def placed(a):
    if isinstance(a, Far):
        return pltpu.with_memory_space_constraint(a.value, pltpu.HBM)
    return a.value if isinstance(a, Free) else fast(a)


def free(values):
    return [Free(v) for v in values]


def apart(values):
    return [Far(v) for v in values]


def sems(count):
    return pltpu.SemaphoreType.DMA((count,))


def after(values, *done):
    kept = lax.optimization_barrier((tuple(values), done))
    return kept[0]


def on_device(
    tokens, documents, attn_gain, qkv_weight, out_weight, mlp_gain, up_weight, down_weight, cotangent, *, n_dp, n_tensor
):
    d = tokens.shape[1]
    width = qkv_weight.shape[2]
    units = up_weight.shape[1]
    heads = width // HEAD
    piece = d // n_dp
    bits = n_dp.bit_length() - 1
    natural = list(range(bits))
    swapped = [1, 0] + natural[2:]
    t = lax.axis_index("tensor").astype(jnp.int32)
    me = lax.axis_index("dp").astype(jnp.int32)
    s, c = t // 2, t % 2
    color = (me ^ (me >> 1)) & 1
    s1, c1, color1 = s.reshape(1), c.reshape(1), color.reshape(1)
    me_nat, me_swap = mapped(me, natural).reshape(1), mapped(me, swapped).reshape(1)

    def over_x(v):
        return lax.ppermute(v, "tensor", [(i, i ^ 2) for i in range(n_tensor)])

    def over_core(v):
        return lax.ppermute(v, "tensor", [(i, i ^ 1) for i in range(n_tensor)])

    def swap_cores(both):
        groups = [[i, i ^ 1] for i in range(0, n_tensor, 2)]
        return lax.all_to_all(both, "tensor", split_axis=0, concat_axis=0, axis_index_groups=groups)

    def over_dp(v, bit):
        return lax.ppermute(v, "dp", [(i, i ^ (1 << bit)) for i in range(n_dp)])

    h, q = n_dp // 2, n_dp // 4

    def pick(weights, name):
        outs = [sds((w.shape[0] // 4, w.shape[1]), BF16) for w in weights for _ in range(2)]
        got = call(
            pick_kernel, (color1,), [Far(w) for w in weights], outs, name, 0,
            [pltpu.SemaphoreType.DMA((len(outs),))],
        )
        return [got[2 * i : 2 * i + 2] for i in range(len(weights))]

    def spread(pair):
        return [*pair, over_dp(pair[0], 0), over_dp(pair[1], 1)]

    w_one = jnp.transpose(qkv_weight, (1, 2, 0)).reshape(3 * width, d)
    wo_one = out_weight
    w_mine, wo_mine = pick([w_one, wo_one], "pick_attention")
    w_halves = [over_x(v) for v in w_mine]
    wo_halves = [over_x(v) for v in wo_mine]

    docs = documents.astype(F32).reshape(tokens.shape[0] // SEQ, 1, SEQ)
    docs = lax.dynamic_slice_in_dim(docs, s, 1, 0)
    gain_one = attn_gain.reshape(1, d)
    gain_two = mlp_gain.reshape(1, d)
    head_far, head_in = far((SEQ, width), BF16), vm((SEQ, width), BF16)
    head_keep = pltpu.VMEM((SEQ, width), BF16)
    keep_low, keep_wide, keep_both = pltpu.VMEM((SEQ, d), BF16), pltpu.VMEM((SEQ, d), F32), pltpu.VMEM((2, SEQ, d), BF16)
    both_open = Own(sds((2, SEQ, d), BF16))
    rows_low, rows_wide, rows_open = vm((SEQ, d), BF16), vm((SEQ, d), F32), sds((SEQ, d), BF16)
    lse_out = vm((8, SEQ), F32)
    low_open = sds((BLK, d), BF16)
    long_cost = 10**12

    n, att_near, n_far, q_one, k_one, v_one, att_one, lse_one = call(
        first_kernel, (s1,), (Far(tokens), gain_one, w_one, docs),
        [rows_low, head_in, far((SEQ, d), BF16), head_far, head_far, head_far, head_far, lse_out],
        "attend_own", 0,
        [keep_low, head_keep, head_keep, head_keep, sems(6)],
    )
    up_mine, down_mine = pick(after((up_weight, down_weight), n), "pick_mlp")
    up_halves = [over_x(v) for v in up_mine]
    down_halves = [over_x(v) for v in down_mine]
    *w_halves, wo_a, wo_b = after((*w_halves, *wo_halves), n)
    w_pieces, wo_pieces = spread(w_halves), spread((wo_a, wo_b))
    w_two, wo_two, q_two, k_two, v_two, att_two, lse_two, attn_sum = call(
        second_kernel, (color1,), (n, *apart(w_pieces), *apart(wo_pieces), docs, att_near, wo_one),
        [far((3 * width, d), BF16), far((width, d), BF16)] + [head_far] * 4 + [lse_out, Own(sds((SEQ, d), BF16))],
        "attend_other", long_cost,
        [pltpu.VMEM((3 * width, d), BF16), pltpu.VMEM((width, d), BF16)] + [head_keep] * 4
        + [keep_low, sems(14 + 2 * NBLK)], mib=20,
    )
    attn_sum, *up_halves = after((attn_sum, *up_halves), attn_sum)
    attn_recv = over_core(attn_sum)
    up_pieces = spread(up_halves)

    grad_out = far((h, piece, units), BF16)
    keep_up, keep_down = pltpu.VMEM((d, units), BF16), pltpu.VMEM((units, d), BF16)
    keep = [pltpu.VMEM((SEQ, units), BF16), pltpu.VMEM((SEQ, units), BF16)]
    grad_all = [pltpu.VMEM((n_dp, piece, units), BF16)] * 2
    orders = (swapped, natural)
    hidden, mlp_in, out_one, back_one, down_a, down_as, up_a, up_as = call(
        functools.partial(mlp_first_kernel, orders), (s1, me_swap, me_nat),
        (*apart((tokens, cotangent)), Own(attn_sum), Own(attn_recv), *apart((up_weight, down_weight)), gain_two),
        [far((SEQ, d), F32), rows_low, rows_low, rows_low] + [grad_out] * 4, "mlp_own", 0,
        [keep_low, keep_low, keep_both, keep_up, keep_down, keep_wide] + keep + grad_all + [sems(4 * NBLK + 7)], mib=26,
    )
    down_pieces = spread(after(down_halves, mlp_in))
    up_ra = over_dp(up_as, 0)
    down_ra = over_dp(down_as, 1)
    mlp_sum, back_both, down_b, down_bs, up_b, up_bs = call(
        functools.partial(mlp_second_kernel, orders), (s1, me_swap, me_nat, color1),
        (mlp_in, out_one, back_one, Far(cotangent), *apart(up_pieces), *apart(down_pieces)),
        [far((SEQ, d), BF16), both_open] + [grad_out] * 4, "mlp_other", long_cost,
        [keep_low, keep_up, keep_down, keep_low, keep_low] + keep + grad_all + [sems(16)], mib=20,
    )
    mlp_recv = over_core(mlp_sum)
    back_both = swap_cores(back_both)
    up_rb = over_dp(up_bs, 0)
    down_rb = over_dp(down_bs, 1)

    block_start, block_low = call(
        block_kernel, (s1, c1), apart((hidden, after((mlp_sum,), back_both)[0], mlp_recv)),
        [far(tokens.shape, BF16), sds((SEQ // 2, d), BF16)], "block_out", 0,
        [keep_wide, keep_low, keep_low, keep_low, sems(4 * NBLK)],
    )
    block_one = over_x(block_low)
    (back_both,) = after((back_both,), block_low)
    go_out = far((n_dp, piece, width), BF16)
    go_keep = pltpu.VMEM((n_dp, piece, width), BF16)
    hidden_grad, da_one, da_two, go_one, go_two = call(
        functools.partial(middle_kernel, natural), (s1, me_nat),
        (*apart((hidden, cotangent)), Own(back_both), *apart((wo_one, wo_two, att_one, att_two)), gain_two),
        [far((SEQ, d), F32), head_in, head_in, go_out, go_out], "middle", long_cost,
        [keep_wide, keep_low, keep_both] + [pltpu.VMEM((width, d), BF16)] * 2
        + [head_keep, head_keep, keep_wide, keep_low, go_keep, go_keep, sems(4 * NBLK + 6)], mib=26,
    )

    wide = 4 * width
    qkv_out = [far((h, piece, wide), BF16)] * 2
    back_scratch = [head_keep] * 3 + [pltpu.VMEM((heads, SEQ, SEQ), BF16), pltpu.VMEM((n_dp, piece, wide), BF16)]
    back_scratch += [keep_low, sems(4 + 2 * NBLK)]
    in_one, g_b, g_bs = call(
        functools.partial(attend_back, False, natural), (me_nat,),
        (q_two, k_two, v_two, att_two, da_two, lse_two, docs, n_far, w_two, go_two), [rows_wide, *qkv_out],
        "attend_back_other", 0, back_scratch, mib=20,
    )
    g_rb = over_dp(g_bs, 0)

    def adds(name, results):
        args, plan, outs = [], [], []

        def place(array):
            for i, known in enumerate(args):
                if known is array:
                    return i
            args.append(array)
            return len(args) - 1

        for dtype, pieces, rows, lanes, segments in results:
            plan.append([(*seg[:4], [(place(v), first, lane) for v, first, lane in seg[4]]) for seg in segments])
            outs.append(sds((pieces, rows, lanes), dtype))
        return call(functools.partial(add_kernel, plan), (), free(args), outs, name, 0)

    def plain(dtype, count, *terms):
        rows, lanes = terms[0][0].shape[1:]
        return (dtype, count, rows, lanes, [(0, count, 0, lanes, [(v, first, 0) for v, first in terms])])

    def split(count, *arrays):
        return [plain(F32, count, *[(v, 0) for v in arrays]), plain(BF16, count, *[(v, count) for v in arrays])]

    def side_by_side(dtype, count, first, *groups):
        lane, segments = 0, []
        for arrays in groups:
            lanes = arrays[0].shape[2]
            segments.append((0, count, lane, lanes, [(v, first, 0) for v in arrays]))
            lane += lanes
        return (dtype, count, piece, lane, segments)

    def fill(start, one):
        both = swap_cores(jnp.stack([one, one]))
        (out,) = call(
            fill_kernel, (s1,), (both, start), [sds(start.shape, start.dtype)], "fill", 0,
            in_specs=[VREF, ANYREF],
            out_specs=[pl.BlockSpec((SEQ // 2, d), lambda i, s_ref, *_: ((1 - s_ref[0]) * 2 + i, 0))],
            grid=(2,), aliases={2: 0},
        )
        return out

    up_ra, up_rb, down_ra, down_rb = after((up_ra, up_rb, down_ra, down_rb), in_one)
    up_2, up_s2, down_2, down_s2 = adds(
        "reduce_mlp_one",
        [plain(F32, h, (up_a, 0), (up_ra, 0)), plain(BF16, h, (up_b, 0), (up_rb, 0))]
        + [plain(F32, h, (down_a, 0), (down_ra, 0)), plain(BF16, h, (down_b, 0), (down_rb, 0))],
    )
    up_r2, down_r2 = over_x(up_s2), over_x(down_s2)
    (in_one,) = after((in_one,), up_s2)
    in_both, g_a, g_as = call(
        functools.partial(attend_back, True, natural), (me_nat,),
        (q_one, k_one, v_one, att_one, da_one, lse_one, docs, n_far, w_one, go_one, in_one), [both_open] + qkv_out,
        "attend_back_own", 0, back_scratch, mib=20,
    )
    g_ra = over_dp(g_as, 0)
    g_rb, block_one = after((g_rb, block_one), g_a)
    g_b2, g_bs2 = adds("reduce_other_one", split(q, g_b, g_rb))
    g_rb2 = over_dp(g_bs2, 1)
    (in_both,) = after((in_both,), g_bs2)
    in_both = swap_cores(in_both)

    input_start, input_low = call(
        last_kernel, (s1, c1), (Far(tokens), Own(in_both), Far(hidden_grad), gain_one),
        [far(tokens.shape, F32), sds((SEQ // 2, d), BF16)], "norm_back", 0,
        [keep_low, keep_both, keep_wide, keep_wide, sems(4 * NBLK)], mib=20,
    )
    up_r2, down_r2, g_rb2 = after((up_r2, down_r2, g_rb2), input_low)
    up_3, up_s3, down_3, down_s3, g_bx = adds(
        "reduce_mlp_two", split(q, up_2, up_r2) + split(q, down_2, down_r2) + [plain(BF16, q, (g_b2, 0), (g_rb2, 0))]
    )
    up_r3, down_r3 = over_dp(up_s3, 1), over_dp(down_s3, 0)
    g_rx = over_x(g_bx)
    (input_low,) = after((input_low,), g_bx)
    input_one = over_x(input_low)
    block_out, block_one = after((block_start, block_one), g_bx)
    block_out = fill(block_out, block_one)
    (g_ra,) = after((g_ra,), block_out)
    g_a2, g_as2 = adds("reduce_own_one", split(q, g_a, g_ra))
    g_ra2 = over_dp(g_as2, 1)
    last = q // 2
    up_r3, down_r3 = after((up_r3, down_r3), g_as2)
    mlp_4, mlp_s4 = adds(
        "reduce_mlp_three", [
            side_by_side(dtype, last, start, (up_3, up_r3), (down_3, down_r3)) for dtype, start in ((F32, 0), (BF16, last))
        ]
    )
    mlp_r4 = over_dp(mlp_s4, natural[2])
    g_ra2, g_rx = after((g_ra2, g_rx), mlp_s4)
    g_4, g_s4 = adds("reduce_own_two", split(last, g_a2, g_ra2, g_rx))
    g_r4 = over_dp(g_s4, natural[2])
    input_grad, input_one = after((input_start, input_one), g_s4)
    input_grad = fill(input_grad, input_one)
    mlp_r4, g_r4 = after((mlp_r4, g_r4), input_grad)
    mlp_5 = mlp_4 + mlp_r4.astype(F32)

    def other_steps(total):
        for bit in natural[3:]:
            count = total.shape[0] // 2
            got = over_dp(total[count:].astype(BF16), bit)
            total = total[:count] + got.astype(F32)
        return total[0]

    mlp_part, g_part = other_steps(mlp_5), other_steps(g_4 + g_r4.astype(F32))
    up_part, down_part = mlp_part[:, :units], mlp_part[:, units:]
    qkv_flat, out_part = g_part[:, : 3 * width], g_part[:, 3 * width :]
    start = me * piece
    w_rows = lax.dynamic_slice_in_dim(qkv_weight, start, piece, 0).reshape(piece, 3 * width).astype(F32)
    up_rows = lax.dynamic_slice_in_dim(up_weight, start, piece, 0).astype(F32)
    gains = jnp.stack([jnp.sum(w_rows * qkv_flat, 1), jnp.sum(up_rows * up_part, 1)])
    gains = gains + over_core(gains)
    gains = gains + over_x(gains)
    gains = gains / lax.dynamic_slice_in_dim(jnp.stack([attn_gain, mlp_gain]), start, piece, 1)
    qkv_part = qkv_flat.reshape(piece, 3, width)
    return (block_out, input_grad, gains[0], qkv_part, out_part.T, gains[1], up_part, down_part.T)


def solution(mesh):
    in_specs = (
        P("dp", None),
        P("dp"),
        P(),
        P(None, None, "tensor"),
        P("tensor", None),
        P(),
        P(None, "tensor"),
        P("tensor", None),
        P("dp", None),
    )
    out_specs = (
        P("dp", None),
        P("dp", None),
        P("dp"),
        P("dp", None, "tensor"),
        P("tensor", "dp"),
        P("dp"),
        P("dp", "tensor"),
        P("tensor", "dp"),
    )
    body = functools.partial(on_device, n_dp=mesh.shape["dp"], n_tensor=mesh.shape["tensor"])
    return jax.shard_map(body, mesh=mesh, in_specs=in_specs, out_specs=out_specs, check_vma=False)
```

```python
import functools
import math

import jax
import jax.numpy as jnp
from jax import lax
from jax.experimental import pallas as pl
from jax.experimental.pallas import tpu as pltpu
from jax.sharding import PartitionSpec as P

HEAD = 64
SEQ = 1024
BLK = 256
NBLK = SEQ // BLK
EPS = 1e-05
VMEM_BYTES = 14 * 1024 * 1024
F32 = jnp.float32
BF16 = jnp.bfloat16
C0 = math.sqrt(2.0 / math.pi)
C1 = 0.044715
NEG = -1e30

NN = (((1,), (0,)), ((), ()))
NT = (((1,), (1,)), ((), ()))
TN = (((0,), (0,)), ((), ()))


def mm(a, b, dims):
    return lax.dot_general(a, b, dims, preferred_element_type=F32)


def normed(rows):
    centered = rows - jnp.mean(rows, -1, keepdims=True)
    inverse = lax.rsqrt(jnp.mean(centered * centered, -1, keepdims=True) + EPS)
    return centered * inverse, inverse


def norm_back(grad_rows, unit, inverse, gain):
    scaled = grad_rows * gain
    first = jnp.mean(scaled, -1, keepdims=True)
    second = jnp.mean(scaled * unit, -1, keepdims=True)
    return inverse * (scaled - first - unit * second)


def head_mask(rows, width, h):
    lane = lax.broadcasted_iota(jnp.int32, (rows, width), 1)
    return (lane >= h * HEAD) & (lane < (h + 1) * HEAD)


def mapped(index, order):
    bits = len(order)
    return sum(((index >> b) & 1) << (bits - 1 - i) for i, b in enumerate(order))


def put_pieces(all_ref, me, grad, order, base=0, lane=0):
    rows = all_ref.shape[1]
    width = grad.shape[1]
    for p in range(grad.shape[0] // rows):
        place = mapped(p + base // rows, order) ^ me
        all_ref[place, :, lane : lane + width] = grad[p * rows : (p + 1) * rows].astype(BF16)


def block(i):
    return slice(i * BLK, (i + 1) * BLK)


def send_out(pairs, sems, base=0):
    copies = [pltpu.make_async_copy(src, dst, sems.at[base + i]) for i, (src, dst) in enumerate(pairs)]
    for one in copies:
        one.start()
    return copies


def wait_all(copies):
    for one in copies:
        one.wait()


def pieces_out(all_ref, refs):
    count = refs[0].shape[0]
    return [(all_ref.at[i * count : (i + 1) * count], ref) for i, ref in enumerate(refs)]


def quarters_in(whole_ref, color, pieces):
    rows = pieces[0].shape[0]
    at = [2 * color, 2 * color + 1, 2 * (1 - color), 2 * (1 - color) + 1]
    return [(ref, whole_ref.at[pl.ds(pl.multiple_of(i * rows, 16), rows)]) for i, ref in zip(at, pieces)]


def forward_scores(q_ref, k_ref, qb, h):
    width = q_ref.shape[1]
    rows = slice(qb * BLK, (qb + 1) * BLK)
    queries = q_ref[rows] * jnp.asarray(0.125, BF16)
    q_h = jnp.where(head_mask(BLK, width, h), queries, jnp.zeros_like(queries))
    return mm(q_h, k_ref[: (qb + 1) * BLK], NT)


def forward_allowed(docs_ref, qb):
    base, end = qb * BLK, (qb + 1) * BLK
    column = jnp.transpose(jnp.broadcast_to(docs_ref[0, :, base:end], (128, BLK)))
    docs_q = jnp.concatenate([column] * (end // 128), 1)
    at_row = lax.broadcasted_iota(jnp.int32, (BLK, end), 0) + base
    at_col = lax.broadcasted_iota(jnp.int32, (BLK, end), 1)
    return (docs_q == docs_ref[0, :, :end]) & (at_col <= at_row)


def forward_attention(q_ref, k_ref, v_ref, docs_ref, lse_ref, att_ref, ahead=2):
    width = q_ref.shape[1]
    heads = width // HEAD
    items = [(qb, h) for qb in range(NBLK) for h in range(heads)]
    pending = [forward_scores(q_ref, k_ref, *items[i]) for i in range(ahead)]
    for i, (qb, h) in enumerate(items):
        rows = slice(qb * BLK, (qb + 1) * BLK)
        if i + ahead < len(items):
            pending.append(forward_scores(q_ref, k_ref, *items[i + ahead]))
        if h == 0:
            allowed = forward_allowed(docs_ref, qb)
            total = jnp.zeros((BLK, width), F32)
        s = jnp.where(allowed, pending.pop(0), NEG)
        row_max = jnp.max(s, -1, keepdims=True)
        e = jnp.exp(s - row_max)
        row_sum = jnp.sum(e, -1, keepdims=True)
        out = mm(e.astype(BF16), v_ref[: (qb + 1) * BLK], NN)
        total = jnp.where(head_mask(BLK, width, h), out / row_sum, total)
        lse = row_max + jnp.log(row_sum)
        lse_ref[h : h + 1, rows] = jnp.transpose(jnp.broadcast_to(lse, (BLK, 128)))[:1]
        if h == heads - 1:
            att_ref[rows] = total.astype(BF16)


def over_blocks(body):
    def step(i, carry):
        body(pl.ds(pl.multiple_of(i * BLK, BLK), BLK))
        return carry

    lax.fori_loop(0, NBLK, step, 0)


def project(n_ref, w_ref, refs):
    width = refs[0].shape[1]
    for i, ref in enumerate(refs):
        ref[...] = mm(n_ref[...], w_ref[i * width : (i + 1) * width], NT).astype(BF16)


def pick_kernel(color_ref, *refs):
    count = (len(refs) - 1) // 3
    sems = refs[-1]
    pairs = []
    for i in range(count):
        src = refs[i]
        rows = src.shape[0] // 4
        for j in range(2):
            at = pl.ds(pl.multiple_of((2 * color_ref[0] + j) * rows, 16), rows)
            pairs.append((src.at[at], refs[count + 2 * i + j]))
    wait_all(send_out(pairs, sems))


def first_kernel(
    s_ref, x_ref, gain_ref, w_ref, docs_ref,
    n_ref, att_ref, n_out, q_out, k_out, v_out, att_out, lse_ref, x_vmem, q_ref, k_ref, v_ref, sems,
):
    mine = pl.ds(pl.multiple_of(s_ref[0] * SEQ, SEQ), SEQ)
    wait_all(send_out([(x_ref.at[mine], x_vmem)], sems, 5))
    for i in range(NBLK):
        unit, _ = normed(x_vmem[block(i)].astype(F32))
        n_ref[block(i)] = (unit * gain_ref[...]).astype(BF16)
    project(n_ref, w_ref, (q_ref, k_ref, v_ref))
    copies = send_out([(n_ref, n_out), (q_ref, q_out), (k_ref, k_out), (v_ref, v_out)], sems)
    forward_attention(q_ref, k_ref, v_ref, docs_ref, lse_ref, att_ref)
    wait_all(copies + send_out([(att_ref, att_out)], sems, 4))


def second_kernel(
    color_ref, n_ref, wa_ref, wb_ref, wc_ref, wd_ref, oa_ref, ob_ref, oc_ref, od_ref, docs_ref, att_one_ref, wo_one_ref,
    w_out, wo_out, q_out, k_out, v_out, att_out, lse_ref, sum_ref,
    w_ref, wo_ref, q_ref, k_ref, v_ref, att_ref, sems,
):
    color = color_ref[0]
    loads = send_out(quarters_in(w_ref, color, (wa_ref, wb_ref, wc_ref, wd_ref)), sems, 6)
    loads_wo = send_out(quarters_in(wo_ref, color, (oa_ref, ob_ref, oc_ref, od_ref)), sems, 10)
    wait_all(loads)
    project(n_ref, w_ref, (q_ref, k_ref, v_ref))
    wait_all(loads_wo)
    copies = send_out([(w_ref, w_out), (wo_ref, wo_out), (q_ref, q_out), (k_ref, k_out), (v_ref, v_out)], sems)
    forward_attention(q_ref, k_ref, v_ref, docs_ref, lse_ref, att_ref)
    copies += send_out([(att_ref, att_out)], sems, 5)
    for i in range(NBLK):
        total = mm(att_one_ref[block(i)], wo_one_ref[...], NN) + mm(att_ref[block(i)], wo_ref[...], NN)
        sum_ref[block(i)] = total.astype(BF16)
    wait_all(copies)


def gelu_pair(u):
    square = u * u
    th = jnp.tanh(u * (C0 + (C0 * C1) * square))
    half = 0.5 * u
    act = half + half * th
    slope = 0.5 + 0.5 * th + half * (1.0 - th * th) * (C0 + (3.0 * C0 * C1) * square)
    return act, slope


def mlp_rows(rows, in_ref, cot, up_ref, down_ref, act_ref, back_in_ref):
    act, slope = gelu_pair(mm(in_ref[rows], up_ref[...], NN))
    act = act.astype(BF16)
    act_ref[rows] = act
    back_in = (mm(cot, down_ref[...], NT) * slope).astype(BF16)
    back_in_ref[rows] = back_in
    return mm(act, down_ref[...], NN), mm(back_in, up_ref[...], NT)


def grad_pieces(order, me_ref, left_ref, right_ref, all_ref):
    wide = left_ref.shape[1] // 2

    def one_half(j, carry):
        lanes = pl.ds(pl.multiple_of(j * wide, 128), wide)
        put_pieces(all_ref, me_ref[0], mm(left_ref[:, lanes], right_ref[...], TN), order, j * wide)
        return carry

    lax.fori_loop(0, 2, one_half, 0)


def mlp_first_kernel(
    orders, s_ref, me_down_ref, me_up_ref, x_any, cot_any, up_any, down_any, a_ref, b_ref, gain_ref,
    hidden_any, in_ref, out_ref, back_ref, down_keep, down_send, up_keep, up_send,
    x_ref, cot_ref, up_ref, down_ref, hidden_ref, act_ref, back_in_ref, down_all, up_all, sems,
):
    def load_x(i):
        at = pl.ds(pl.multiple_of(s_ref[0] * SEQ + i * BLK, BLK), BLK)
        to = pl.ds(pl.multiple_of(i * BLK, BLK), BLK)
        return pltpu.make_async_copy(x_any.at[at], x_ref.at[to], sems.at[i])

    def norm_block(i):
        load_x(i).wait()
        rows = pl.ds(pl.multiple_of(i * BLK, BLK), BLK)
        hidden = x_ref[rows].astype(F32) + (a_ref[rows].astype(F32) + b_ref[rows].astype(F32))
        hidden_ref[rows] = hidden.astype(BF16)
        unit, _ = normed(hidden)
        in_ref[rows] = (unit * gain_ref[...]).astype(BF16)

    load_x(0).start()
    loads = send_out([(up_any, up_ref)], sems, NBLK)
    for i in range(1, NBLK):
        load_x(i).start()
    mine = pl.ds(pl.multiple_of(s_ref[0] * SEQ, SEQ), SEQ)
    loads += send_out([(cot_any.at[mine], cot_ref), (down_any, down_ref)], sems, NBLK + 1)
    norm_block(0)
    wait_all(loads)

    def one_block(i, carry):
        rows = pl.ds(pl.multiple_of(i * BLK, BLK), BLK)
        norm_block(i + 1)
        out, back = mlp_rows(rows, in_ref, cot_ref[rows], up_ref, down_ref, act_ref, back_in_ref)
        out_ref[rows] = out.astype(BF16)
        back_ref[rows] = back.astype(BF16)
        return carry

    lax.fori_loop(0, NBLK - 1, one_block, 0)
    copies = send_out([(hidden_ref, hidden_any)], sems, NBLK + 3)
    rows = block(NBLK - 1)
    out, back = mlp_rows(rows, in_ref, cot_ref[rows], up_ref, down_ref, act_ref, back_in_ref)
    out_ref[rows] = out.astype(BF16)
    back_ref[rows] = back.astype(BF16)
    grad_pieces(orders[0], me_down_ref, cot_ref, act_ref, down_all)
    copies += send_out(pieces_out(down_all, (down_keep, down_send)), sems, NBLK + 4)
    grad_pieces(orders[1], me_up_ref, in_ref, back_in_ref, up_all)
    wait_all(copies + send_out(pieces_out(up_all, (up_keep, up_send)), sems, NBLK + 6))


def mlp_second_kernel(
    orders, s_ref, me_down_ref, me_up_ref, color_ref, in_ref, out_one_ref, back_one_ref, cot_any,
    ua_ref, ub_ref, uc_ref, ud_ref, da_ref, db_ref, dc_ref, dd_ref,
    out_any, both_ref, down_keep, down_send, up_keep, up_send,
    cot_ref, up_ref, down_ref, out_ref, act_ref, back_in_ref, down_all, up_all, sems,
):
    color = color_ref[0]
    mine = pl.ds(pl.multiple_of(s_ref[0] * SEQ, SEQ), SEQ)
    loads = send_out(quarters_in(up_ref, color, (ua_ref, ub_ref, uc_ref, ud_ref)), sems)
    loads += send_out([(cot_any.at[mine], cot_ref)], sems, 4)
    loads += send_out(quarters_in(down_ref, color, (da_ref, db_ref, dc_ref, dd_ref)), sems, 5)
    wait_all(loads)

    def one_block(rows):
        out, back = mlp_rows(rows, in_ref, cot_ref[rows], up_ref, down_ref, act_ref, back_in_ref)
        out_ref[rows] = (out_one_ref[rows].astype(F32) + out).astype(BF16)
        back = (back_one_ref[rows].astype(F32) + back).astype(BF16)
        both_ref[0, rows] = back
        both_ref[1, rows] = back

    over_blocks(one_block)
    copies = send_out([(out_ref, out_any)], sems, 9)
    grad_pieces(orders[0], me_down_ref, cot_ref, act_ref, down_all)
    copies += send_out(pieces_out(down_all, (down_keep, down_send)), sems, 10)
    grad_pieces(orders[1], me_up_ref, in_ref, back_in_ref, up_all)
    wait_all(copies + send_out(pieces_out(up_all, (up_keep, up_send)), sems, 12))


def middle_kernel(
    order, s_ref, me_ref, hidden_any, cot_any, wo_one_any, wo_two_any, att_one_any, att_two_any, both_ref, gain_ref,
    grad_any, da_one_ref, da_two_ref, go_one_any, go_two_any,
    hidden_ref, cot_ref, wo_one_ref, wo_two_ref, att_one_ref, att_two_ref, grad_ref, low_ref, go_one, go_two, sems,
):
    at = [pl.ds(pl.multiple_of(s_ref[0] * SEQ + i * BLK, BLK), BLK) for i in range(NBLK)]
    loads = []
    for i in range(NBLK):
        rows = block(i)
        pairs = [
            (hidden_any.at[rows], hidden_ref.at[rows]),
            (cot_any.at[at[i]], cot_ref.at[rows]),
        ]
        loads.append(send_out(pairs, sems, 3 * i))
        if i == 0:
            loads_wo = send_out([(wo_one_any, wo_one_ref), (wo_two_any, wo_two_ref)], sems, 3 * NBLK)
    loads_att = send_out([(att_one_any, att_one_ref), (att_two_any, att_two_ref)], sems, 3 * NBLK + 2)
    copies = []
    for i in range(NBLK):
        rows = block(i)
        wait_all(loads[i])
        unit, inverse = normed(hidden_ref[rows].astype(F32))
        grad = both_ref[0, rows].astype(F32) + both_ref[1, rows].astype(F32)
        hidden_grad = cot_ref[rows].astype(F32) + norm_back(grad, unit, inverse, gain_ref[...])
        grad_ref[rows] = hidden_grad.astype(BF16)
        copies += send_out([(grad_ref.at[rows], grad_any.at[rows])], sems, 3 * NBLK + 4 + i)
        low = hidden_grad.astype(BF16)
        low_ref[rows] = low
        if i == 0:
            wait_all(loads_wo)
        da_one_ref[rows] = mm(low, wo_one_ref[...], NT).astype(BF16)
        da_two_ref[rows] = mm(low, wo_two_ref[...], NT).astype(BF16)
    wait_all(loads_att)
    put_pieces(go_one, me_ref[0], mm(low_ref[...], att_one_ref[...], TN), order)
    put_pieces(go_two, me_ref[0], mm(low_ref[...], att_two_ref[...], TN), order)
    wait_all(copies + send_out([(go_one, go_one_any), (go_two, go_two_any)], sems, 4 * NBLK + 4))


def attend_back(
    add_first, order, me_ref, q_ref, k_ref, v_ref, att_ref, da_ref, lse_ref, docs_ref, n_ref, w_ref, go_ref, *rest
):
    if add_first:
        before_ref, both_ref = rest[:2]
    else:
        (sum_ref,) = rest[:1]
    *grad_refs, dq_ref, dk_ref, dv_ref, ds_ref, all_ref, sems = rest[1 + add_first :]
    width = q_ref.shape[1]
    heads = width // HEAD
    eighth = jnp.asarray(0.125, BF16)
    prod = da_ref[...].astype(F32) * att_ref[...].astype(F32)
    pick_lane = lax.broadcasted_iota(jnp.int32, (8, width), 1)
    pick_row = lax.broadcasted_iota(jnp.int32, (8, width), 0)
    pick = jnp.where((pick_lane >= pick_row * HEAD) & (pick_lane < (pick_row + 1) * HEAD), 1.0, 0.0).astype(F32)
    inner = lax.dot_general(pick, prod, NT, precision=lax.Precision.HIGHEST, preferred_element_type=F32)
    for kb in range(NBLK):
        keys = slice(kb * BLK, (kb + 1) * BLK)
        start = kb * BLK
        count = SEQ - start
        column = jnp.transpose(jnp.broadcast_to(docs_ref[0, :, keys], (128, BLK)))
        docs_k = jnp.concatenate([column] * (count // 128), 1)
        at_row = lax.broadcasted_iota(jnp.int32, (BLK, count), 0)
        at_col = lax.broadcasted_iota(jnp.int32, (BLK, count), 1)
        allowed = (docs_k == docs_ref[0, :, start:]) & (at_row <= at_col)
        dk = jnp.zeros((BLK, width), F32)
        dv = jnp.zeros((BLK, width), F32)
        for h in range(heads):
            mask = head_mask(count, width, h)
            q_h = jnp.where(mask, q_ref[start:] * eighth, jnp.zeros((count, width), BF16))
            da_h = jnp.where(mask, da_ref[start:], jnp.zeros((count, width), BF16))
            s = mm(k_ref[keys], q_h, NT) - lse_ref[h : h + 1, start:]
            p = jnp.exp(jnp.where(allowed, s, NEG))
            dp = mm(v_ref[keys], da_h, NT)
            ds = (p * (dp - inner[h : h + 1, start:])).astype(BF16)
            ds_ref[h, keys, start:] = ds
            dv = dv + mm(p.astype(BF16), da_h, NN)
            dk = dk + mm(ds, q_h, NN)
        dk_ref[keys] = dk.astype(BF16)
        dv_ref[keys] = dv.astype(BF16)
    for qb in range(NBLK):
        rows = slice(qb * BLK, (qb + 1) * BLK)
        end = (qb + 1) * BLK
        dq = jnp.zeros((BLK, width), F32)
        for h in range(heads):
            k_h = jnp.where(head_mask(end, width, h), k_ref[:end] * eighth, jnp.zeros((end, width), BF16))
            dq = dq + mm(ds_ref[h, :end, rows], k_h, TN)
        dq_ref[rows] = dq.astype(BF16)
    for qb in range(NBLK):
        rows = slice(qb * BLK, (qb + 1) * BLK)
        total = mm(dq_ref[rows], w_ref[:width], NN)
        total = total + mm(dk_ref[rows], w_ref[width : 2 * width], NN)
        total = total + mm(dv_ref[rows], w_ref[2 * width :], NN)
        if add_first:
            total = (before_ref[rows] + total).astype(BF16)
            both_ref[0, rows] = total
            both_ref[1, rows] = total
        else:
            sum_ref[rows] = total
    n = n_ref[...]
    all_ref[:, :, 3 * width :] = go_ref[...]
    for i, ref in enumerate((dq_ref, dk_ref, dv_ref)):
        put_pieces(all_ref, me_ref[0], mm(n, ref[...], TN), order, 0, i * width)
    wait_all(send_out(pieces_out(all_ref, grad_refs), sems))


def last_kernel(
    s_ref, c_ref, x_any, grad_any, both_ref, gain_ref, out_any, low_ref, x_ref, grad_ref, out_ref, sems,
):
    at = [pl.ds(pl.multiple_of(s_ref[0] * SEQ + i * BLK, BLK), BLK) for i in range(NBLK)]
    loads = []
    for i in range(NBLK):
        rows = block(i)
        pairs = [
            (x_any.at[at[i]], x_ref.at[rows]),
            (grad_any.at[rows], grad_ref.at[rows]),
        ]
        loads.append(send_out(pairs, sems, 3 * i))
    stores = []
    for i in range(NBLK):
        rows = block(i)
        wait_all(loads[i])
        unit, inverse = normed(x_ref[rows].astype(F32))
        grad = both_ref[0, rows].astype(F32) + both_ref[1, rows].astype(F32)
        out = grad_ref[rows].astype(F32) + norm_back(grad, unit, inverse, gain_ref[...])
        out_ref[rows] = out
        stores += send_out([(out_ref.at[rows], out_any.at[at[i]])], sems, 3 * NBLK + i)
    half = low_ref.shape[0]
    low_ref[...] = out_ref[pl.ds(pl.multiple_of(c_ref[0] * half, half), half)].astype(BF16)
    wait_all(stores)


def block_kernel(
    s_ref, c_ref, hidden_any, a_any, b_any, out_any, low_ref, hidden_ref, a_ref, b_ref, out_ref, sems
):
    loads, stores = [], []
    for i in range(NBLK):
        rows = block(i)
        pairs = [(src.at[rows], dst.at[rows]) for src, dst in ((hidden_any, hidden_ref), (a_any, a_ref), (b_any, b_ref))]
        loads.append(send_out(pairs, sems, 3 * i))
    for i in range(NBLK):
        rows = block(i)
        wait_all(loads[i])
        at = pl.ds(pl.multiple_of(s_ref[0] * SEQ + i * BLK, BLK), BLK)
        out_ref[rows] = (hidden_ref[rows].astype(F32) + (a_ref[rows].astype(F32) + b_ref[rows].astype(F32))).astype(BF16)
        stores += send_out([(out_ref.at[rows], out_any.at[at])], sems, 3 * NBLK + i)
    half = low_ref.shape[0]
    low_ref[...] = out_ref[pl.ds(pl.multiple_of(c_ref[0] * half, half), half)]
    wait_all(stores)


def fill_kernel(s_ref, both_ref, before_ref, out_ref):
    out_ref[...] = both_ref[pl.program_id(0)].astype(out_ref.dtype)


def add_kernel(plan, *refs):
    outs = refs[len(refs) - len(plan) :]
    for out, segments in zip(outs, plan):
        for place, count, lane, width, terms in segments:
            for j in range(count):
                total = None
                for index, first, start in terms:
                    term = refs[index][first + j, :, start : start + width].astype(F32)
                    total = term if total is None else total + term
                out[place + j, :, lane : lane + width] = total.astype(out.dtype)


VREF = pl.BlockSpec(memory_space=pltpu.VMEM)
SREF = pl.BlockSpec(memory_space=pltpu.SMEM)
ANYREF = pl.BlockSpec(memory_space=pl.ANY)


def vm(shape, dtype):
    return pltpu.VMEM(shape, dtype)


def far(shape, dtype):
    return pltpu.HBM(shape, dtype)


def sds(shape, dtype):
    return jax.ShapeDtypeStruct(shape, dtype)


def fast(v):
    return pltpu.with_memory_space_constraint(v, pltpu.VMEM)


class Free:
    def __init__(self, value):
        self.value = value


class Own(Free):
    pass


class Far(Own):
    pass


def call(
    kernel, scalars, args, outs, name, flops, scratch=(), in_specs=None, out_specs=None, grid=None, aliases=None, mib=14
):
    params = pltpu.CompilerParams(vmem_limit_bytes=mib * 1024 * 1024)
    cost = pl.CostEstimate(flops=int(flops), bytes_accessed=0, transcendentals=0)
    if grid is None:
        specs = [ANYREF if isinstance(a, Own) else VREF for a in args]
        args = [placed(a) for a in args]
        out_specs = [
            ANYREF if isinstance(o, Own) or getattr(o, "memory_space", None) == pltpu.HBM else VREF for o in outs
        ]
        outs = [o.value if isinstance(o, Own) else o for o in outs]
        return pl.pallas_call(
            kernel,
            out_shape=outs,
            in_specs=[SREF] * len(scalars) + specs,
            out_specs=out_specs,
            scratch_shapes=list(scratch),
            compiler_params=params,
            cost_estimate=cost,
            name=name,
        )(*scalars, *args)
    return pl.pallas_call(
        kernel,
        out_shape=outs,
        grid_spec=pltpu.PrefetchScalarGridSpec(
            num_scalar_prefetch=len(scalars),
            grid=grid,
            in_specs=[VREF] * len(args) if in_specs is None else in_specs,
            out_specs=out_specs,
            scratch_shapes=list(scratch),
        ),
        input_output_aliases=aliases or {},
        compiler_params=params,
        cost_estimate=cost,
        name=name,
    )(*scalars, *args)


def placed(a):
    if isinstance(a, Far):
        return pltpu.with_memory_space_constraint(a.value, pltpu.HBM)
    return a.value if isinstance(a, Free) else fast(a)


def free(values):
    return [Free(v) for v in values]


def own(values):
    return [Own(v) for v in values]


def apart(values):
    return [Far(v) for v in values]


def sems(count):
    return pltpu.SemaphoreType.DMA((count,))


def after(values, *done):
    kept = lax.optimization_barrier((tuple(values), done))
    return kept[0]


def on_device(
    tokens, documents, attn_gain, qkv_weight, out_weight, mlp_gain, up_weight, down_weight, cotangent, *, n_dp, n_tensor
):
    d = tokens.shape[1]
    width = qkv_weight.shape[2]
    units = up_weight.shape[1]
    heads = width // HEAD
    piece = d // n_dp
    bits = n_dp.bit_length() - 1
    natural = list(range(bits))
    swapped = [1, 0] + natural[2:]
    t = lax.axis_index("tensor").astype(jnp.int32)
    me = lax.axis_index("dp").astype(jnp.int32)
    s, c = t // 2, t % 2
    color = (me ^ (me >> 1)) & 1
    s1, c1, color1 = s.reshape(1), c.reshape(1), color.reshape(1)
    me_nat, me_swap = mapped(me, natural).reshape(1), mapped(me, swapped).reshape(1)

    def over_x(v):
        return lax.ppermute(v, "tensor", [(i, i ^ 2) for i in range(n_tensor)])

    def over_core(v):
        return lax.ppermute(v, "tensor", [(i, i ^ 1) for i in range(n_tensor)])

    def swap_cores(both):
        groups = [[i, i ^ 1] for i in range(0, n_tensor, 2)]
        return lax.all_to_all(both, "tensor", split_axis=0, concat_axis=0, axis_index_groups=groups)

    def over_dp(v, bit):
        return lax.ppermute(v, "dp", [(i, i ^ (1 << bit)) for i in range(n_dp)])

    h, q = n_dp // 2, n_dp // 4

    def pick(weights, name):
        outs = [sds((w.shape[0] // 4, w.shape[1]), BF16) for w in weights for _ in range(2)]
        got = call(
            pick_kernel, (color1,), [Far(w) for w in weights], outs, name, 0,
            [pltpu.SemaphoreType.DMA((len(outs),))],
        )
        return [got[2 * i : 2 * i + 2] for i in range(len(weights))]

    def spread(pair):
        return [*pair, over_dp(pair[0], 0), over_dp(pair[1], 1)]

    w_one = jnp.transpose(qkv_weight, (1, 2, 0)).reshape(3 * width, d)
    wo_one = out_weight
    w_mine, wo_mine, up_mine, down_mine = pick([w_one, wo_one, up_weight, down_weight], "pick")
    w_halves = [over_x(v) for v in w_mine]
    wo_halves = [over_x(v) for v in wo_mine]

    docs = documents.astype(F32).reshape(tokens.shape[0] // SEQ, 1, SEQ)
    docs = lax.dynamic_slice_in_dim(docs, s, 1, 0)
    gain_one = attn_gain.reshape(1, d)
    gain_two = mlp_gain.reshape(1, d)
    head_far, head_in = far((SEQ, width), BF16), vm((SEQ, width), BF16)
    head_keep = pltpu.VMEM((SEQ, width), BF16)
    keep_low, keep_wide, keep_both = pltpu.VMEM((SEQ, d), BF16), pltpu.VMEM((SEQ, d), F32), pltpu.VMEM((2, SEQ, d), BF16)
    both_open = vm((2, SEQ, d), BF16)
    rows_low, rows_wide, rows_open = vm((SEQ, d), BF16), vm((SEQ, d), F32), sds((SEQ, d), BF16)
    lse_out = vm((8, SEQ), F32)
    low_open = sds((BLK, d), BF16)
    long_cost = 10**12

    n, att_near, n_far, q_one, k_one, v_one, att_one, lse_one = call(
        first_kernel, (s1,), (Far(tokens), gain_one, w_one, docs),
        [rows_low, head_in, far((SEQ, d), BF16), head_far, head_far, head_far, head_far, lse_out],
        "attend_own", 0,
        [keep_low, head_keep, head_keep, head_keep, sems(6)],
    )
    *up_mine, down_a_mine, down_b_mine = after((*up_mine, *down_mine), n)
    down_mine = [down_a_mine, down_b_mine]
    up_halves = [over_x(v) for v in up_mine]
    down_halves = [over_x(v) for v in down_mine]
    *w_halves, wo_a, wo_b = after((*w_halves, *wo_halves), n)
    w_pieces, wo_pieces = spread(w_halves), spread((wo_a, wo_b))
    w_two, wo_two, q_two, k_two, v_two, att_two, lse_two, attn_sum = call(
        second_kernel, (color1,), (n, *own(w_pieces), *own(wo_pieces), docs, att_near, wo_one),
        [far((3 * width, d), BF16), far((width, d), BF16)] + [head_far] * 4 + [lse_out, rows_low],
        "attend_other", long_cost,
        [pltpu.VMEM((3 * width, d), BF16), pltpu.VMEM((width, d), BF16)] + [head_keep] * 4
        + [sems(14)], mib=15,
    )
    attn_sum, *up_halves = after((attn_sum, *up_halves), attn_sum)
    attn_recv = over_core(attn_sum)
    up_pieces = spread(up_halves)

    grad_out = far((h, piece, units), BF16)
    keep_up, keep_down = pltpu.VMEM((d, units), BF16), pltpu.VMEM((units, d), BF16)
    keep = [pltpu.VMEM((SEQ, units), BF16), pltpu.VMEM((SEQ, units), BF16)]
    grad_all = [pltpu.VMEM((n_dp, piece, units), BF16)] * 2
    orders = (swapped, natural)
    hidden, mlp_in, out_one, back_one, down_a, down_as, up_a, up_as = call(
        functools.partial(mlp_first_kernel, orders), (s1, me_swap, me_nat),
        (*apart((tokens, cotangent, up_weight, down_weight)), attn_sum, attn_recv, gain_two),
        [far((SEQ, d), BF16), rows_low, rows_low, rows_low] + [grad_out] * 4, "mlp_own", 0,
        [keep_low, keep_low, keep_up, keep_down, keep_low] + keep + grad_all + [sems(NBLK + 8)], mib=19,
    )
    down_pieces = spread(after(down_halves, mlp_in))
    up_ra = over_dp(up_as, 0)
    down_ra = over_dp(down_as, 1)
    mlp_sum, back_both, down_b, down_bs, up_b, up_bs = call(
        functools.partial(mlp_second_kernel, orders), (s1, me_swap, me_nat, color1),
        (mlp_in, out_one, back_one, Far(cotangent), *own(up_pieces), *own(down_pieces)),
        [far((SEQ, d), BF16), both_open] + [grad_out] * 4, "mlp_other", long_cost,
        [keep_low, keep_up, keep_down, keep_low] + keep + grad_all + [sems(14)], mib=16,
    )
    mlp_recv = over_core(mlp_sum)
    back_both = swap_cores(back_both)
    up_rb = over_dp(up_bs, 0)
    down_rb = over_dp(down_bs, 1)

    block_start, block_low = call(
        block_kernel, (s1, c1), apart((hidden, after((mlp_sum,), back_both)[0], mlp_recv)),
        [far(tokens.shape, BF16), sds((SEQ // 2, d), BF16)], "block_out", 0,
        [keep_low, keep_low, keep_low, keep_low, sems(4 * NBLK)],
    )
    block_one = over_x(block_low)
    (back_both,) = after((back_both,), block_low)
    go_out = far((n_dp, piece, width), BF16)
    go_keep = pltpu.VMEM((n_dp, piece, width), BF16)
    hidden_grad, da_one, da_two, go_one, go_two = call(
        functools.partial(middle_kernel, natural), (s1, me_nat),
        (*apart((hidden, cotangent, wo_one, wo_two, att_one, att_two)), back_both, gain_two),
        [far((SEQ, d), BF16), head_in, head_in, go_out, go_out], "middle", long_cost,
        [keep_low, keep_low] + [pltpu.VMEM((width, d), BF16)] * 2
        + [head_keep, head_keep, keep_low, keep_low, go_keep, go_keep, sems(4 * NBLK + 6)], mib=14,
    )

    wide = 4 * width
    qkv_out = [far((h, piece, wide), BF16)] * 2
    back_scratch = [head_keep] * 3 + [pltpu.VMEM((heads, SEQ, SEQ), BF16), pltpu.VMEM((n_dp, piece, wide), BF16)]
    back_scratch += [sems(2)]
    in_one, g_b, g_bs = call(
        functools.partial(attend_back, False, natural), (me_nat,),
        (q_two, k_two, v_two, att_two, da_two, lse_two, docs, n_far, w_two, go_two), [rows_wide, *qkv_out],
        "attend_back_other", 0, back_scratch, mib=14,
    )
    g_rb = over_dp(g_bs, 0)

    def adds(name, results):
        args, plan, outs = [], [], []

        def place(array):
            for i, known in enumerate(args):
                if known is array:
                    return i
            args.append(array)
            return len(args) - 1

        for dtype, pieces, rows, lanes, segments in results:
            plan.append([(*seg[:4], [(place(v), first, lane) for v, first, lane in seg[4]]) for seg in segments])
            outs.append(sds((pieces, rows, lanes), dtype))
        return call(functools.partial(add_kernel, plan), (), free(args), outs, name, 0)

    def plain(dtype, count, *terms):
        rows, lanes = terms[0][0].shape[1:]
        return (dtype, count, rows, lanes, [(0, count, 0, lanes, [(v, first, 0) for v, first in terms])])

    def split(count, *arrays):
        return [plain(F32, count, *[(v, 0) for v in arrays]), plain(BF16, count, *[(v, count) for v in arrays])]

    def side_by_side(dtype, count, first, *groups):
        lane, segments = 0, []
        for arrays in groups:
            lanes = arrays[0].shape[2]
            segments.append((0, count, lane, lanes, [(v, first, 0) for v in arrays]))
            lane += lanes
        return (dtype, count, piece, lane, segments)

    def fill(start, one):
        both = swap_cores(jnp.stack([one, one]))
        (out,) = call(
            fill_kernel, (s1,), (both, start), [sds(start.shape, start.dtype)], "fill", 0,
            in_specs=[VREF, ANYREF],
            out_specs=[pl.BlockSpec((SEQ // 2, d), lambda i, s_ref, *_: ((1 - s_ref[0]) * 2 + i, 0))],
            grid=(2,), aliases={2: 0},
        )
        return out

    up_ra, up_rb, down_ra, down_rb = after((up_ra, up_rb, down_ra, down_rb), in_one)
    up_2, up_s2, down_2, down_s2 = adds(
        "reduce_mlp_one",
        [plain(F32, h, (up_a, 0), (up_ra, 0)), plain(BF16, h, (up_b, 0), (up_rb, 0))]
        + [plain(F32, h, (down_a, 0), (down_ra, 0)), plain(BF16, h, (down_b, 0), (down_rb, 0))],
    )
    up_r2, down_r2 = over_x(up_s2), over_x(down_s2)
    (in_one,) = after((in_one,), up_s2)
    in_both, g_a, g_as = call(
        functools.partial(attend_back, True, natural), (me_nat,),
        (q_one, k_one, v_one, att_one, da_one, lse_one, docs, n_far, w_one, go_one, in_one), [both_open] + qkv_out,
        "attend_back_own", 0, back_scratch, mib=14,
    )
    g_ra = over_dp(g_as, 0)
    g_rb, block_one = after((g_rb, block_one), g_a)
    g_b2, g_bs2 = adds("reduce_other_one", split(q, g_b, g_rb))
    g_rb2 = over_dp(g_bs2, 1)
    (in_both,) = after((in_both,), g_bs2)
    in_both = swap_cores(in_both)

    input_start, input_low = call(
        last_kernel, (s1, c1), (Far(tokens), Far(hidden_grad), in_both, gain_one),
        [far(tokens.shape, F32), sds((SEQ // 2, d), BF16)], "norm_back", 0,
        [keep_low, keep_low, keep_wide, sems(4 * NBLK)], mib=14,
    )
    up_r2, down_r2, g_rb2 = after((up_r2, down_r2, g_rb2), input_low)
    up_3, up_s3, down_3, down_s3, g_bx = adds(
        "reduce_mlp_two", split(q, up_2, up_r2) + split(q, down_2, down_r2) + [plain(BF16, q, (g_b2, 0), (g_rb2, 0))]
    )
    up_r3, down_r3 = over_dp(up_s3, 1), over_dp(down_s3, 0)
    g_rx = over_x(g_bx)
    (input_low,) = after((input_low,), g_bx)
    input_one = over_x(input_low)
    (g_ra,) = after((g_ra,), g_bx)
    g_a2, g_as2 = adds("reduce_own_one", split(q, g_a, g_ra))
    g_ra2 = over_dp(g_as2, 1)
    last = q // 2
    up_r3, down_r3 = after((up_r3, down_r3), g_as2)
    mlp_4, mlp_s4 = adds(
        "reduce_mlp_three", [
            side_by_side(dtype, last, start, (up_3, up_r3), (down_3, down_r3)) for dtype, start in ((F32, 0), (BF16, last))
        ]
    )
    mlp_r4 = over_dp(mlp_s4, natural[2])
    block_out, block_one = after((block_start, block_one), mlp_s4)
    block_out = fill(block_out, block_one)
    g_ra2, g_rx = after((g_ra2, g_rx), block_out)
    g_4, g_s4 = adds("reduce_own_two", split(last, g_a2, g_ra2, g_rx))
    g_r4 = over_dp(g_s4, natural[2])
    input_grad, input_one = after((input_start, input_one), g_s4)
    input_grad = fill(input_grad, input_one)
    mlp_r4, g_r4 = after((mlp_r4, g_r4), input_grad)
    mlp_5 = mlp_4 + mlp_r4.astype(F32)

    def other_steps(total):
        for bit in natural[3:]:
            count = total.shape[0] // 2
            got = over_dp(total[count:].astype(BF16), bit)
            total = total[:count] + got.astype(F32)
        return total[0]

    mlp_part, g_part = other_steps(mlp_5), other_steps(g_4 + g_r4.astype(F32))
    up_part, down_part = mlp_part[:, :units], mlp_part[:, units:]
    qkv_flat, out_part = g_part[:, : 3 * width], g_part[:, 3 * width :]
    start = me * piece
    w_rows = lax.dynamic_slice_in_dim(qkv_weight, start, piece, 0).reshape(piece, 3 * width).astype(F32)
    up_rows = lax.dynamic_slice_in_dim(up_weight, start, piece, 0).astype(F32)
    gains = jnp.stack([jnp.sum(w_rows * qkv_flat, 1), jnp.sum(up_rows * up_part, 1)])
    gains = gains + over_core(gains)
    gains = gains + over_x(gains)
    gains = gains / lax.dynamic_slice_in_dim(jnp.stack([attn_gain, mlp_gain]), start, piece, 1)
    qkv_part = qkv_flat.reshape(piece, 3, width)
    return (block_out, input_grad, gains[0], qkv_part, out_part.T, gains[1], up_part, down_part.T)


def solution(mesh):
    in_specs = (
        P("dp", None),
        P("dp"),
        P(),
        P(None, None, "tensor"),
        P("tensor", None),
        P(),
        P(None, "tensor"),
        P("tensor", None),
        P("dp", None),
    )
    out_specs = (
        P("dp", None),
        P("dp", None),
        P("dp"),
        P("dp", None, "tensor"),
        P("tensor", "dp"),
        P("dp"),
        P("dp", "tensor"),
        P("tensor", "dp"),
    )
    body = functools.partial(on_device, n_dp=mesh.shape["dp"], n_tensor=mesh.shape["tensor"])
    return jax.shard_map(body, mesh=mesh, in_specs=in_specs, out_specs=out_specs, check_vma=False)
```

```python
import functools
import math

import jax
import jax.numpy as jnp
from jax import lax
from jax.experimental import pallas as pl
from jax.experimental.pallas import tpu as pltpu
from jax.sharding import PartitionSpec as P

HEAD = 64
SEQ = 1024
BLK = 256
NBLK = SEQ // BLK
EPS = 1e-05
VMEM_BYTES = 14 * 1024 * 1024
F32 = jnp.float32
BF16 = jnp.bfloat16
C0 = math.sqrt(2.0 / math.pi)
C1 = 0.044715
NEG = -1e30

NN = (((1,), (0,)), ((), ()))
NT = (((1,), (1,)), ((), ()))
TN = (((0,), (0,)), ((), ()))


def mm(a, b, dims):
    return lax.dot_general(a, b, dims, preferred_element_type=F32)


def normed(rows):
    centered = rows - jnp.mean(rows, -1, keepdims=True)
    inverse = lax.rsqrt(jnp.mean(centered * centered, -1, keepdims=True) + EPS)
    return centered * inverse, inverse


def norm_back(grad_rows, unit, inverse, gain):
    scaled = grad_rows * gain
    first = jnp.mean(scaled, -1, keepdims=True)
    second = jnp.mean(scaled * unit, -1, keepdims=True)
    return inverse * (scaled - first - unit * second)


def head_mask(rows, width, h):
    lane = lax.broadcasted_iota(jnp.int32, (rows, width), 1)
    return (lane >= h * HEAD) & (lane < (h + 1) * HEAD)


def mapped(index, order):
    bits = len(order)
    return sum(((index >> b) & 1) << (bits - 1 - i) for i, b in enumerate(order))


def put_pieces(all_ref, me, grad, order, base=0, lane=0):
    rows = all_ref.shape[1]
    width = grad.shape[1]
    for p in range(grad.shape[0] // rows):
        place = mapped(p + base // rows, order) ^ me
        all_ref[place, :, lane : lane + width] = grad[p * rows : (p + 1) * rows].astype(BF16)


def block(i):
    return slice(i * BLK, (i + 1) * BLK)


def send_out(pairs, sems, base=0):
    copies = [pltpu.make_async_copy(src, dst, sems.at[base + i]) for i, (src, dst) in enumerate(pairs)]
    for one in copies:
        one.start()
    return copies


def wait_all(copies):
    for one in copies:
        one.wait()


def pieces_out(all_ref, refs):
    count = refs[0].shape[0]
    return [(all_ref.at[i * count : (i + 1) * count], ref) for i, ref in enumerate(refs)]


def quarters_in(whole_ref, color, pieces):
    rows = pieces[0].shape[0]
    at = [2 * color, 2 * color + 1, 2 * (1 - color), 2 * (1 - color) + 1]
    return [(ref, whole_ref.at[pl.ds(pl.multiple_of(i * rows, 16), rows)]) for i, ref in zip(at, pieces)]


def forward_scores(q_ref, k_ref, qb, h):
    width = q_ref.shape[1]
    rows = slice(qb * BLK, (qb + 1) * BLK)
    queries = q_ref[rows] * jnp.asarray(0.125, BF16)
    q_h = jnp.where(head_mask(BLK, width, h), queries, jnp.zeros_like(queries))
    return mm(q_h, k_ref[: (qb + 1) * BLK], NT)


def forward_allowed(docs_ref, qb):
    base, end = qb * BLK, (qb + 1) * BLK
    column = jnp.transpose(jnp.broadcast_to(docs_ref[0, :, base:end], (128, BLK)))
    docs_q = jnp.concatenate([column] * (end // 128), 1)
    at_row = lax.broadcasted_iota(jnp.int32, (BLK, end), 0) + base
    at_col = lax.broadcasted_iota(jnp.int32, (BLK, end), 1)
    return (docs_q == docs_ref[0, :, :end]) & (at_col <= at_row)


def forward_attention(q_ref, k_ref, v_ref, docs_ref, lse_ref, att_ref, ahead=2):
    width = q_ref.shape[1]
    heads = width // HEAD
    items = [(qb, h) for qb in range(NBLK) for h in range(heads)]
    pending = [forward_scores(q_ref, k_ref, *items[i]) for i in range(ahead)]
    for i, (qb, h) in enumerate(items):
        rows = slice(qb * BLK, (qb + 1) * BLK)
        if i + ahead < len(items):
            pending.append(forward_scores(q_ref, k_ref, *items[i + ahead]))
        if h == 0:
            allowed = forward_allowed(docs_ref, qb)
            total = jnp.zeros((BLK, width), F32)
        s = jnp.where(allowed, pending.pop(0), NEG)
        row_max = jnp.max(s, -1, keepdims=True)
        e = jnp.exp(s - row_max)
        row_sum = jnp.sum(e, -1, keepdims=True)
        out = mm(e.astype(BF16), v_ref[: (qb + 1) * BLK], NN)
        total = jnp.where(head_mask(BLK, width, h), out / row_sum, total)
        lse = row_max + jnp.log(row_sum)
        lse_ref[h : h + 1, rows] = jnp.transpose(jnp.broadcast_to(lse, (BLK, 128)))[:1]
        if h == heads - 1:
            att_ref[rows] = total.astype(BF16)


def over_blocks(body):
    def step(i, carry):
        body(pl.ds(pl.multiple_of(i * BLK, BLK), BLK))
        return carry

    lax.fori_loop(0, NBLK, step, 0)


def project(n_ref, w_ref, refs):
    width = refs[0].shape[1]
    for i, ref in enumerate(refs):
        ref[...] = mm(n_ref[...], w_ref[i * width : (i + 1) * width], NT).astype(BF16)


def pick_kernel(color_ref, *refs):
    count = (len(refs) - 1) // 3
    sems = refs[-1]
    pairs = []
    for i in range(count):
        src = refs[i]
        rows = src.shape[0] // 4
        for j in range(2):
            at = pl.ds(pl.multiple_of((2 * color_ref[0] + j) * rows, 16), rows)
            pairs.append((src.at[at], refs[count + 2 * i + j]))
    wait_all(send_out(pairs, sems))


def first_kernel(
    s_ref, x_ref, gain_ref, w_ref, docs_ref,
    n_ref, att_ref, n_out, q_out, k_out, v_out, att_out, lse_ref, x_vmem, q_ref, k_ref, v_ref, sems,
):
    mine = pl.ds(pl.multiple_of(s_ref[0] * SEQ, SEQ), SEQ)
    wait_all(send_out([(x_ref.at[mine], x_vmem)], sems, 5))
    for i in range(NBLK):
        unit, _ = normed(x_vmem[block(i)].astype(F32))
        n_ref[block(i)] = (unit * gain_ref[0:1]).astype(BF16)
    project(n_ref, w_ref, (q_ref, k_ref, v_ref))
    copies = send_out([(n_ref, n_out), (q_ref, q_out), (k_ref, k_out), (v_ref, v_out)], sems)
    forward_attention(q_ref, k_ref, v_ref, docs_ref, lse_ref, att_ref)
    wait_all(copies + send_out([(att_ref, att_out)], sems, 4))


def second_kernel(
    color_ref, n_ref, wa_ref, wb_ref, wc_ref, wd_ref, wo_any, docs_ref, att_one_ref, wo_one_ref,
    w_out, q_out, k_out, v_out, att_out, lse_ref, sum_ref,
    w_ref, wo_ref, q_ref, k_ref, v_ref, att_ref, sems,
):
    color = color_ref[0]
    loads = send_out(quarters_in(w_ref, color, (wa_ref, wb_ref, wc_ref, wd_ref)), sems, 6)
    loads_wo = send_out([(wo_any, wo_ref)], sems, 10)
    wait_all(loads)
    project(n_ref, w_ref, (q_ref, k_ref, v_ref))
    wait_all(loads_wo)
    copies = send_out([(w_ref, w_out), (q_ref, q_out), (k_ref, k_out), (v_ref, v_out)], sems)
    forward_attention(q_ref, k_ref, v_ref, docs_ref, lse_ref, att_ref)
    copies += send_out([(att_ref, att_out)], sems, 5)
    for i in range(NBLK):
        total = mm(att_one_ref[block(i)], wo_one_ref[...], NN) + mm(att_ref[block(i)], wo_ref[...], NN)
        sum_ref[block(i)] = total.astype(BF16)
    wait_all(copies)


def gelu_pair(u):
    square = u * u
    th = jnp.tanh(u * (C0 + (C0 * C1) * square))
    half = 0.5 * u
    act = half + half * th
    slope = 0.5 + 0.5 * th + half * (1.0 - th * th) * (C0 + (3.0 * C0 * C1) * square)
    return act, slope


def mlp_rows(rows, in_ref, cot, up_ref, down_ref, act_ref, back_in_ref):
    act, slope = gelu_pair(mm(in_ref[rows], up_ref[...], NN))
    act = act.astype(BF16)
    act_ref[rows] = act
    back_in = (mm(cot, down_ref[...], NT) * slope).astype(BF16)
    back_in_ref[rows] = back_in
    return mm(act, down_ref[...], NN), mm(back_in, up_ref[...], NT)


def grad_pieces(order, me_ref, left_ref, right_ref, all_ref):
    wide = left_ref.shape[1] // 2

    def one_half(j, carry):
        lanes = pl.ds(pl.multiple_of(j * wide, 128), wide)
        put_pieces(all_ref, me_ref[0], mm(left_ref[:, lanes], right_ref[...], TN), order, j * wide)
        return carry

    lax.fori_loop(0, 2, one_half, 0)


def mlp_first_kernel(
    orders, s_ref, me_down_ref, me_up_ref, x_any, cot_any, up_any, down_any, a_ref, b_ref, gain_ref,
    hidden_any, in_any, out_any, back_any, down_keep, down_send, up_keep, up_send,
    x_ref, cot_ref, up_ref, down_ref, hidden_ref, in_ref, out_ref, back_ref, act_ref, back_in_ref, down_all, up_all,
    sems,
):
    loads = []
    for i in range(NBLK):
        at = pl.ds(pl.multiple_of(s_ref[0] * SEQ + i * BLK, BLK), BLK)
        loads.append(send_out([(x_any.at[at], x_ref.at[block(i)])], sems, i))
    mine = pl.ds(pl.multiple_of(s_ref[0] * SEQ, SEQ), SEQ)
    loads_more = send_out([(up_any, up_ref), (cot_any.at[mine], cot_ref), (down_any, down_ref)], sems, NBLK)
    for i in range(NBLK):
        wait_all(loads[i])
        rows = block(i)
        hidden = x_ref[rows].astype(F32) + (a_ref[rows].astype(F32) + b_ref[rows].astype(F32))
        hidden_ref[rows] = hidden.astype(BF16)
        unit, _ = normed(hidden)
        in_ref[rows] = (unit * gain_ref[1:2]).astype(BF16)
    copies = send_out([(hidden_ref, hidden_any), (in_ref, in_any)], sems, NBLK + 8)
    wait_all(loads_more)

    def one_block(rows):
        out, back = mlp_rows(rows, in_ref, cot_ref[rows], up_ref, down_ref, act_ref, back_in_ref)
        out_ref[rows] = out.astype(BF16)
        back_ref[rows] = back.astype(BF16)

    over_blocks(one_block)
    copies += send_out([(out_ref, out_any), (back_ref, back_any)], sems, NBLK + 10)
    grad_pieces(orders[0], me_down_ref, cot_ref, act_ref, down_all)
    copies += send_out(pieces_out(down_all, (down_keep, down_send)), sems, NBLK + 4)
    grad_pieces(orders[1], me_up_ref, in_ref, back_in_ref, up_all)
    wait_all(copies + send_out(pieces_out(up_all, (up_keep, up_send)), sems, NBLK + 6))


def mlp_second_kernel(
    orders, s_ref, c_ref, me_down_ref, me_up_ref, color_ref, in_any, out_one_any, back_one_any, cot_any,
    ua_ref, ub_ref, uc_ref, ud_ref, da_ref, db_ref, dc_ref, dd_ref,
    out_keep, out_send, both_ref, down_keep, down_send, up_keep, up_send,
    in_ref, out_one_ref, back_one_ref, cot_ref, up_ref, down_ref, out_ref, act_ref, back_in_ref, down_all, up_all, sems,
):
    color = color_ref[0]
    mine = pl.ds(pl.multiple_of(s_ref[0] * SEQ, SEQ), SEQ)
    loads = send_out(quarters_in(up_ref, color, (ua_ref, ub_ref, uc_ref, ud_ref)), sems)
    loads += send_out([(cot_any.at[mine], cot_ref)], sems, 4)
    loads += send_out([(in_any, in_ref)], sems, 16)
    late = [(out_one_any, out_one_ref, 17), (back_one_any, back_one_ref, 18)]
    loads += send_out(quarters_in(down_ref, color, (da_ref, db_ref, dc_ref, dd_ref)), sems, 5)
    for src, dst, i in late:
        pltpu.make_async_copy(src, dst, sems.at[i]).start()
    wait_all(loads)
    for src, dst, i in late:
        pltpu.make_async_copy(src, dst, sems.at[i]).wait()

    def one_block(rows):
        out, back = mlp_rows(rows, in_ref, cot_ref[rows], up_ref, down_ref, act_ref, back_in_ref)
        out_ref[rows] = (out_one_ref[rows].astype(F32) + out).astype(BF16)
        back = (back_one_ref[rows].astype(F32) + back).astype(BF16)
        both_ref[0, rows] = back
        both_ref[1, rows] = back

    over_blocks(one_block)
    half = SEQ // 2
    parts = [pl.ds(pl.multiple_of(c * half, half), half) for c in (c_ref[0], 1 - c_ref[0])]
    copies = send_out([(out_ref.at[parts[0]], out_keep), (out_ref.at[parts[1]], out_send)], sems, 14)
    grad_pieces(orders[0], me_down_ref, cot_ref, act_ref, down_all)
    copies += send_out(pieces_out(down_all, (down_keep, down_send)), sems, 10)
    grad_pieces(orders[1], me_up_ref, in_ref, back_in_ref, up_all)
    wait_all(copies + send_out(pieces_out(up_all, (up_keep, up_send)), sems, 12))


def middle_kernel(
    order, s_ref, me_ref, hidden_any, cot_any, wo_one_any, wo_two_any, att_one_any, att_two_any, both_ref, gain_ref,
    grad_any, da_one_ref, da_two_ref, go_one_any, go_two_any,
    hidden_ref, cot_ref, wo_one_ref, wo_two_ref, att_one_ref, att_two_ref, grad_ref, low_ref, go_one, go_two, sems,
):
    at = [pl.ds(pl.multiple_of(s_ref[0] * SEQ + i * BLK, BLK), BLK) for i in range(NBLK)]
    loads = []
    for i in range(NBLK):
        rows = block(i)
        pairs = [
            (hidden_any.at[rows], hidden_ref.at[rows]),
            (cot_any.at[at[i]], cot_ref.at[rows]),
        ]
        loads.append(send_out(pairs, sems, 3 * i))
        if i == 0:
            loads_wo = send_out([(wo_one_any, wo_one_ref), (wo_two_any, wo_two_ref)], sems, 3 * NBLK)
    loads_att = send_out([(att_one_any, att_one_ref), (att_two_any, att_two_ref)], sems, 3 * NBLK + 2)
    copies = []
    for i in range(NBLK):
        rows = block(i)
        wait_all(loads[i])
        unit, inverse = normed(hidden_ref[rows].astype(F32))
        grad = both_ref[0, rows].astype(F32) + both_ref[1, rows].astype(F32)
        hidden_grad = cot_ref[rows].astype(F32) + norm_back(grad, unit, inverse, gain_ref[1:2])
        grad_ref[rows] = hidden_grad.astype(BF16)
        copies += send_out([(grad_ref.at[rows], grad_any.at[rows])], sems, 3 * NBLK + 4 + i)
        low = hidden_grad.astype(BF16)
        low_ref[rows] = low
        if i == 0:
            wait_all(loads_wo)
        da_one_ref[rows] = mm(low, wo_one_ref[...], NT).astype(BF16)
        da_two_ref[rows] = mm(low, wo_two_ref[...], NT).astype(BF16)
    wait_all(loads_att)
    put_pieces(go_one, me_ref[0], mm(low_ref[...], att_one_ref[...], TN), order)
    put_pieces(go_two, me_ref[0], mm(low_ref[...], att_two_ref[...], TN), order)
    wait_all(copies + send_out([(go_one, go_one_any), (go_two, go_two_any)], sems, 4 * NBLK + 4))


def attend_back(
    add_first, order, me_ref, q_ref, k_ref, v_ref, att_ref, da_ref, lse_ref, docs_ref, n_ref, w_ref, go_ref, *rest
):
    if add_first:
        before_ref, both_ref = rest[:2]
    else:
        (sum_ref,) = rest[:1]
    *grad_refs, dq_ref, dk_ref, dv_ref, ds_ref, all_ref, sems = rest[1 + add_first :]
    width = q_ref.shape[1]
    heads = width // HEAD
    eighth = jnp.asarray(0.125, BF16)
    prod = da_ref[...].astype(F32) * att_ref[...].astype(F32)
    pick_lane = lax.broadcasted_iota(jnp.int32, (8, width), 1)
    pick_row = lax.broadcasted_iota(jnp.int32, (8, width), 0)
    pick = jnp.where((pick_lane >= pick_row * HEAD) & (pick_lane < (pick_row + 1) * HEAD), 1.0, 0.0).astype(F32)
    inner = lax.dot_general(pick, prod, NT, precision=lax.Precision.HIGHEST, preferred_element_type=F32)
    for kb in range(NBLK):
        keys = slice(kb * BLK, (kb + 1) * BLK)
        start = kb * BLK
        count = SEQ - start
        column = jnp.transpose(jnp.broadcast_to(docs_ref[0, :, keys], (128, BLK)))
        docs_k = jnp.concatenate([column] * (count // 128), 1)
        at_row = lax.broadcasted_iota(jnp.int32, (BLK, count), 0)
        at_col = lax.broadcasted_iota(jnp.int32, (BLK, count), 1)
        allowed = (docs_k == docs_ref[0, :, start:]) & (at_row <= at_col)
        dk = jnp.zeros((BLK, width), F32)
        dv = jnp.zeros((BLK, width), F32)
        for h in range(heads):
            mask = head_mask(count, width, h)
            q_h = jnp.where(mask, q_ref[start:] * eighth, jnp.zeros((count, width), BF16))
            da_h = jnp.where(mask, da_ref[start:], jnp.zeros((count, width), BF16))
            s = mm(k_ref[keys], q_h, NT) - lse_ref[h : h + 1, start:]
            p = jnp.exp(jnp.where(allowed, s, NEG))
            dp = mm(v_ref[keys], da_h, NT)
            ds = (p * (dp - inner[h : h + 1, start:])).astype(BF16)
            ds_ref[h, keys, start:] = ds
            dv = dv + mm(p.astype(BF16), da_h, NN)
            dk = dk + mm(ds, q_h, NN)
        dk_ref[keys] = dk.astype(BF16)
        dv_ref[keys] = dv.astype(BF16)
    for qb in range(NBLK):
        rows = slice(qb * BLK, (qb + 1) * BLK)
        end = (qb + 1) * BLK
        dq = jnp.zeros((BLK, width), F32)
        for h in range(heads):
            k_h = jnp.where(head_mask(end, width, h), k_ref[:end] * eighth, jnp.zeros((end, width), BF16))
            dq = dq + mm(ds_ref[h, :end, rows], k_h, TN)
        dq_ref[rows] = dq.astype(BF16)
    for qb in range(NBLK):
        rows = slice(qb * BLK, (qb + 1) * BLK)
        total = mm(dq_ref[rows], w_ref[:width], NN)
        total = total + mm(dk_ref[rows], w_ref[width : 2 * width], NN)
        total = total + mm(dv_ref[rows], w_ref[2 * width :], NN)
        if add_first:
            total = (before_ref[rows] + total).astype(BF16)
            both_ref[0, rows] = total
            both_ref[1, rows] = total
        else:
            sum_ref[rows] = total
    n = n_ref[...]
    all_ref[:, :, 3 * width :] = go_ref[...]
    for i, ref in enumerate((dq_ref, dk_ref, dv_ref)):
        put_pieces(all_ref, me_ref[0], mm(n, ref[...], TN), order, 0, i * width)
    wait_all(send_out(pieces_out(all_ref, grad_refs), sems))


def last_kernel(
    s_ref, c_ref, x_any, grad_any, both_ref, gain_ref, out_any, low_ref, x_ref, grad_ref, out_ref, sems,
):
    at = [pl.ds(pl.multiple_of(s_ref[0] * SEQ + i * BLK, BLK), BLK) for i in range(NBLK)]
    loads = []
    for i in range(NBLK):
        rows = block(i)
        pairs = [
            (x_any.at[at[i]], x_ref.at[rows]),
            (grad_any.at[rows], grad_ref.at[rows]),
        ]
        loads.append(send_out(pairs, sems, 3 * i))
    stores = []
    for i in range(NBLK):
        rows = block(i)
        wait_all(loads[i])
        unit, inverse = normed(x_ref[rows].astype(F32))
        grad = both_ref[0, rows].astype(F32) + both_ref[1, rows].astype(F32)
        out = grad_ref[rows].astype(F32) + norm_back(grad, unit, inverse, gain_ref[0:1])
        out_ref[rows] = out
        stores += send_out([(out_ref.at[rows], out_any.at[at[i]])], sems, 3 * NBLK + i)
    half = low_ref.shape[0]
    low_ref[...] = out_ref[pl.ds(pl.multiple_of(c_ref[0] * half, half), half)].astype(BF16)
    wait_all(stores)


def block_kernel(c_ref, hidden_any, a_any, b_any, low_ref, hidden_ref, a_ref, b_ref, sems):
    half = SEQ // 2
    mine = pl.multiple_of(c_ref[0] * half, half)
    loads = []
    for i in range(half // BLK):
        rows = block(i)
        pairs = [(hidden_any.at[pl.ds(mine + i * BLK, BLK)], hidden_ref.at[rows])]
        pairs += [(a_any.at[rows], a_ref.at[rows]), (b_any.at[rows], b_ref.at[rows])]
        loads.append(send_out(pairs, sems, 3 * i))
    for i in range(half // BLK):
        rows = block(i)
        wait_all(loads[i])
        low_ref[rows] = (hidden_ref[rows].astype(F32) + (a_ref[rows].astype(F32) + b_ref[rows].astype(F32))).astype(BF16)


def fill_kernel(s_ref, both_ref, before_ref, out_ref):
    out_ref[...] = both_ref[pl.program_id(0)].astype(out_ref.dtype)


def place_kernel(s_ref, both_ref, out_ref):
    half = out_ref.shape[0]
    step = pl.program_id(0)
    other = jnp.where(step // 2 == s_ref[0], 0, half)
    out_ref[...] = both_ref[step % 2, pl.ds(pl.multiple_of(other, half), half)]


def add_kernel(plan, *refs):
    outs = refs[len(refs) - len(plan) :]
    for out, segments in zip(outs, plan):
        for place, count, lane, width, terms in segments:
            for j in range(count):
                total = None
                for index, first, start in terms:
                    term = refs[index][first + j, :, start : start + width].astype(F32)
                    total = term if total is None else total + term
                out[place + j, :, lane : lane + width] = total.astype(out.dtype)


VREF = pl.BlockSpec(memory_space=pltpu.VMEM)
SREF = pl.BlockSpec(memory_space=pltpu.SMEM)
ANYREF = pl.BlockSpec(memory_space=pl.ANY)


def vm(shape, dtype):
    return pltpu.VMEM(shape, dtype)


def far(shape, dtype):
    return pltpu.HBM(shape, dtype)


def sds(shape, dtype):
    return jax.ShapeDtypeStruct(shape, dtype)


def fast(v):
    return pltpu.with_memory_space_constraint(v, pltpu.VMEM)


class Free:
    def __init__(self, value):
        self.value = value


class Own(Free):
    pass


class Window(Free):
    pass


class Far(Own):
    pass


def call(
    kernel, scalars, args, outs, name, flops, scratch=(), in_specs=None, out_specs=None, grid=None, aliases=None, mib=14
):
    params = pltpu.CompilerParams(vmem_limit_bytes=mib * 1024 * 1024)
    cost = pl.CostEstimate(flops=int(flops), bytes_accessed=0, transcendentals=0)
    if grid is None:
        specs = [ANYREF if isinstance(a, Own) else VREF for a in args]
        args = [placed(a) for a in args]
        out_specs = [
            ANYREF if isinstance(o, Own) or getattr(o, "memory_space", None) == pltpu.HBM else VREF for o in outs
        ]
        outs = [o.value if isinstance(o, Free) else o for o in outs]
        return pl.pallas_call(
            kernel,
            out_shape=outs,
            in_specs=[SREF] * len(scalars) + specs,
            out_specs=out_specs,
            scratch_shapes=list(scratch),
            compiler_params=params,
            cost_estimate=cost,
            name=name,
        )(*scalars, *args)
    return pl.pallas_call(
        kernel,
        out_shape=outs,
        grid_spec=pltpu.PrefetchScalarGridSpec(
            num_scalar_prefetch=len(scalars),
            grid=grid,
            in_specs=[VREF] * len(args) if in_specs is None else in_specs,
            out_specs=out_specs,
            scratch_shapes=list(scratch),
        ),
        input_output_aliases=aliases or {},
        compiler_params=params,
        cost_estimate=cost,
        name=name,
    )(*scalars, *args)


def placed(a):
    if isinstance(a, Far):
        return pltpu.with_memory_space_constraint(a.value, pltpu.HBM)
    return a.value if isinstance(a, Free) else fast(a)


def free(values):
    return [Free(v) for v in values]


def own(values):
    return [Own(v) for v in values]


def apart(values):
    return [Far(v) for v in values]


def sems(count):
    return pltpu.SemaphoreType.DMA((count,))


def after(values, *done):
    kept = lax.optimization_barrier((tuple(values), done))
    return kept[0]


def on_device(
    tokens, documents, attn_gain, qkv_weight, out_weight, mlp_gain, up_weight, down_weight, cotangent, *, n_dp, n_tensor
):
    d = tokens.shape[1]
    width = qkv_weight.shape[2]
    units = up_weight.shape[1]
    heads = width // HEAD
    piece = d // n_dp
    bits = n_dp.bit_length() - 1
    natural = list(range(bits))
    swapped = [1, 0] + natural[2:]
    t = lax.axis_index("tensor").astype(jnp.int32)
    me = lax.axis_index("dp").astype(jnp.int32)
    s, c = t // 2, t % 2
    color = (me ^ (me >> 1)) & 1
    s1, c1, color1 = s.reshape(1), c.reshape(1), color.reshape(1)
    me_nat, me_swap = mapped(me, natural).reshape(1), mapped(me, swapped).reshape(1)

    def over_x(v):
        return lax.ppermute(v, "tensor", [(i, i ^ 2) for i in range(n_tensor)])

    def over_core(v):
        return lax.ppermute(v, "tensor", [(i, i ^ 1) for i in range(n_tensor)])

    def swap_cores(both):
        groups = [[i, i ^ 1] for i in range(0, n_tensor, 2)]
        return lax.all_to_all(both, "tensor", split_axis=0, concat_axis=0, axis_index_groups=groups)

    def over_dp(v, bit):
        return lax.ppermute(v, "dp", [(i, i ^ (1 << bit)) for i in range(n_dp)])

    h, q = n_dp // 2, n_dp // 4

    def pick(weights, name):
        outs = [Window(far((w.shape[0] // 4, w.shape[1]), BF16)) for w in weights for _ in range(2)]
        got = call(
            pick_kernel, (color1,), [Far(w) for w in weights], outs, name, 0,
            [pltpu.SemaphoreType.DMA((len(outs),))],
        )
        return [got[2 * i : 2 * i + 2] for i in range(len(weights))]

    def spread(pair):
        return [*pair, over_dp(pair[0], 0), over_dp(pair[1], 1)]

    w_one = jnp.transpose(qkv_weight, (1, 2, 0)).reshape(3 * width, d)
    wo_one = out_weight
    w_mine, up_mine, down_mine = pick([w_one, up_weight, down_weight], "pick")
    w_halves = [over_x(v) for v in w_mine]
    wo_two = over_x(wo_one)

    docs = documents.astype(F32).reshape(tokens.shape[0] // SEQ, 1, SEQ)
    docs = lax.dynamic_slice_in_dim(docs, s, 1, 0)
    both_gains = jnp.stack([attn_gain, mlp_gain])
    head_far, head_in = far((SEQ, width), BF16), vm((SEQ, width), BF16)
    head_keep = pltpu.VMEM((SEQ, width), BF16)
    keep_low, keep_wide, keep_both = pltpu.VMEM((SEQ, d), BF16), pltpu.VMEM((SEQ, d), F32), pltpu.VMEM((2, SEQ, d), BF16)
    both_open, half_far = vm((2, SEQ, d), BF16), far((SEQ // 2, d), BF16)
    rows_low, rows_wide, rows_open = vm((SEQ, d), BF16), vm((SEQ, d), F32), sds((SEQ, d), BF16)
    lse_out = vm((8, SEQ), F32)
    low_open = sds((BLK, d), BF16)
    long_cost, some_cost = 10**12, 2 * 10**10

    n, att_near, n_far, q_one, k_one, v_one, att_one, lse_one = call(
        first_kernel, (s1,), (Far(tokens), both_gains, w_one, docs),
        [rows_low, head_in, far((SEQ, d), BF16), head_far, head_far, head_far, head_far, lse_out],
        "attend_own", 0,
        [keep_low, head_keep, head_keep, head_keep, sems(6)],
    )
    *up_mine, down_a_mine, down_b_mine = after((*up_mine, *down_mine), n)
    down_mine = [down_a_mine, down_b_mine]
    up_halves = [over_x(v) for v in up_mine]
    down_halves = [over_x(v) for v in down_mine]
    w_pieces = spread(after(w_halves, n))
    w_two, q_two, k_two, v_two, att_two, lse_two, attn_sum = call(
        second_kernel, (color1,), (n, *own(w_pieces), Own(wo_two), docs, att_near, wo_one),
        [far((3 * width, d), BF16)] + [head_far] * 4 + [lse_out, rows_low],
        "attend_other", long_cost,
        [pltpu.VMEM((3 * width, d), BF16), pltpu.VMEM((width, d), BF16)] + [head_keep] * 4
        + [sems(14)], mib=15,
    )
    attn_sum, *up_halves = after((attn_sum, *up_halves), attn_sum)
    attn_recv = over_core(attn_sum)
    up_pieces = spread(up_halves)

    grad_out = far((h, piece, units), BF16)
    keep_up, keep_down = pltpu.VMEM((d, units), BF16), pltpu.VMEM((units, d), BF16)
    keep = [pltpu.VMEM((SEQ, units), BF16), pltpu.VMEM((SEQ, units), BF16)]
    grad_all = [pltpu.VMEM((n_dp, piece, units), BF16)] * 2
    orders = (swapped, natural)
    hidden, mlp_in, out_one, back_one, down_a, down_as, up_a, up_as = call(
        functools.partial(mlp_first_kernel, orders), (s1, me_swap, me_nat),
        (*apart((tokens, cotangent, up_weight, down_weight)), attn_sum, attn_recv, both_gains),
        [far((SEQ, d), BF16)] * 4 + [grad_out] * 4, "mlp_own", 0,
        [keep_low, keep_low, keep_up, keep_down] + [keep_low] * 4 + keep + grad_all + [sems(NBLK + 12)], mib=22,
    )
    down_pieces = spread(after(down_halves, mlp_in))
    up_ra = over_dp(up_as, 0)
    down_ra = over_dp(down_as, 1)
    mlp_keep, mlp_send, back_both, down_b, down_bs, up_b, up_bs = call(
        functools.partial(mlp_second_kernel, orders), (s1, c1, me_swap, me_nat, color1),
        (*apart((mlp_in, out_one, back_one, cotangent)), *own(up_pieces), *own(down_pieces)),
        [half_far, half_far, both_open] + [grad_out] * 4, "mlp_other", some_cost,
        [keep_low] * 4 + [keep_up, keep_down, keep_low] + keep + grad_all + [sems(19)], mib=19,
    )
    mlp_recv = over_core(mlp_send)
    back_both = swap_cores(back_both)
    up_rb = over_dp(up_bs, 0)
    down_rb = over_dp(down_bs, 1)

    half_keep = pltpu.VMEM((SEQ // 2, d), BF16)
    (block_low,) = call(
        block_kernel, (c1,), apart((hidden, after((mlp_keep,), back_both)[0], mlp_recv)), [sds((SEQ // 2, d), BF16)],
        "block_out", 0, [half_keep, half_keep, half_keep, sems(3 * NBLK)],
    )
    block_one = over_x(block_low)
    (back_both,) = after((back_both,), block_low)
    go_out = far((n_dp, piece, width), BF16)
    go_keep = pltpu.VMEM((n_dp, piece, width), BF16)
    hidden_grad, da_one, da_two, go_one, go_two = call(
        functools.partial(middle_kernel, natural), (s1, me_nat),
        (*apart((hidden, cotangent, wo_one, wo_two, att_one, att_two)), back_both, both_gains),
        [far((SEQ, d), BF16), head_in, head_in, go_out, go_out], "middle", some_cost,
        [keep_low, keep_low] + [pltpu.VMEM((width, d), BF16)] * 2
        + [head_keep, head_keep, keep_low, keep_low, go_keep, go_keep, sems(4 * NBLK + 6)], mib=12,
    )

    wide = 4 * width
    qkv_out = [far((h, piece, wide), BF16)] * 2
    back_scratch = [head_keep] * 3 + [pltpu.VMEM((heads, SEQ, SEQ), BF16), pltpu.VMEM((n_dp, piece, wide), BF16)]
    back_scratch += [sems(2)]
    in_one, g_b, g_bs = call(
        functools.partial(attend_back, False, natural), (me_nat,),
        (q_two, k_two, v_two, att_two, da_two, lse_two, docs, n_far, w_two, go_two), [rows_wide, *qkv_out],
        "attend_back_other", 0, back_scratch, mib=14,
    )
    g_rb = over_dp(g_bs, 0)

    def adds(name, results):
        args, plan, outs = [], [], []

        def place(array):
            for i, known in enumerate(args):
                if known is array:
                    return i
            args.append(array)
            return len(args) - 1

        for dtype, pieces, rows, lanes, segments in results:
            plan.append([(*seg[:4], [(place(v), first, lane) for v, first, lane in seg[4]]) for seg in segments])
            outs.append(sds((pieces, rows, lanes), dtype))
        return call(functools.partial(add_kernel, plan), (), free(args), outs, name, 0)

    def plain(dtype, count, *terms):
        rows, lanes = terms[0][0].shape[1:]
        return (dtype, count, rows, lanes, [(0, count, 0, lanes, [(v, first, 0) for v, first in terms])])

    def split(count, *arrays):
        return [plain(F32, count, *[(v, 0) for v in arrays]), plain(BF16, count, *[(v, count) for v in arrays])]

    def side_by_side(dtype, count, first, *groups):
        lane, segments = 0, []
        for arrays in groups:
            lanes = arrays[0].shape[2]
            segments.append((0, count, lane, lanes, [(v, first, 0) for v in arrays]))
            lane += lanes
        return (dtype, count, piece, lane, segments)

    def fill(start, one):
        both = swap_cores(jnp.stack([one, one]))
        (out,) = call(
            fill_kernel, (s1,), (both, start), [sds(start.shape, start.dtype)], "fill", 0,
            in_specs=[VREF, ANYREF],
            out_specs=[pl.BlockSpec((SEQ // 2, d), lambda i, s_ref, *_: ((1 - s_ref[0]) * 2 + i, 0))],
            grid=(2,), aliases={2: 0},
        )
        return out

    up_ra, up_rb, down_ra, down_rb = after((up_ra, up_rb, down_ra, down_rb), in_one)
    up_s2, down_s2 = adds(
        "reduce_mlp_one", [plain(BF16, h, (up_b, 0), (up_rb, 0)), plain(BF16, h, (down_b, 0), (down_rb, 0))]
    )
    up_r2, down_r2 = over_x(up_s2), over_x(down_s2)
    (in_one,) = after((in_one,), up_s2)
    in_both, g_a, g_as = call(
        functools.partial(attend_back, True, natural), (me_nat,),
        (q_one, k_one, v_one, att_one, da_one, lse_one, docs, n_far, w_one, go_one, in_one), [both_open] + qkv_out,
        "attend_back_own", 0, back_scratch, mib=14,
    )
    g_ra = over_dp(g_as, 0)
    g_rb, block_one = after((g_rb, block_one), g_a)
    g_b2, g_bs2 = adds("reduce_other_one", split(q, g_b, g_rb))
    g_rb2 = over_dp(g_bs2, 1)
    (in_both,) = after((in_both,), g_bs2)
    in_both = swap_cores(in_both)

    input_start, input_low = call(
        last_kernel, (s1, c1), (Far(tokens), Far(hidden_grad), in_both, both_gains),
        [far(tokens.shape, F32), sds((SEQ // 2, d), BF16)], "norm_back", 0,
        [keep_low, keep_low, keep_wide, sems(4 * NBLK)], mib=14,
    )
    up_r2, down_r2, g_rb2 = after((up_r2, down_r2, g_rb2), input_low)
    up_3, up_s3, down_3, down_s3, g_bx = adds(
        "reduce_mlp_two", split(q, up_a, up_ra, up_r2) + split(q, down_a, down_ra, down_r2) + [plain(BF16, q, (g_b2, 0), (g_rb2, 0))]
    )
    up_r3, down_r3 = over_dp(up_s3, 1), over_dp(down_s3, 0)
    g_rx = over_x(g_bx)
    (input_low,) = after((input_low,), g_bx)
    input_one = over_x(input_low)
    (g_ra,) = after((g_ra,), g_bx)
    g_a2, g_as2 = adds("reduce_own_one", split(q, g_a, g_ra))
    g_ra2 = over_dp(g_as2, 1)
    last = q // 2
    up_r3, down_r3 = after((up_r3, down_r3), g_as2)
    mlp_4, mlp_s4 = adds(
        "reduce_mlp_three", [
            side_by_side(dtype, last, start, (up_3, up_r3), (down_3, down_r3)) for dtype, start in ((F32, 0), (BF16, last))
        ]
    )
    mlp_r4 = over_dp(mlp_s4, natural[2])
    block_both = jnp.concatenate(after((block_low, block_one), mlp_s4))
    block_both = swap_cores(jnp.stack([block_both, block_both]))
    (block_out,) = call(
        place_kernel, (s1,), (block_both,), [sds(tokens.shape, BF16)], "place", 0,
        in_specs=[VREF], out_specs=[pl.BlockSpec((SEQ // 2, d), lambda i, *_: (i, 0))], grid=(4,),
    )
    g_ra2, g_rx = after((g_ra2, g_rx), block_out)
    g_4, g_s4 = adds("reduce_own_two", split(last, g_a2, g_ra2, g_rx))
    g_r4 = over_dp(g_s4, natural[2])
    input_grad, input_one = after((input_start, input_one), g_s4)
    input_grad = fill(input_grad, input_one)
    mlp_r4, g_r4 = after((mlp_r4, g_r4), input_grad)
    mlp_5 = mlp_4 + mlp_r4.astype(F32)

    def other_steps(total):
        for bit in natural[3:]:
            count = total.shape[0] // 2
            got = over_dp(total[count:].astype(BF16), bit)
            total = total[:count] + got.astype(F32)
        return total[0]

    mlp_part, g_part = other_steps(mlp_5), other_steps(g_4 + g_r4.astype(F32))
    up_part, down_part = mlp_part[:, :units], mlp_part[:, units:]
    qkv_flat, out_part = g_part[:, : 3 * width], g_part[:, 3 * width :]
    start = me * piece
    w_rows = lax.dynamic_slice_in_dim(qkv_weight, start, piece, 0).reshape(piece, 3 * width).astype(F32)
    up_rows = lax.dynamic_slice_in_dim(up_weight, start, piece, 0).astype(F32)
    gains = jnp.stack([jnp.sum(w_rows * qkv_flat, 1), jnp.sum(up_rows * up_part, 1)])
    gains = gains + over_core(gains)
    gains = gains + over_x(gains)
    gains = gains / lax.dynamic_slice_in_dim(jnp.stack([attn_gain, mlp_gain]), start, piece, 1)
    qkv_part = qkv_flat.reshape(piece, 3, width)
    return (block_out, input_grad, gains[0], qkv_part, out_part.T, gains[1], up_part, down_part.T)


def solution(mesh):
    in_specs = (
        P("dp", None),
        P("dp"),
        P(),
        P(None, None, "tensor"),
        P("tensor", None),
        P(),
        P(None, "tensor"),
        P("tensor", None),
        P("dp", None),
    )
    out_specs = (
        P("dp", None),
        P("dp", None),
        P("dp"),
        P("dp", None, "tensor"),
        P("tensor", "dp"),
        P("dp"),
        P("dp", "tensor"),
        P("tensor", "dp"),
    )
    body = functools.partial(on_device, n_dp=mesh.shape["dp"], n_tensor=mesh.shape["tensor"])
    return jax.shard_map(body, mesh=mesh, in_specs=in_specs, out_specs=out_specs, check_vma=False)
```

```python
import functools
import math

import jax
import jax.numpy as jnp
from jax import lax
from jax.experimental import pallas as pl
from jax.experimental.pallas import tpu as pltpu
from jax.sharding import PartitionSpec as P

HEAD = 64
SEQ = 1024
BLK = 256
NBLK = SEQ // BLK
EPS = 1e-05
VMEM_BYTES = 14 * 1024 * 1024
F32 = jnp.float32
BF16 = jnp.bfloat16
C0 = math.sqrt(2.0 / math.pi)
C1 = 0.044715
NEG = -1e30

NN = (((1,), (0,)), ((), ()))
NT = (((1,), (1,)), ((), ()))
TN = (((0,), (0,)), ((), ()))


def mm(a, b, dims):
    return lax.dot_general(a, b, dims, preferred_element_type=F32)


def normed(rows):
    centered = rows - jnp.mean(rows, -1, keepdims=True)
    inverse = lax.rsqrt(jnp.mean(centered * centered, -1, keepdims=True) + EPS)
    return centered * inverse, inverse


def norm_back(grad_rows, unit, inverse, gain):
    scaled = grad_rows * gain
    first = jnp.mean(scaled, -1, keepdims=True)
    second = jnp.mean(scaled * unit, -1, keepdims=True)
    return inverse * (scaled - first - unit * second)


def head_mask(rows, width, h):
    lane = lax.broadcasted_iota(jnp.int32, (rows, width), 1)
    return (lane >= h * HEAD) & (lane < (h + 1) * HEAD)


def mapped(index, order):
    bits = len(order)
    return sum(((index >> b) & 1) << (bits - 1 - i) for i, b in enumerate(order))


def put_pieces(all_ref, me, grad, order, base=0, lane=0):
    rows = all_ref.shape[1]
    width = grad.shape[1]
    for p in range(grad.shape[0] // rows):
        place = mapped(p + base // rows, order) ^ me
        all_ref[place, :, lane : lane + width] = grad[p * rows : (p + 1) * rows].astype(BF16)


def block(i):
    return slice(i * BLK, (i + 1) * BLK)


def send_out(pairs, sems, base=0):
    copies = [pltpu.make_async_copy(src, dst, sems.at[base + i]) for i, (src, dst) in enumerate(pairs)]
    for one in copies:
        one.start()
    return copies


def wait_all(copies):
    for one in copies:
        one.wait()


def pieces_out(all_ref, refs):
    count = refs[0].shape[0]
    return [(all_ref.at[i * count : (i + 1) * count], ref) for i, ref in enumerate(refs)]


def quarters_in(whole_ref, color, pieces):
    rows = pieces[0].shape[0]
    at = [2 * color, 2 * color + 1, 2 * (1 - color), 2 * (1 - color) + 1]
    return [(ref, whole_ref.at[pl.ds(pl.multiple_of(i * rows, 16), rows)]) for i, ref in zip(at, pieces)]


def forward_scores(q_ref, k_ref, qb, h):
    width = q_ref.shape[1]
    rows = slice(qb * BLK, (qb + 1) * BLK)
    queries = q_ref[rows] * jnp.asarray(0.125, BF16)
    q_h = jnp.where(head_mask(BLK, width, h), queries, jnp.zeros_like(queries))
    return mm(q_h, k_ref[: (qb + 1) * BLK], NT)


def forward_allowed(docs_ref, qb):
    base, end = qb * BLK, (qb + 1) * BLK
    column = jnp.transpose(jnp.broadcast_to(docs_ref[0, :, base:end], (128, BLK)))
    docs_q = jnp.concatenate([column] * (end // 128), 1)
    at_row = lax.broadcasted_iota(jnp.int32, (BLK, end), 0) + base
    at_col = lax.broadcasted_iota(jnp.int32, (BLK, end), 1)
    return (docs_q == docs_ref[0, :, :end]) & (at_col <= at_row)


def forward_attention(q_ref, k_ref, v_ref, docs_ref, lse_ref, att_ref, ahead=2):
    width = q_ref.shape[1]
    heads = width // HEAD
    items = [(qb, h) for qb in range(NBLK) for h in range(heads)]
    pending = [forward_scores(q_ref, k_ref, *items[i]) for i in range(ahead)]
    for i, (qb, h) in enumerate(items):
        rows = slice(qb * BLK, (qb + 1) * BLK)
        if i + ahead < len(items):
            pending.append(forward_scores(q_ref, k_ref, *items[i + ahead]))
        if h == 0:
            allowed = forward_allowed(docs_ref, qb)
            total = jnp.zeros((BLK, width), F32)
        s = jnp.where(allowed, pending.pop(0), NEG)
        row_max = jnp.max(s, -1, keepdims=True)
        e = jnp.exp(s - row_max)
        row_sum = jnp.sum(e, -1, keepdims=True)
        out = mm(e.astype(BF16), v_ref[: (qb + 1) * BLK], NN)
        total = jnp.where(head_mask(BLK, width, h), out / row_sum, total)
        lse = row_max + jnp.log(row_sum)
        lse_ref[h : h + 1, rows] = jnp.transpose(jnp.broadcast_to(lse, (BLK, 128)))[:1]
        if h == heads - 1:
            att_ref[rows] = total.astype(BF16)


def over_blocks(body):
    def step(i, carry):
        body(pl.ds(pl.multiple_of(i * BLK, BLK), BLK))
        return carry

    lax.fori_loop(0, NBLK, step, 0)


def project(n_ref, w_ref, refs):
    width = refs[0].shape[1]
    for i, ref in enumerate(refs):
        ref[...] = mm(n_ref[...], w_ref[i * width : (i + 1) * width], NT).astype(BF16)


def pick_kernel(color_ref, *refs):
    count = (len(refs) - 1) // 3
    sems = refs[-1]
    pairs = []
    for i in range(count):
        src = refs[i]
        rows = src.shape[0] // 4
        for j in range(2):
            at = pl.ds(pl.multiple_of((2 * color_ref[0] + j) * rows, 16), rows)
            pairs.append((src.at[at], refs[count + 2 * i + j]))
    wait_all(send_out(pairs, sems))


def first_kernel(
    s_ref, x_ref, gain_ref, w_ref, docs_ref,
    n_ref, att_ref, n_out, q_out, k_out, v_out, att_out, lse_ref, x_vmem, q_ref, k_ref, v_ref, sems,
):
    mine = pl.ds(pl.multiple_of(s_ref[0] * SEQ, SEQ), SEQ)
    wait_all(send_out([(x_ref.at[mine], x_vmem)], sems, 5))
    for i in range(NBLK):
        unit, _ = normed(x_vmem[block(i)].astype(F32))
        n_ref[block(i)] = (unit * gain_ref[0:1]).astype(BF16)
    project(n_ref, w_ref, (q_ref, k_ref, v_ref))
    copies = send_out([(n_ref, n_out), (q_ref, q_out), (k_ref, k_out), (v_ref, v_out)], sems)
    forward_attention(q_ref, k_ref, v_ref, docs_ref, lse_ref, att_ref)
    wait_all(copies + send_out([(att_ref, att_out)], sems, 4))


def second_kernel(
    color_ref, n_ref, wa_ref, wb_ref, wc_ref, wd_ref, wo_any, docs_ref, att_one_ref, wo_one_ref,
    w_out, q_out, k_out, v_out, att_out, lse_ref, sum_ref,
    w_ref, wo_ref, q_ref, k_ref, v_ref, att_ref, sems,
):
    color = color_ref[0]
    loads = send_out(quarters_in(w_ref, color, (wa_ref, wb_ref, wc_ref, wd_ref)), sems, 6)
    loads_wo = send_out([(wo_any, wo_ref)], sems, 10)
    wait_all(loads)
    project(n_ref, w_ref, (q_ref, k_ref, v_ref))
    wait_all(loads_wo)
    copies = send_out([(w_ref, w_out), (q_ref, q_out), (k_ref, k_out), (v_ref, v_out)], sems)
    forward_attention(q_ref, k_ref, v_ref, docs_ref, lse_ref, att_ref)
    copies += send_out([(att_ref, att_out)], sems, 5)
    for i in range(NBLK):
        total = mm(att_one_ref[block(i)], wo_one_ref[...], NN) + mm(att_ref[block(i)], wo_ref[...], NN)
        sum_ref[block(i)] = total.astype(BF16)
    wait_all(copies)


def gelu_pair(u):
    square = u * u
    th = jnp.tanh(u * (C0 + (C0 * C1) * square))
    half = 0.5 * u
    act = half + half * th
    slope = 0.5 + 0.5 * th + half * (1.0 - th * th) * (C0 + (3.0 * C0 * C1) * square)
    return act, slope


def mlp_rows(rows, in_ref, cot, up_ref, down_ref, act_ref, back_in_ref):
    act, slope = gelu_pair(mm(in_ref[rows], up_ref[...], NN))
    act = act.astype(BF16)
    act_ref[rows] = act
    back_in = (mm(cot, down_ref[...], NT) * slope).astype(BF16)
    back_in_ref[rows] = back_in
    return mm(act, down_ref[...], NN), mm(back_in, up_ref[...], NT)


def grad_pieces(order, me_ref, left_ref, right_ref, all_ref):
    wide = left_ref.shape[1] // 2

    def one_half(j, carry):
        lanes = pl.ds(pl.multiple_of(j * wide, 128), wide)
        put_pieces(all_ref, me_ref[0], mm(left_ref[:, lanes], right_ref[...], TN), order, j * wide)
        return carry

    lax.fori_loop(0, 2, one_half, 0)


def mlp_first_kernel(
    orders, s_ref, me_down_ref, me_up_ref, x_any, cot_any, up_any, down_any, a_ref, b_ref, gain_ref,
    hidden_any, in_any, out_any, back_any, down_keep, down_send, up_keep, up_send,
    x_ref, cot_ref, up_ref, down_ref, hidden_ref, in_ref, out_ref, back_ref, act_ref, back_in_ref, down_all, up_all,
    sems,
):
    loads = []
    for i in range(NBLK):
        at = pl.ds(pl.multiple_of(s_ref[0] * SEQ + i * BLK, BLK), BLK)
        loads.append(send_out([(x_any.at[at], x_ref.at[block(i)])], sems, i))
    mine = pl.ds(pl.multiple_of(s_ref[0] * SEQ, SEQ), SEQ)
    loads_more = send_out([(up_any, up_ref), (cot_any.at[mine], cot_ref), (down_any, down_ref)], sems, NBLK)
    for i in range(NBLK):
        wait_all(loads[i])
        rows = block(i)
        hidden = x_ref[rows].astype(F32) + (a_ref[rows].astype(F32) + b_ref[rows].astype(F32))
        hidden_ref[rows] = hidden.astype(BF16)
        unit, _ = normed(hidden)
        in_ref[rows] = (unit * gain_ref[1:2]).astype(BF16)
    copies = send_out([(hidden_ref, hidden_any), (in_ref, in_any)], sems, NBLK + 8)
    wait_all(loads_more)

    def one_block(rows):
        out, back = mlp_rows(rows, in_ref, cot_ref[rows], up_ref, down_ref, act_ref, back_in_ref)
        out_ref[rows] = out.astype(BF16)
        back_ref[rows] = back.astype(BF16)

    over_blocks(one_block)
    copies += send_out([(out_ref, out_any), (back_ref, back_any)], sems, NBLK + 10)
    grad_pieces(orders[0], me_down_ref, cot_ref, act_ref, down_all)
    copies += send_out(pieces_out(down_all, (down_keep, down_send)), sems, NBLK + 4)
    grad_pieces(orders[1], me_up_ref, in_ref, back_in_ref, up_all)
    wait_all(copies + send_out(pieces_out(up_all, (up_keep, up_send)), sems, NBLK + 6))


def mlp_second_kernel(
    orders, s_ref, c_ref, me_down_ref, me_up_ref, color_ref, in_any, out_one_any, back_one_any, cot_any,
    ua_ref, ub_ref, uc_ref, ud_ref, da_ref, db_ref, dc_ref, dd_ref,
    out_keep, out_send, both_ref, down_keep, down_send, up_keep, up_send,
    in_ref, out_one_ref, back_one_ref, cot_ref, up_ref, down_ref, out_ref, act_ref, back_in_ref, down_all, up_all, sems,
):
    color = color_ref[0]
    mine = pl.ds(pl.multiple_of(s_ref[0] * SEQ, SEQ), SEQ)
    loads = send_out(quarters_in(up_ref, color, (ua_ref, ub_ref, uc_ref, ud_ref)), sems)
    loads += send_out([(cot_any.at[mine], cot_ref)], sems, 4)
    loads += send_out([(in_any, in_ref)], sems, 16)
    late = [(out_one_any, out_one_ref, 17), (back_one_any, back_one_ref, 18)]
    loads += send_out(quarters_in(down_ref, color, (da_ref, db_ref, dc_ref, dd_ref)), sems, 5)
    for src, dst, i in late:
        pltpu.make_async_copy(src, dst, sems.at[i]).start()
    wait_all(loads)
    for src, dst, i in late:
        pltpu.make_async_copy(src, dst, sems.at[i]).wait()

    def one_block(rows):
        out, back = mlp_rows(rows, in_ref, cot_ref[rows], up_ref, down_ref, act_ref, back_in_ref)
        out_ref[rows] = (out_one_ref[rows].astype(F32) + out).astype(BF16)
        back = (back_one_ref[rows].astype(F32) + back).astype(BF16)
        both_ref[0, rows] = back
        both_ref[1, rows] = back

    over_blocks(one_block)
    half = SEQ // 2
    parts = [pl.ds(pl.multiple_of(c * half, half), half) for c in (c_ref[0], 1 - c_ref[0])]
    copies = send_out([(out_ref.at[parts[0]], out_keep), (out_ref.at[parts[1]], out_send)], sems, 14)
    grad_pieces(orders[0], me_down_ref, cot_ref, act_ref, down_all)
    copies += send_out(pieces_out(down_all, (down_keep, down_send)), sems, 10)
    grad_pieces(orders[1], me_up_ref, in_ref, back_in_ref, up_all)
    wait_all(copies + send_out(pieces_out(up_all, (up_keep, up_send)), sems, 12))


def middle_kernel(
    order, s_ref, me_ref, hidden_any, cot_any, wo_one_any, wo_two_any, att_one_any, att_two_any, both_ref, gain_ref,
    grad_any, da_one_ref, da_two_ref, go_one_any, go_two_any,
    hidden_ref, cot_ref, wo_one_ref, wo_two_ref, att_one_ref, att_two_ref, grad_ref, low_ref, go_one, go_two, sems,
):
    at = [pl.ds(pl.multiple_of(s_ref[0] * SEQ + i * BLK, BLK), BLK) for i in range(NBLK)]
    loads = []
    for i in range(NBLK):
        rows = block(i)
        pairs = [
            (hidden_any.at[rows], hidden_ref.at[rows]),
            (cot_any.at[at[i]], cot_ref.at[rows]),
        ]
        loads.append(send_out(pairs, sems, 3 * i))
        if i == 0:
            loads_wo = send_out([(wo_one_any, wo_one_ref), (wo_two_any, wo_two_ref)], sems, 3 * NBLK)
    loads_att = send_out([(att_one_any, att_one_ref), (att_two_any, att_two_ref)], sems, 3 * NBLK + 2)
    copies = []
    for i in range(NBLK):
        rows = block(i)
        wait_all(loads[i])
        unit, inverse = normed(hidden_ref[rows].astype(F32))
        grad = both_ref[0, rows].astype(F32) + both_ref[1, rows].astype(F32)
        hidden_grad = cot_ref[rows].astype(F32) + norm_back(grad, unit, inverse, gain_ref[1:2])
        grad_ref[rows] = hidden_grad.astype(BF16)
        copies += send_out([(grad_ref.at[rows], grad_any.at[rows])], sems, 3 * NBLK + 4 + i)
        low = hidden_grad.astype(BF16)
        low_ref[rows] = low
        if i == 0:
            wait_all(loads_wo)
        da_one_ref[rows] = mm(low, wo_one_ref[...], NT).astype(BF16)
        da_two_ref[rows] = mm(low, wo_two_ref[...], NT).astype(BF16)
    wait_all(loads_att)
    put_pieces(go_one, me_ref[0], mm(low_ref[...], att_one_ref[...], TN), order)
    put_pieces(go_two, me_ref[0], mm(low_ref[...], att_two_ref[...], TN), order)
    wait_all(copies + send_out([(go_one, go_one_any), (go_two, go_two_any)], sems, 4 * NBLK + 4))


def attend_back(
    add_first, order, me_ref, q_ref, k_ref, v_ref, att_ref, da_ref, lse_ref, docs_ref, n_ref, w_ref, go_ref, *rest
):
    if add_first:
        before_ref, both_ref = rest[:2]
    else:
        (sum_ref,) = rest[:1]
    *grad_refs, dq_ref, dk_ref, dv_ref, ds_ref, all_ref, sems = rest[1 + add_first :]
    width = q_ref.shape[1]
    heads = width // HEAD
    eighth = jnp.asarray(0.125, BF16)
    prod = da_ref[...].astype(F32) * att_ref[...].astype(F32)
    pick_lane = lax.broadcasted_iota(jnp.int32, (8, width), 1)
    pick_row = lax.broadcasted_iota(jnp.int32, (8, width), 0)
    pick = jnp.where((pick_lane >= pick_row * HEAD) & (pick_lane < (pick_row + 1) * HEAD), 1.0, 0.0).astype(BF16)
    high = prod.astype(BF16)
    rest = prod - high.astype(F32)
    middle = rest.astype(BF16)
    inner = mm(pick, high, NT) + mm(pick, middle, NT) + mm(pick, (rest - middle.astype(F32)).astype(BF16), NT)
    for kb in range(NBLK):
        keys = slice(kb * BLK, (kb + 1) * BLK)
        start = kb * BLK
        count = SEQ - start
        column = jnp.transpose(jnp.broadcast_to(docs_ref[0, :, keys], (128, BLK)))
        docs_k = jnp.concatenate([column] * (count // 128), 1)
        at_row = lax.broadcasted_iota(jnp.int32, (BLK, count), 0)
        at_col = lax.broadcasted_iota(jnp.int32, (BLK, count), 1)
        allowed = (docs_k == docs_ref[0, :, start:]) & (at_row <= at_col)
        dk = jnp.zeros((BLK, width), F32)
        dv = jnp.zeros((BLK, width), F32)
        for h in range(heads):
            mask = head_mask(count, width, h)
            q_h = jnp.where(mask, q_ref[start:] * eighth, jnp.zeros((count, width), BF16))
            da_h = jnp.where(mask, da_ref[start:], jnp.zeros((count, width), BF16))
            s = mm(k_ref[keys], q_h, NT) - lse_ref[h : h + 1, start:]
            p = jnp.exp(jnp.where(allowed, s, NEG))
            dp = mm(v_ref[keys], da_h, NT)
            ds = (p * (dp - inner[h : h + 1, start:])).astype(BF16)
            ds_ref[h, keys, start:] = ds
            dv = dv + mm(p.astype(BF16), da_h, NN)
            dk = dk + mm(ds, q_h, NN)
        dk_ref[keys] = dk.astype(BF16)
        dv_ref[keys] = dv.astype(BF16)
    for qb in range(NBLK):
        rows = slice(qb * BLK, (qb + 1) * BLK)
        end = (qb + 1) * BLK
        dq = jnp.zeros((BLK, width), F32)
        for h in range(heads):
            k_h = jnp.where(head_mask(end, width, h), k_ref[:end] * eighth, jnp.zeros((end, width), BF16))
            dq = dq + mm(ds_ref[h, :end, rows], k_h, TN)
        dq_ref[rows] = dq.astype(BF16)
    for qb in range(NBLK):
        rows = slice(qb * BLK, (qb + 1) * BLK)
        total = mm(dq_ref[rows], w_ref[:width], NN)
        total = total + mm(dk_ref[rows], w_ref[width : 2 * width], NN)
        total = total + mm(dv_ref[rows], w_ref[2 * width :], NN)
        if add_first:
            total = (before_ref[rows] + total).astype(BF16)
            both_ref[0, rows] = total
            both_ref[1, rows] = total
        else:
            sum_ref[rows] = total
    n = n_ref[...]
    all_ref[:, :, 3 * width :] = go_ref[...]
    for i, ref in enumerate((dq_ref, dk_ref, dv_ref)):
        put_pieces(all_ref, me_ref[0], mm(n, ref[...], TN), order, 0, i * width)
    wait_all(send_out(pieces_out(all_ref, grad_refs), sems))


def last_kernel(
    s_ref, c_ref, x_any, grad_any, both_ref, gain_ref, out_any, low_ref, x_ref, grad_ref, out_ref, sems,
):
    at = [pl.ds(pl.multiple_of(s_ref[0] * SEQ + i * BLK, BLK), BLK) for i in range(NBLK)]
    loads = []
    for i in range(NBLK):
        rows = block(i)
        pairs = [
            (x_any.at[at[i]], x_ref.at[rows]),
            (grad_any.at[rows], grad_ref.at[rows]),
        ]
        loads.append(send_out(pairs, sems, 3 * i))
    stores = []
    for i in range(NBLK):
        rows = block(i)
        wait_all(loads[i])
        unit, inverse = normed(x_ref[rows].astype(F32))
        grad = both_ref[0, rows].astype(F32) + both_ref[1, rows].astype(F32)
        out = grad_ref[rows].astype(F32) + norm_back(grad, unit, inverse, gain_ref[0:1])
        out_ref[rows] = out
        stores += send_out([(out_ref.at[rows], out_any.at[at[i]])], sems, 3 * NBLK + i)
    half = low_ref.shape[0]
    low_ref[...] = out_ref[pl.ds(pl.multiple_of(c_ref[0] * half, half), half)].astype(BF16)
    wait_all(stores)


def block_kernel(c_ref, hidden_any, a_any, b_any, low_ref, hidden_ref, a_ref, b_ref, sems):
    half = SEQ // 2
    mine = pl.multiple_of(c_ref[0] * half, half)
    loads = []
    for i in range(half // BLK):
        rows = block(i)
        pairs = [(hidden_any.at[pl.ds(mine + i * BLK, BLK)], hidden_ref.at[rows])]
        pairs += [(a_any.at[rows], a_ref.at[rows]), (b_any.at[rows], b_ref.at[rows])]
        loads.append(send_out(pairs, sems, 3 * i))
    for i in range(half // BLK):
        rows = block(i)
        wait_all(loads[i])
        low_ref[rows] = (hidden_ref[rows].astype(F32) + (a_ref[rows].astype(F32) + b_ref[rows].astype(F32))).astype(BF16)


def fill_kernel(s_ref, both_ref, before_ref, out_ref):
    out_ref[...] = both_ref[pl.program_id(0)].astype(out_ref.dtype)


def place_kernel(s_ref, both_ref, out_ref):
    half = out_ref.shape[0]
    step = pl.program_id(0)
    other = jnp.where(step // 2 == s_ref[0], 0, half)
    out_ref[...] = both_ref[step % 2, pl.ds(pl.multiple_of(other, half), half)]


def add_kernel(plan, *refs):
    outs = refs[len(refs) - len(plan) :]
    for out, segments in zip(outs, plan):
        for place, count, lane, width, terms in segments:
            for j in range(count):
                total = None
                for index, first, start in terms:
                    term = refs[index][first + j, :, start : start + width].astype(F32)
                    total = term if total is None else total + term
                out[place + j, :, lane : lane + width] = total.astype(out.dtype)


VREF = pl.BlockSpec(memory_space=pltpu.VMEM)
SREF = pl.BlockSpec(memory_space=pltpu.SMEM)
ANYREF = pl.BlockSpec(memory_space=pl.ANY)


def vm(shape, dtype):
    return pltpu.VMEM(shape, dtype)


def far(shape, dtype):
    return pltpu.HBM(shape, dtype)


def sds(shape, dtype):
    return jax.ShapeDtypeStruct(shape, dtype)


def fast(v):
    return pltpu.with_memory_space_constraint(v, pltpu.VMEM)


class Free:
    def __init__(self, value):
        self.value = value


class Own(Free):
    pass


class Window(Free):
    pass


class Far(Own):
    pass


def call(
    kernel, scalars, args, outs, name, flops, scratch=(), in_specs=None, out_specs=None, grid=None, aliases=None, mib=14
):
    params = pltpu.CompilerParams(vmem_limit_bytes=mib * 1024 * 1024)
    cost = pl.CostEstimate(flops=int(flops), bytes_accessed=0, transcendentals=0)
    if grid is None:
        specs = [ANYREF if isinstance(a, Own) else VREF for a in args]
        args = [placed(a) for a in args]
        out_specs = [
            ANYREF if isinstance(o, Own) or getattr(o, "memory_space", None) == pltpu.HBM else VREF for o in outs
        ]
        outs = [o.value if isinstance(o, Free) else o for o in outs]
        return pl.pallas_call(
            kernel,
            out_shape=outs,
            in_specs=[SREF] * len(scalars) + specs,
            out_specs=out_specs,
            scratch_shapes=list(scratch),
            compiler_params=params,
            cost_estimate=cost,
            name=name,
        )(*scalars, *args)
    return pl.pallas_call(
        kernel,
        out_shape=outs,
        grid_spec=pltpu.PrefetchScalarGridSpec(
            num_scalar_prefetch=len(scalars),
            grid=grid,
            in_specs=[VREF] * len(args) if in_specs is None else in_specs,
            out_specs=out_specs,
            scratch_shapes=list(scratch),
        ),
        input_output_aliases=aliases or {},
        compiler_params=params,
        cost_estimate=cost,
        name=name,
    )(*scalars, *args)


def placed(a):
    if isinstance(a, Far):
        return pltpu.with_memory_space_constraint(a.value, pltpu.HBM)
    return a.value if isinstance(a, Free) else fast(a)


def free(values):
    return [Free(v) for v in values]


def own(values):
    return [Own(v) for v in values]


def apart(values):
    return [Far(v) for v in values]


def sems(count):
    return pltpu.SemaphoreType.DMA((count,))


def after(values, *done):
    kept = lax.optimization_barrier((tuple(values), done))
    return kept[0]


def on_device(
    tokens, documents, attn_gain, qkv_weight, out_weight, mlp_gain, up_weight, down_weight, cotangent, *, n_dp, n_tensor
):
    d = tokens.shape[1]
    width = qkv_weight.shape[2]
    units = up_weight.shape[1]
    heads = width // HEAD
    piece = d // n_dp
    bits = n_dp.bit_length() - 1
    natural = list(range(bits))
    swapped = [1, 0] + natural[2:]
    t = lax.axis_index("tensor").astype(jnp.int32)
    me = lax.axis_index("dp").astype(jnp.int32)
    s, c = t // 2, t % 2
    color = (me ^ (me >> 1)) & 1
    s1, c1, color1 = s.reshape(1), c.reshape(1), color.reshape(1)
    me_nat, me_swap = mapped(me, natural).reshape(1), mapped(me, swapped).reshape(1)

    def over_x(v):
        return lax.ppermute(v, "tensor", [(i, i ^ 2) for i in range(n_tensor)])

    def over_core(v):
        return lax.ppermute(v, "tensor", [(i, i ^ 1) for i in range(n_tensor)])

    def swap_cores(both):
        groups = [[i, i ^ 1] for i in range(0, n_tensor, 2)]
        return lax.all_to_all(both, "tensor", split_axis=0, concat_axis=0, axis_index_groups=groups)

    def over_dp(v, bit):
        return lax.ppermute(v, "dp", [(i, i ^ (1 << bit)) for i in range(n_dp)])

    h, q = n_dp // 2, n_dp // 4

    def pick(weights, name):
        outs = [Window(far((w.shape[0] // 4, w.shape[1]), BF16)) for w in weights for _ in range(2)]
        got = call(
            pick_kernel, (color1,), [Far(w) for w in weights], outs, name, 0,
            [pltpu.SemaphoreType.DMA((len(outs),))],
        )
        return [got[2 * i : 2 * i + 2] for i in range(len(weights))]

    def spread(pair):
        return [*pair, over_dp(pair[0], 0), over_dp(pair[1], 1)]

    w_one = jnp.transpose(qkv_weight, (1, 2, 0)).reshape(3 * width, d)
    wo_one = out_weight
    w_mine, up_mine, down_mine = pick([w_one, up_weight, down_weight], "pick")
    w_halves = [over_x(v) for v in w_mine]
    wo_two = over_x(wo_one)

    docs = documents.astype(F32).reshape(tokens.shape[0] // SEQ, 1, SEQ)
    docs = lax.dynamic_slice_in_dim(docs, s, 1, 0)
    both_gains = jnp.stack([attn_gain, mlp_gain])
    head_far, head_in = far((SEQ, width), BF16), vm((SEQ, width), BF16)
    head_keep = pltpu.VMEM((SEQ, width), BF16)
    keep_low, keep_wide, keep_both = pltpu.VMEM((SEQ, d), BF16), pltpu.VMEM((SEQ, d), F32), pltpu.VMEM((2, SEQ, d), BF16)
    both_open, half_far = vm((2, SEQ, d), BF16), far((SEQ // 2, d), BF16)
    rows_low, rows_wide, rows_open = vm((SEQ, d), BF16), vm((SEQ, d), F32), sds((SEQ, d), BF16)
    lse_out = vm((8, SEQ), F32)
    low_open = sds((BLK, d), BF16)
    long_cost, some_cost = 10**12, 2 * 10**10

    n, att_near, n_far, q_one, k_one, v_one, att_one, lse_one = call(
        first_kernel, (s1,), (Far(tokens), both_gains, w_one, docs),
        [rows_low, head_in, far((SEQ, d), BF16), head_far, head_far, head_far, head_far, lse_out],
        "attend_own", 0,
        [keep_low, head_keep, head_keep, head_keep, sems(6)],
    )
    *up_mine, down_a_mine, down_b_mine = after((*up_mine, *down_mine), n)
    down_mine = [down_a_mine, down_b_mine]
    up_halves = [over_x(v) for v in up_mine]
    down_halves = [over_x(v) for v in down_mine]
    w_pieces = spread(after(w_halves, n))
    w_two, q_two, k_two, v_two, att_two, lse_two, attn_sum = call(
        second_kernel, (color1,), (n, *own(w_pieces), Own(wo_two), docs, att_near, wo_one),
        [far((3 * width, d), BF16)] + [head_far] * 4 + [lse_out, rows_low],
        "attend_other", long_cost,
        [pltpu.VMEM((3 * width, d), BF16), pltpu.VMEM((width, d), BF16)] + [head_keep] * 4
        + [sems(14)], mib=15,
    )
    attn_sum, *up_halves = after((attn_sum, *up_halves), attn_sum)
    attn_recv = over_core(attn_sum)
    up_pieces = spread(up_halves)

    grad_out = far((h, piece, units), BF16)
    keep_up, keep_down = pltpu.VMEM((d, units), BF16), pltpu.VMEM((units, d), BF16)
    keep = [pltpu.VMEM((SEQ, units), BF16), pltpu.VMEM((SEQ, units), BF16)]
    grad_all = [pltpu.VMEM((n_dp, piece, units), BF16)] * 2
    orders = (swapped, natural)
    hidden, mlp_in, out_one, back_one, down_a, down_as, up_a, up_as = call(
        functools.partial(mlp_first_kernel, orders), (s1, me_swap, me_nat),
        (*apart((tokens, cotangent, up_weight, down_weight)), attn_sum, attn_recv, both_gains),
        [far((SEQ, d), BF16)] * 4 + [grad_out] * 4, "mlp_own", 0,
        [keep_low, keep_low, keep_up, keep_down] + [keep_low] * 4 + keep + grad_all + [sems(NBLK + 12)], mib=22,
    )
    down_pieces = spread(after(down_halves, mlp_in))
    up_ra = over_dp(up_as, 0)
    down_ra = over_dp(down_as, 1)
    mlp_keep, mlp_send, back_both, down_b, down_bs, up_b, up_bs = call(
        functools.partial(mlp_second_kernel, orders), (s1, c1, me_swap, me_nat, color1),
        (*apart((mlp_in, out_one, back_one, cotangent)), *own(up_pieces), *own(down_pieces)),
        [half_far, half_far, both_open] + [grad_out] * 4, "mlp_other", some_cost,
        [keep_low] * 4 + [keep_up, keep_down, keep_low] + keep + grad_all + [sems(19)], mib=19,
    )
    mlp_recv = over_core(mlp_send)
    back_both = swap_cores(back_both)
    up_rb = over_dp(up_bs, 0)
    down_rb = over_dp(down_bs, 1)

    half_keep = pltpu.VMEM((SEQ // 2, d), BF16)
    (block_low,) = call(
        block_kernel, (c1,), apart((hidden, after((mlp_keep,), back_both)[0], mlp_recv)), [sds((SEQ // 2, d), BF16)],
        "block_out", 0, [half_keep, half_keep, half_keep, sems(3 * NBLK)],
    )
    block_one = over_x(block_low)
    (back_both,) = after((back_both,), block_low)
    go_out = far((n_dp, piece, width), BF16)
    go_keep = pltpu.VMEM((n_dp, piece, width), BF16)
    hidden_grad, da_one, da_two, go_one, go_two = call(
        functools.partial(middle_kernel, natural), (s1, me_nat),
        (*apart((hidden, cotangent, wo_one, wo_two, att_one, att_two)), back_both, both_gains),
        [far((SEQ, d), BF16), head_in, head_in, go_out, go_out], "middle", some_cost,
        [keep_low, keep_low] + [pltpu.VMEM((width, d), BF16)] * 2
        + [head_keep, head_keep, keep_low, keep_low, go_keep, go_keep, sems(4 * NBLK + 6)], mib=12,
    )

    wide = 4 * width
    qkv_out = [far((h, piece, wide), BF16)] * 2
    back_scratch = [head_keep] * 3 + [pltpu.VMEM((heads, SEQ, SEQ), BF16), pltpu.VMEM((n_dp, piece, wide), BF16)]
    back_scratch += [sems(2)]
    in_one, g_b, g_bs = call(
        functools.partial(attend_back, False, natural), (me_nat,),
        (q_two, k_two, v_two, att_two, da_two, lse_two, docs, n_far, w_two, go_two), [rows_wide, *qkv_out],
        "attend_back_other", 0, back_scratch, mib=14,
    )
    g_rb = over_dp(g_bs, 0)

    def adds(name, results, leave=False):
        args, plan, outs = [], [], []

        def place(array):
            for i, known in enumerate(args):
                if known is array:
                    return i
            args.append(array)
            return len(args) - 1

        for dtype, pieces, rows, lanes, segments in results:
            plan.append([(*seg[:4], [(place(v), first, lane) for v, first, lane in seg[4]]) for seg in segments])
            shape = (pieces, rows, lanes)
            outs.append(Window(far(shape, dtype)) if leave and dtype == BF16 else sds(shape, dtype))
        return call(functools.partial(add_kernel, plan), (), free(args), outs, name, 0)

    def plain(dtype, count, *terms):
        rows, lanes = terms[0][0].shape[1:]
        return (dtype, count, rows, lanes, [(0, count, 0, lanes, [(v, first, 0) for v, first in terms])])

    def split(count, *arrays):
        return [plain(F32, count, *[(v, 0) for v in arrays]), plain(BF16, count, *[(v, count) for v in arrays])]

    def side_by_side(dtype, count, first, *groups):
        lane, segments = 0, []
        for arrays in groups:
            lanes = arrays[0].shape[2]
            segments.append((0, count, lane, lanes, [(v, first, 0) for v in arrays]))
            lane += lanes
        return (dtype, count, piece, lane, segments)

    def fill(start, one):
        both = swap_cores(jnp.stack([one, one]))
        (out,) = call(
            fill_kernel, (s1,), (both, start), [sds(start.shape, start.dtype)], "fill", 0,
            in_specs=[VREF, ANYREF],
            out_specs=[pl.BlockSpec((SEQ // 2, d), lambda i, s_ref, *_: ((1 - s_ref[0]) * 2 + i, 0))],
            grid=(2,), aliases={2: 0},
        )
        return out

    up_ra, up_rb, down_ra, down_rb = after((up_ra, up_rb, down_ra, down_rb), in_one)
    up_s2, down_s2 = adds(
        "reduce_mlp_one", [plain(BF16, h, (up_b, 0), (up_rb, 0)), plain(BF16, h, (down_b, 0), (down_rb, 0))]
    )
    up_r2, down_r2 = over_x(up_s2), over_x(down_s2)
    (in_one,) = after((in_one,), up_s2)
    in_both, g_a, g_as = call(
        functools.partial(attend_back, True, natural), (me_nat,),
        (q_one, k_one, v_one, att_one, da_one, lse_one, docs, n_far, w_one, go_one, in_one), [both_open] + qkv_out,
        "attend_back_own", 0, back_scratch, mib=14,
    )
    g_ra = over_dp(g_as, 0)
    g_rb, block_one = after((g_rb, block_one), g_a)
    g_b2, g_bs2 = adds("reduce_other_one", split(q, g_b, g_rb))
    g_rb2 = over_dp(g_bs2, 1)
    (in_both,) = after((in_both,), g_bs2)
    in_both = swap_cores(in_both)

    input_start, input_low = call(
        last_kernel, (s1, c1), (Far(tokens), Far(hidden_grad), in_both, both_gains),
        [far(tokens.shape, F32), sds((SEQ // 2, d), BF16)], "norm_back", 0,
        [keep_low, keep_low, keep_wide, sems(4 * NBLK)], mib=14,
    )
    up_r2, down_r2, g_rb2 = after((up_r2, down_r2, g_rb2), input_low)
    up_3, up_s3, down_3, down_s3, g_bx = adds(
        "reduce_mlp_two", split(q, up_a, up_ra, up_r2) + split(q, down_a, down_ra, down_r2) + [plain(BF16, q, (g_b2, 0), (g_rb2, 0))],
        leave=True,
    )
    up_r3, down_r3 = over_dp(up_s3, 1), over_dp(down_s3, 0)
    g_rx = over_x(g_bx)
    (input_low,) = after((input_low,), g_bx)
    input_one = over_x(input_low)
    (g_ra,) = after((g_ra,), g_bx)
    g_a2, g_as2 = adds("reduce_own_one", split(q, g_a, g_ra))
    g_ra2 = over_dp(g_as2, 1)
    last = q // 2
    up_r3, down_r3 = after((up_r3, down_r3), g_as2)
    mlp_4, mlp_s4 = adds(
        "reduce_mlp_three", [
            side_by_side(dtype, last, start, (up_3, up_r3), (down_3, down_r3)) for dtype, start in ((F32, 0), (BF16, last))
        ]
    )
    mlp_r4 = over_dp(mlp_s4, natural[2])
    block_both = jnp.concatenate(after((block_low, block_one), mlp_s4))
    block_both = swap_cores(jnp.stack([block_both, block_both]))
    (block_out,) = call(
        place_kernel, (s1,), (block_both,), [sds(tokens.shape, BF16)], "place", 0,
        in_specs=[VREF], out_specs=[pl.BlockSpec((SEQ // 2, d), lambda i, *_: (i, 0))], grid=(4,),
    )
    g_ra2, g_rx = after((g_ra2, g_rx), block_out)
    g_4, g_s4 = adds("reduce_own_two", split(last, g_a2, g_ra2, g_rx))
    g_r4 = over_dp(g_s4, natural[2])
    input_grad, input_one = after((input_start, input_one), g_s4)
    input_grad = fill(input_grad, input_one)
    mlp_r4, g_r4 = after((mlp_r4, g_r4), input_grad)
    mlp_5 = mlp_4 + mlp_r4.astype(F32)

    def other_steps(total):
        for bit in natural[3:]:
            count = total.shape[0] // 2
            got = over_dp(total[count:].astype(BF16), bit)
            total = total[:count] + got.astype(F32)
        return total[0]

    mlp_part, g_part = other_steps(mlp_5), other_steps(g_4 + g_r4.astype(F32))
    up_part, down_part = mlp_part[:, :units], mlp_part[:, units:]
    qkv_flat, out_part = g_part[:, : 3 * width], g_part[:, 3 * width :]
    start = me * piece
    w_rows = lax.dynamic_slice_in_dim(qkv_weight, start, piece, 0).reshape(piece, 3 * width).astype(F32)
    up_rows = lax.dynamic_slice_in_dim(up_weight, start, piece, 0).astype(F32)
    gains = jnp.stack([jnp.sum(w_rows * qkv_flat, 1), jnp.sum(up_rows * up_part, 1)])
    others = [lax.ppermute(gains, "tensor", [(i, i ^ m) for i in range(n_tensor)]) for m in (1, 2, 3)]
    gains = (gains + others[0]) + (others[1] + others[2])
    gains = gains / lax.dynamic_slice_in_dim(jnp.stack([attn_gain, mlp_gain]), start, piece, 1)
    qkv_part = qkv_flat.reshape(piece, 3, width)
    return (block_out, input_grad, gains[0], qkv_part, out_part.T, gains[1], up_part, down_part.T)


def solution(mesh):
    in_specs = (
        P("dp", None),
        P("dp"),
        P(),
        P(None, None, "tensor"),
        P("tensor", None),
        P(),
        P(None, "tensor"),
        P("tensor", None),
        P("dp", None),
    )
    out_specs = (
        P("dp", None),
        P("dp", None),
        P("dp"),
        P("dp", None, "tensor"),
        P("tensor", "dp"),
        P("dp"),
        P("dp", "tensor"),
        P("tensor", "dp"),
    )
    body = functools.partial(on_device, n_dp=mesh.shape["dp"], n_tensor=mesh.shape["tensor"])
    return jax.shard_map(body, mesh=mesh, in_specs=in_specs, out_specs=out_specs, check_vma=False)
```

```python
import functools
import math

import jax
import jax.numpy as jnp
from jax import lax
from jax.experimental import pallas as pl
from jax.experimental.pallas import tpu as pltpu
from jax.sharding import PartitionSpec as P

HEAD = 64
SEQ = 1024
BLK = 256
NBLK = SEQ // BLK
EPS = 1e-05
VMEM_BYTES = 14 * 1024 * 1024
F32 = jnp.float32
BF16 = jnp.bfloat16
C0 = math.sqrt(2.0 / math.pi)
C1 = 0.044715
NEG = -1e30

NN = (((1,), (0,)), ((), ()))
NT = (((1,), (1,)), ((), ()))
TN = (((0,), (0,)), ((), ()))


def mm(a, b, dims):
    return lax.dot_general(a, b, dims, preferred_element_type=F32)


def normed(rows):
    centered = rows - jnp.mean(rows, -1, keepdims=True)
    inverse = lax.rsqrt(jnp.mean(centered * centered, -1, keepdims=True) + EPS)
    return centered * inverse, inverse


def norm_back(grad_rows, unit, inverse, gain):
    scaled = grad_rows * gain
    first = jnp.mean(scaled, -1, keepdims=True)
    second = jnp.mean(scaled * unit, -1, keepdims=True)
    return inverse * (scaled - first - unit * second)


def head_mask(rows, width, h):
    lane = lax.broadcasted_iota(jnp.int32, (rows, width), 1)
    return (lane >= h * HEAD) & (lane < (h + 1) * HEAD)


def mapped(index, order):
    bits = len(order)
    return sum(((index >> b) & 1) << (bits - 1 - i) for i, b in enumerate(order))


def put_pieces(all_ref, me, grad, order, base=0, lane=0):
    rows = all_ref.shape[1]
    width = grad.shape[1]
    for p in range(grad.shape[0] // rows):
        place = mapped(p + base // rows, order) ^ me
        all_ref[place, :, lane : lane + width] = grad[p * rows : (p + 1) * rows].astype(BF16)


def block(i):
    return slice(i * BLK, (i + 1) * BLK)


def send_out(pairs, sems, base=0):
    copies = [pltpu.make_async_copy(src, dst, sems.at[base + i]) for i, (src, dst) in enumerate(pairs)]
    for one in copies:
        one.start()
    return copies


def wait_all(copies):
    for one in copies:
        one.wait()


def pieces_out(all_ref, refs):
    count = refs[0].shape[0]
    return [(all_ref.at[i * count : (i + 1) * count], ref) for i, ref in enumerate(refs)]


def quarters_in(whole_ref, color, pieces):
    rows = pieces[0].shape[0]
    at = [2 * color, 2 * color + 1, 2 * (1 - color), 2 * (1 - color) + 1]
    return [(ref, whole_ref.at[pl.ds(pl.multiple_of(i * rows, 16), rows)]) for i, ref in zip(at, pieces)]


def forward_scores(q_ref, k_ref, qb, h):
    width = q_ref.shape[1]
    rows = slice(qb * BLK, (qb + 1) * BLK)
    queries = q_ref[rows] * jnp.asarray(0.125, BF16)
    q_h = jnp.where(head_mask(BLK, width, h), queries, jnp.zeros_like(queries))
    return mm(q_h, k_ref[: (qb + 1) * BLK], NT)


def forward_allowed(docs_ref, qb):
    base, end = qb * BLK, (qb + 1) * BLK
    column = jnp.transpose(jnp.broadcast_to(docs_ref[0, :, base:end], (128, BLK)))
    docs_q = jnp.concatenate([column] * (end // 128), 1)
    at_row = lax.broadcasted_iota(jnp.int32, (BLK, end), 0) + base
    at_col = lax.broadcasted_iota(jnp.int32, (BLK, end), 1)
    return (docs_q == docs_ref[0, :, :end]) & (at_col <= at_row)


def forward_attention(q_ref, k_ref, v_ref, docs_ref, lse_ref, att_ref, ahead=2):
    width = q_ref.shape[1]
    heads = width // HEAD
    items = [(qb, h) for qb in range(NBLK) for h in range(heads)]
    pending = [forward_scores(q_ref, k_ref, *items[i]) for i in range(ahead)]
    for i, (qb, h) in enumerate(items):
        rows = slice(qb * BLK, (qb + 1) * BLK)
        if i + ahead < len(items):
            pending.append(forward_scores(q_ref, k_ref, *items[i + ahead]))
        if h == 0:
            allowed = forward_allowed(docs_ref, qb)
            total = jnp.zeros((BLK, width), F32)
        s = jnp.where(allowed, pending.pop(0), NEG)
        row_max = jnp.max(s, -1, keepdims=True)
        e = jnp.exp(s - row_max)
        row_sum = jnp.sum(e, -1, keepdims=True)
        out = mm(e.astype(BF16), v_ref[: (qb + 1) * BLK], NN)
        total = jnp.where(head_mask(BLK, width, h), out / row_sum, total)
        lse = row_max + jnp.log(row_sum)
        lse_ref[h : h + 1, rows] = jnp.transpose(jnp.broadcast_to(lse, (BLK, 128)))[:1]
        if h == heads - 1:
            att_ref[rows] = total.astype(BF16)


def over_blocks(body):
    rows = 2 * BLK

    def step(i, carry):
        body(pl.ds(pl.multiple_of(i * rows, rows), rows))
        return carry

    lax.fori_loop(0, SEQ // rows, step, 0)


def project(n_ref, w_ref, refs):
    width = refs[0].shape[1]
    for i, ref in enumerate(refs):
        ref[...] = mm(n_ref[...], w_ref[i * width : (i + 1) * width], NT).astype(BF16)


def pick_kernel(color_ref, *refs):
    count = (len(refs) - 1) // 3
    sems = refs[-1]
    pairs = []
    for i in range(count):
        src = refs[i]
        rows = src.shape[0] // 4
        for j in range(2):
            at = pl.ds(pl.multiple_of((2 * color_ref[0] + j) * rows, 16), rows)
            pairs.append((src.at[at], refs[count + 2 * i + j]))
    wait_all(send_out(pairs, sems))


def first_kernel(
    s_ref, x_ref, gain_ref, w_ref, docs_ref,
    n_ref, att_ref, n_out, q_out, k_out, v_out, att_out, lse_ref, x_vmem, q_ref, k_ref, v_ref, sems,
):
    mine = pl.ds(pl.multiple_of(s_ref[0] * SEQ, SEQ), SEQ)
    wait_all(send_out([(x_ref.at[mine], x_vmem)], sems, 5))
    for i in range(NBLK):
        unit, _ = normed(x_vmem[block(i)].astype(F32))
        n_ref[block(i)] = (unit * gain_ref[0:1]).astype(BF16)
    project(n_ref, w_ref, (q_ref, k_ref, v_ref))
    copies = send_out([(n_ref, n_out), (q_ref, q_out), (k_ref, k_out), (v_ref, v_out)], sems)
    forward_attention(q_ref, k_ref, v_ref, docs_ref, lse_ref, att_ref)
    wait_all(copies + send_out([(att_ref, att_out)], sems, 4))


def second_kernel(
    color_ref, n_ref, wa_ref, wb_ref, wc_ref, wd_ref, wo_any, docs_ref, att_one_ref, wo_one_ref,
    w_out, q_out, k_out, v_out, att_out, lse_ref, sum_ref,
    w_ref, wo_ref, q_ref, k_ref, v_ref, att_ref, sems,
):
    color = color_ref[0]
    loads = send_out(quarters_in(w_ref, color, (wa_ref, wb_ref, wc_ref, wd_ref)), sems, 6)
    loads_wo = send_out([(wo_any, wo_ref)], sems, 10)
    wait_all(loads)
    project(n_ref, w_ref, (q_ref, k_ref, v_ref))
    wait_all(loads_wo)
    copies = send_out([(w_ref, w_out), (q_ref, q_out), (k_ref, k_out), (v_ref, v_out)], sems)
    forward_attention(q_ref, k_ref, v_ref, docs_ref, lse_ref, att_ref)
    copies += send_out([(att_ref, att_out)], sems, 5)
    for i in range(NBLK):
        total = mm(att_one_ref[block(i)], wo_one_ref[...], NN) + mm(att_ref[block(i)], wo_ref[...], NN)
        sum_ref[block(i)] = total.astype(BF16)
    wait_all(copies)


def gelu_pair(u):
    square = u * u
    th = jnp.tanh(u * (C0 + (C0 * C1) * square))
    half = 0.5 * u
    act = half + half * th
    slope = 0.5 + 0.5 * th + half * (1.0 - th * th) * (C0 + (3.0 * C0 * C1) * square)
    return act, slope


def mlp_rows(rows, in_ref, cot, up_ref, down_ref, act_ref, back_in_ref):
    act, slope = gelu_pair(mm(in_ref[rows], up_ref[...], NN))
    act = act.astype(BF16)
    act_ref[rows] = act
    back_in = (mm(cot, down_ref[...], NT) * slope).astype(BF16)
    back_in_ref[rows] = back_in
    return mm(act, down_ref[...], NN), mm(back_in, up_ref[...], NT)


def grad_pieces(order, me_ref, left_ref, right_ref, all_ref):
    wide = left_ref.shape[1] // 2

    def one_half(j, carry):
        lanes = pl.ds(pl.multiple_of(j * wide, 128), wide)
        put_pieces(all_ref, me_ref[0], mm(left_ref[:, lanes], right_ref[...], TN), order, j * wide)
        return carry

    lax.fori_loop(0, 2, one_half, 0)


def mlp_first_kernel(
    orders, s_ref, me_down_ref, me_up_ref, x_any, cot_any, up_any, down_any, a_ref, b_ref, gain_ref,
    hidden_any, in_any, out_any, back_any, down_keep, down_send, up_keep, up_send,
    x_ref, cot_ref, up_ref, down_ref, hidden_ref, in_ref, out_ref, back_ref, act_ref, back_in_ref, down_all, up_all,
    sems,
):
    loads = []
    for i in range(NBLK):
        at = pl.ds(pl.multiple_of(s_ref[0] * SEQ + i * BLK, BLK), BLK)
        loads.append(send_out([(x_any.at[at], x_ref.at[block(i)])], sems, i))
    mine = pl.ds(pl.multiple_of(s_ref[0] * SEQ, SEQ), SEQ)
    loads_more = send_out([(up_any, up_ref), (cot_any.at[mine], cot_ref), (down_any, down_ref)], sems, NBLK)
    for i in range(NBLK):
        wait_all(loads[i])
        rows = block(i)
        hidden = x_ref[rows].astype(F32) + (a_ref[rows].astype(F32) + b_ref[rows].astype(F32))
        hidden_ref[rows] = hidden.astype(BF16)
        unit, _ = normed(hidden)
        in_ref[rows] = (unit * gain_ref[1:2]).astype(BF16)
    copies = send_out([(hidden_ref, hidden_any), (in_ref, in_any)], sems, NBLK + 8)
    wait_all(loads_more)

    def one_block(rows):
        out, back = mlp_rows(rows, in_ref, cot_ref[rows], up_ref, down_ref, act_ref, back_in_ref)
        out_ref[rows] = out.astype(BF16)
        back_ref[rows] = back.astype(BF16)

    over_blocks(one_block)
    copies += send_out([(out_ref, out_any), (back_ref, back_any)], sems, NBLK + 10)
    grad_pieces(orders[0], me_down_ref, cot_ref, act_ref, down_all)
    copies += send_out(pieces_out(down_all, (down_keep, down_send)), sems, NBLK + 4)
    grad_pieces(orders[1], me_up_ref, in_ref, back_in_ref, up_all)
    wait_all(copies + send_out(pieces_out(up_all, (up_keep, up_send)), sems, NBLK + 6))


def mlp_second_kernel(
    orders, s_ref, c_ref, me_down_ref, me_up_ref, color_ref, in_any, out_one_any, back_one_any, cot_any,
    ua_ref, ub_ref, uc_ref, ud_ref, da_ref, db_ref, dc_ref, dd_ref,
    out_keep, out_send, both_ref, down_keep, down_send, up_keep, up_send,
    in_ref, out_one_ref, back_one_ref, cot_ref, up_ref, down_ref, out_ref, act_ref, back_in_ref, down_all, up_all, sems,
):
    color = color_ref[0]
    mine = pl.ds(pl.multiple_of(s_ref[0] * SEQ, SEQ), SEQ)
    loads = send_out(quarters_in(up_ref, color, (ua_ref, ub_ref, uc_ref, ud_ref)), sems)
    loads += send_out([(cot_any.at[mine], cot_ref)], sems, 4)
    loads += send_out([(in_any, in_ref)], sems, 16)
    late = [(out_one_any, out_one_ref, 17), (back_one_any, back_one_ref, 18)]
    loads += send_out(quarters_in(down_ref, color, (da_ref, db_ref, dc_ref, dd_ref)), sems, 5)
    for src, dst, i in late:
        pltpu.make_async_copy(src, dst, sems.at[i]).start()
    wait_all(loads)

    def one_block(rows):
        out, back = mlp_rows(rows, in_ref, cot_ref[rows], up_ref, down_ref, act_ref, back_in_ref)

        @pl.when(rows.start == 0)
        def _():
            for src, dst, i in late:
                pltpu.make_async_copy(src, dst, sems.at[i]).wait()

        out_ref[rows] = (out_one_ref[rows].astype(F32) + out).astype(BF16)
        back = (back_one_ref[rows].astype(F32) + back).astype(BF16)
        both_ref[0, rows] = back
        both_ref[1, rows] = back

    over_blocks(one_block)
    half = SEQ // 2
    parts = [pl.ds(pl.multiple_of(c * half, half), half) for c in (c_ref[0], 1 - c_ref[0])]
    copies = send_out([(out_ref.at[parts[0]], out_keep), (out_ref.at[parts[1]], out_send)], sems, 14)
    grad_pieces(orders[0], me_down_ref, cot_ref, act_ref, down_all)
    copies += send_out(pieces_out(down_all, (down_keep, down_send)), sems, 10)
    grad_pieces(orders[1], me_up_ref, in_ref, back_in_ref, up_all)
    wait_all(copies + send_out(pieces_out(up_all, (up_keep, up_send)), sems, 12))


def middle_kernel(
    order, s_ref, me_ref, hidden_any, cot_any, wo_one_any, wo_two_any, att_one_any, att_two_any, both_ref, gain_ref,
    grad_any, da_one_ref, da_two_ref, go_one_any, go_two_any,
    hidden_ref, cot_ref, wo_one_ref, wo_two_ref, att_one_ref, att_two_ref, grad_ref, low_ref, go_one, go_two, sems,
):
    at = [pl.ds(pl.multiple_of(s_ref[0] * SEQ + i * BLK, BLK), BLK) for i in range(NBLK)]
    loads = []
    for i in range(NBLK):
        rows = block(i)
        pairs = [
            (hidden_any.at[rows], hidden_ref.at[rows]),
            (cot_any.at[at[i]], cot_ref.at[rows]),
        ]
        loads.append(send_out(pairs, sems, 3 * i))
        if i == 0:
            loads_wo = send_out([(wo_one_any, wo_one_ref), (wo_two_any, wo_two_ref)], sems, 3 * NBLK)
    loads_att = send_out([(att_one_any, att_one_ref), (att_two_any, att_two_ref)], sems, 3 * NBLK + 2)
    copies = []
    for i in range(NBLK):
        rows = block(i)
        wait_all(loads[i])
        unit, inverse = normed(hidden_ref[rows].astype(F32))
        grad = both_ref[0, rows].astype(F32) + both_ref[1, rows].astype(F32)
        hidden_grad = cot_ref[rows].astype(F32) + norm_back(grad, unit, inverse, gain_ref[1:2])
        grad_ref[rows] = hidden_grad.astype(BF16)
        copies += send_out([(grad_ref.at[rows], grad_any.at[rows])], sems, 3 * NBLK + 4 + i)
        low = hidden_grad.astype(BF16)
        low_ref[rows] = low
        if i == 0:
            wait_all(loads_wo)
        da_one_ref[rows] = mm(low, wo_one_ref[...], NT).astype(BF16)
        da_two_ref[rows] = mm(low, wo_two_ref[...], NT).astype(BF16)
    wait_all(loads_att)
    put_pieces(go_one, me_ref[0], mm(low_ref[...], att_one_ref[...], TN), order)
    put_pieces(go_two, me_ref[0], mm(low_ref[...], att_two_ref[...], TN), order)
    wait_all(copies + send_out([(go_one, go_one_any), (go_two, go_two_any)], sems, 4 * NBLK + 4))


def attend_back(
    add_first, order, me_ref, q_ref, k_ref, v_ref, att_ref, da_ref, lse_ref, docs_ref, n_ref, w_ref, go_ref, *rest
):
    if add_first:
        before_ref, both_ref = rest[:2]
    else:
        (sum_ref,) = rest[:1]
    *grad_refs, dq_ref, dk_ref, dv_ref, ds_ref, all_ref, sems = rest[1 + add_first :]
    width = q_ref.shape[1]
    heads = width // HEAD
    eighth = jnp.asarray(0.125, BF16)
    prod = da_ref[...].astype(F32) * att_ref[...].astype(F32)
    pick_lane = lax.broadcasted_iota(jnp.int32, (8, width), 1)
    pick_row = lax.broadcasted_iota(jnp.int32, (8, width), 0)
    pick = jnp.where((pick_lane >= pick_row * HEAD) & (pick_lane < (pick_row + 1) * HEAD), 1.0, 0.0).astype(BF16)
    high = prod.astype(BF16)
    rest = prod - high.astype(F32)
    middle = rest.astype(BF16)
    inner = mm(pick, high, NT) + mm(pick, middle, NT) + mm(pick, (rest - middle.astype(F32)).astype(BF16), NT)
    for kb in range(NBLK):
        keys = slice(kb * BLK, (kb + 1) * BLK)
        start = kb * BLK
        count = SEQ - start
        column = jnp.transpose(jnp.broadcast_to(docs_ref[0, :, keys], (128, BLK)))
        docs_k = jnp.concatenate([column] * (count // 128), 1)
        at_row = lax.broadcasted_iota(jnp.int32, (BLK, count), 0)
        at_col = lax.broadcasted_iota(jnp.int32, (BLK, count), 1)
        allowed = (docs_k == docs_ref[0, :, start:]) & (at_row <= at_col)
        dk = jnp.zeros((BLK, width), F32)
        dv = jnp.zeros((BLK, width), F32)
        for h in range(heads):
            mask = head_mask(count, width, h)
            q_h = jnp.where(mask, q_ref[start:] * eighth, jnp.zeros((count, width), BF16))
            da_h = jnp.where(mask, da_ref[start:], jnp.zeros((count, width), BF16))
            s = mm(k_ref[keys], q_h, NT) - lse_ref[h : h + 1, start:]
            p = jnp.exp(jnp.where(allowed, s, NEG))
            dp = mm(v_ref[keys], da_h, NT)
            ds = (p * (dp - inner[h : h + 1, start:])).astype(BF16)
            ds_ref[h, keys, start:] = ds
            dv = dv + mm(p.astype(BF16), da_h, NN)
            dk = dk + mm(ds, q_h, NN)
        dk_ref[keys] = dk.astype(BF16)
        dv_ref[keys] = dv.astype(BF16)
    for qb in range(NBLK):
        rows = slice(qb * BLK, (qb + 1) * BLK)
        end = (qb + 1) * BLK
        dq = jnp.zeros((BLK, width), F32)
        for h in range(heads):
            k_h = jnp.where(head_mask(end, width, h), k_ref[:end] * eighth, jnp.zeros((end, width), BF16))
            dq = dq + mm(ds_ref[h, :end, rows], k_h, TN)
        dq_ref[rows] = dq.astype(BF16)
    for qb in range(NBLK):
        rows = slice(qb * BLK, (qb + 1) * BLK)
        total = mm(dq_ref[rows], w_ref[:width], NN)
        total = total + mm(dk_ref[rows], w_ref[width : 2 * width], NN)
        total = total + mm(dv_ref[rows], w_ref[2 * width :], NN)
        if add_first:
            total = (before_ref[rows] + total).astype(BF16)
            both_ref[0, rows] = total
            both_ref[1, rows] = total
        else:
            sum_ref[rows] = total
    n = n_ref[...]
    all_ref[:, :, 3 * width :] = go_ref[...]
    for i, ref in enumerate((dq_ref, dk_ref, dv_ref)):
        put_pieces(all_ref, me_ref[0], mm(n, ref[...], TN), order, 0, i * width)
    wait_all(send_out(pieces_out(all_ref, grad_refs), sems))


def last_kernel(
    s_ref, c_ref, x_any, grad_any, both_ref, gain_ref, out_any, low_ref, x_ref, grad_ref, out_ref, sems,
):
    at = [pl.ds(pl.multiple_of(s_ref[0] * SEQ + i * BLK, BLK), BLK) for i in range(NBLK)]
    loads = []
    for i in range(NBLK):
        rows = block(i)
        pairs = [
            (x_any.at[at[i]], x_ref.at[rows]),
            (grad_any.at[rows], grad_ref.at[rows]),
        ]
        loads.append(send_out(pairs, sems, 3 * i))
    stores = []
    for i in range(NBLK):
        rows = block(i)
        wait_all(loads[i])
        unit, inverse = normed(x_ref[rows].astype(F32))
        grad = both_ref[0, rows].astype(F32) + both_ref[1, rows].astype(F32)
        out = grad_ref[rows].astype(F32) + norm_back(grad, unit, inverse, gain_ref[0:1])
        out_ref[rows] = out
        stores += send_out([(out_ref.at[rows], out_any.at[at[i]])], sems, 3 * NBLK + i)
    half = low_ref.shape[0]
    low_ref[...] = out_ref[pl.ds(pl.multiple_of(c_ref[0] * half, half), half)].astype(BF16)
    wait_all(stores)


def block_kernel(c_ref, hidden_any, a_any, b_any, low_ref, hidden_ref, a_ref, b_ref, sems):
    half = SEQ // 2
    mine = pl.multiple_of(c_ref[0] * half, half)
    loads = []
    for i in range(half // BLK):
        rows = block(i)
        pairs = [(hidden_any.at[pl.ds(mine + i * BLK, BLK)], hidden_ref.at[rows])]
        pairs += [(a_any.at[rows], a_ref.at[rows]), (b_any.at[rows], b_ref.at[rows])]
        loads.append(send_out(pairs, sems, 3 * i))
    for i in range(half // BLK):
        rows = block(i)
        wait_all(loads[i])
        low_ref[rows] = (hidden_ref[rows].astype(F32) + (a_ref[rows].astype(F32) + b_ref[rows].astype(F32))).astype(BF16)


def fill_kernel(s_ref, both_ref, before_ref, out_ref):
    out_ref[...] = both_ref[pl.program_id(0)].astype(out_ref.dtype)


def place_kernel(s_ref, both_ref, out_ref):
    half = out_ref.shape[0]
    step = pl.program_id(0)
    other = jnp.where(step // 2 == s_ref[0], 0, half)
    out_ref[...] = both_ref[step % 2, pl.ds(pl.multiple_of(other, half), half)]


def add_kernel(plan, *refs):
    outs = refs[len(refs) - len(plan) :]
    for out, segments in zip(outs, plan):
        for place, count, lane, width, terms in segments:
            for j in range(count):
                total = None
                for index, first, start in terms:
                    term = refs[index][first + j, :, start : start + width].astype(F32)
                    total = term if total is None else total + term
                out[place + j, :, lane : lane + width] = total.astype(out.dtype)


VREF = pl.BlockSpec(memory_space=pltpu.VMEM)
SREF = pl.BlockSpec(memory_space=pltpu.SMEM)
ANYREF = pl.BlockSpec(memory_space=pl.ANY)


def vm(shape, dtype):
    return pltpu.VMEM(shape, dtype)


def far(shape, dtype):
    return pltpu.HBM(shape, dtype)


def sds(shape, dtype):
    return jax.ShapeDtypeStruct(shape, dtype)


def fast(v):
    return pltpu.with_memory_space_constraint(v, pltpu.VMEM)


class Free:
    def __init__(self, value):
        self.value = value


class Own(Free):
    pass


class Window(Free):
    pass


class Far(Own):
    pass


def call(
    kernel, scalars, args, outs, name, flops, scratch=(), in_specs=None, out_specs=None, grid=None, aliases=None, mib=14
):
    params = pltpu.CompilerParams(vmem_limit_bytes=mib * 1024 * 1024)
    cost = pl.CostEstimate(flops=int(flops), bytes_accessed=0, transcendentals=0)
    if grid is None:
        specs = [ANYREF if isinstance(a, Own) else VREF for a in args]
        args = [placed(a) for a in args]
        out_specs = [
            ANYREF if isinstance(o, Own) or getattr(o, "memory_space", None) == pltpu.HBM else VREF for o in outs
        ]
        outs = [o.value if isinstance(o, Free) else o for o in outs]
        return pl.pallas_call(
            kernel,
            out_shape=outs,
            in_specs=[SREF] * len(scalars) + specs,
            out_specs=out_specs,
            scratch_shapes=list(scratch),
            compiler_params=params,
            cost_estimate=cost,
            name=name,
        )(*scalars, *args)
    return pl.pallas_call(
        kernel,
        out_shape=outs,
        grid_spec=pltpu.PrefetchScalarGridSpec(
            num_scalar_prefetch=len(scalars),
            grid=grid,
            in_specs=[VREF] * len(args) if in_specs is None else in_specs,
            out_specs=out_specs,
            scratch_shapes=list(scratch),
        ),
        input_output_aliases=aliases or {},
        compiler_params=params,
        cost_estimate=cost,
        name=name,
    )(*scalars, *args)


def placed(a):
    if isinstance(a, Far):
        return pltpu.with_memory_space_constraint(a.value, pltpu.HBM)
    return a.value if isinstance(a, Free) else fast(a)


def free(values):
    return [Free(v) for v in values]


def own(values):
    return [Own(v) for v in values]


def apart(values):
    return [Far(v) for v in values]


def sems(count):
    return pltpu.SemaphoreType.DMA((count,))


def after(values, *done):
    kept = lax.optimization_barrier((tuple(values), done))
    return kept[0]


def on_device(
    tokens, documents, attn_gain, qkv_weight, out_weight, mlp_gain, up_weight, down_weight, cotangent, *, n_dp, n_tensor
):
    d = tokens.shape[1]
    width = qkv_weight.shape[2]
    units = up_weight.shape[1]
    heads = width // HEAD
    piece = d // n_dp
    bits = n_dp.bit_length() - 1
    natural = list(range(bits))
    swapped = [1, 0] + natural[2:]
    t = lax.axis_index("tensor").astype(jnp.int32)
    me = lax.axis_index("dp").astype(jnp.int32)
    s, c = t // 2, t % 2
    color = (me ^ (me >> 1)) & 1
    s1, c1, color1 = s.reshape(1), c.reshape(1), color.reshape(1)
    me_nat, me_swap = mapped(me, natural).reshape(1), mapped(me, swapped).reshape(1)

    def over_x(v):
        return lax.ppermute(v, "tensor", [(i, i ^ 2) for i in range(n_tensor)])

    def over_core(v):
        return lax.ppermute(v, "tensor", [(i, i ^ 1) for i in range(n_tensor)])

    def swap_cores(both):
        groups = [[i, i ^ 1] for i in range(0, n_tensor, 2)]
        return lax.all_to_all(both, "tensor", split_axis=0, concat_axis=0, axis_index_groups=groups)

    def over_dp(v, bit):
        return lax.ppermute(v, "dp", [(i, i ^ (1 << bit)) for i in range(n_dp)])

    h, q = n_dp // 2, n_dp // 4

    def pick(weights, name):
        outs = [Window(far((w.shape[0] // 4, w.shape[1]), BF16)) for w in weights for _ in range(2)]
        got = call(
            pick_kernel, (color1,), [Far(w) for w in weights], outs, name, 0,
            [pltpu.SemaphoreType.DMA((len(outs),))],
        )
        return [got[2 * i : 2 * i + 2] for i in range(len(weights))]

    def spread(pair):
        return [*pair, over_dp(pair[0], 0), over_dp(pair[1], 1)]

    w_one = jnp.transpose(qkv_weight, (1, 2, 0)).reshape(3 * width, d)
    wo_one = out_weight
    w_mine, up_mine, down_mine = pick([w_one, up_weight, down_weight], "pick")
    w_halves = [over_x(v) for v in w_mine]
    wo_two = over_x(wo_one)

    docs = documents.astype(F32).reshape(tokens.shape[0] // SEQ, 1, SEQ)
    docs = lax.dynamic_slice_in_dim(docs, s, 1, 0)
    both_gains = jnp.stack([attn_gain, mlp_gain])
    head_far, head_in = far((SEQ, width), BF16), vm((SEQ, width), BF16)
    head_keep = pltpu.VMEM((SEQ, width), BF16)
    keep_low, keep_wide, keep_both = pltpu.VMEM((SEQ, d), BF16), pltpu.VMEM((SEQ, d), F32), pltpu.VMEM((2, SEQ, d), BF16)
    both_open, half_far = vm((2, SEQ, d), BF16), far((SEQ // 2, d), BF16)
    rows_low, rows_wide, rows_open = vm((SEQ, d), BF16), vm((SEQ, d), F32), sds((SEQ, d), BF16)
    lse_out = vm((8, SEQ), F32)
    low_open = sds((BLK, d), BF16)
    long_cost, some_cost = 10**12, 2 * 10**10

    n, att_near, n_far, q_one, k_one, v_one, att_one, lse_one = call(
        first_kernel, (s1,), (Far(tokens), both_gains, w_one, docs),
        [rows_low, head_in, far((SEQ, d), BF16), head_far, head_far, head_far, head_far, lse_out],
        "attend_own", 0,
        [keep_low, head_keep, head_keep, head_keep, sems(6)],
    )
    *up_mine, down_a_mine, down_b_mine = after((*up_mine, *down_mine), n)
    down_mine = [down_a_mine, down_b_mine]
    up_halves = [over_x(v) for v in up_mine]
    down_halves = [over_x(v) for v in down_mine]
    w_pieces = spread(after(w_halves, n))
    w_two, q_two, k_two, v_two, att_two, lse_two, attn_sum = call(
        second_kernel, (color1,), (n, *own(w_pieces), Own(wo_two), docs, att_near, wo_one),
        [far((3 * width, d), BF16)] + [head_far] * 4 + [lse_out, rows_low],
        "attend_other", long_cost,
        [pltpu.VMEM((3 * width, d), BF16), pltpu.VMEM((width, d), BF16)] + [head_keep] * 4
        + [sems(14)], mib=15,
    )
    attn_sum, *up_halves = after((attn_sum, *up_halves), attn_sum)
    attn_recv = over_core(attn_sum)
    up_pieces = spread(up_halves)

    grad_out = far((h, piece, units), BF16)
    keep_up, keep_down = pltpu.VMEM((d, units), BF16), pltpu.VMEM((units, d), BF16)
    keep = [pltpu.VMEM((SEQ, units), BF16), pltpu.VMEM((SEQ, units), BF16)]
    grad_all = [pltpu.VMEM((n_dp, piece, units), BF16)] * 2
    orders = (swapped, natural)
    hidden, mlp_in, out_one, back_one, down_a, down_as, up_a, up_as = call(
        functools.partial(mlp_first_kernel, orders), (s1, me_swap, me_nat),
        (*apart((tokens, cotangent, up_weight, down_weight)), attn_sum, attn_recv, both_gains),
        [far((SEQ, d), BF16)] * 4 + [grad_out] * 4, "mlp_own", 0,
        [keep_low, keep_low, keep_up, keep_down] + [keep_low] * 4 + keep + grad_all + [sems(NBLK + 12)], mib=27,
    )
    down_pieces = spread(after(down_halves, mlp_in))
    up_ra = over_dp(up_as, 0)
    down_ra = over_dp(down_as, 1)
    mlp_keep, mlp_send, back_both, down_b, down_bs, up_b, up_bs = call(
        functools.partial(mlp_second_kernel, orders), (s1, c1, me_swap, me_nat, color1),
        (*apart((mlp_in, out_one, back_one, cotangent)), *own(up_pieces), *own(down_pieces)),
        [half_far, half_far, both_open] + [grad_out] * 4, "mlp_other", some_cost,
        [keep_low] * 4 + [keep_up, keep_down, keep_low] + keep + grad_all + [sems(19)], mib=24,
    )
    mlp_recv = over_core(mlp_send)
    back_both = swap_cores(back_both)
    up_rb = over_dp(up_bs, 0)
    down_rb = over_dp(down_bs, 1)

    half_keep = pltpu.VMEM((SEQ // 2, d), BF16)
    (block_low,) = call(
        block_kernel, (c1,), apart((hidden, after((mlp_keep,), back_both)[0], mlp_recv)), [sds((SEQ // 2, d), BF16)],
        "block_out", 0, [half_keep, half_keep, half_keep, sems(3 * NBLK)],
    )
    block_one = over_x(block_low)
    (back_both,) = after((back_both,), block_low)
    go_out = far((n_dp, piece, width), BF16)
    go_keep = pltpu.VMEM((n_dp, piece, width), BF16)
    hidden_grad, da_one, da_two, go_one, go_two = call(
        functools.partial(middle_kernel, natural), (s1, me_nat),
        (*apart((hidden, cotangent, wo_one, wo_two, att_one, att_two)), back_both, both_gains),
        [far((SEQ, d), BF16), head_in, head_in, go_out, go_out], "middle", some_cost,
        [keep_low, keep_low] + [pltpu.VMEM((width, d), BF16)] * 2
        + [head_keep, head_keep, keep_low, keep_low, go_keep, go_keep, sems(4 * NBLK + 6)], mib=12,
    )

    wide = 4 * width
    qkv_out = [far((h, piece, wide), BF16)] * 2
    back_scratch = [head_keep] * 3 + [pltpu.VMEM((heads, SEQ, SEQ), BF16), pltpu.VMEM((n_dp, piece, wide), BF16)]
    back_scratch += [sems(2)]
    in_one, g_b, g_bs = call(
        functools.partial(attend_back, False, natural), (me_nat,),
        (q_two, k_two, v_two, att_two, da_two, lse_two, docs, n_far, w_two, go_two), [rows_wide, *qkv_out],
        "attend_back_other", 0, back_scratch, mib=14,
    )
    g_rb = over_dp(g_bs, 0)

    def adds(name, results, leave=False):
        args, plan, outs = [], [], []

        def place(array):
            for i, known in enumerate(args):
                if known is array:
                    return i
            args.append(array)
            return len(args) - 1

        for dtype, pieces, rows, lanes, segments in results:
            plan.append([(*seg[:4], [(place(v), first, lane) for v, first, lane in seg[4]]) for seg in segments])
            shape = (pieces, rows, lanes)
            outs.append(Window(far(shape, dtype)) if leave and dtype == BF16 else sds(shape, dtype))
        return call(functools.partial(add_kernel, plan), (), free(args), outs, name, 0)

    def plain(dtype, count, *terms):
        rows, lanes = terms[0][0].shape[1:]
        return (dtype, count, rows, lanes, [(0, count, 0, lanes, [(v, first, 0) for v, first in terms])])

    def split(count, *arrays):
        return [plain(F32, count, *[(v, 0) for v in arrays]), plain(BF16, count, *[(v, count) for v in arrays])]

    def side_by_side(dtype, count, first, *groups):
        lane, segments = 0, []
        for arrays in groups:
            lanes = arrays[0].shape[2]
            segments.append((0, count, lane, lanes, [(v, first, 0) for v in arrays]))
            lane += lanes
        return (dtype, count, piece, lane, segments)

    def fill(start, one):
        both = swap_cores(jnp.stack([one, one]))
        (out,) = call(
            fill_kernel, (s1,), (both, start), [sds(start.shape, start.dtype)], "fill", 0,
            in_specs=[VREF, ANYREF],
            out_specs=[pl.BlockSpec((SEQ // 2, d), lambda i, s_ref, *_: ((1 - s_ref[0]) * 2 + i, 0))],
            grid=(2,), aliases={2: 0},
        )
        return out

    up_ra, up_rb, down_ra, down_rb = after((up_ra, up_rb, down_ra, down_rb), in_one)
    up_s2, down_s2 = adds(
        "reduce_mlp_one", [plain(BF16, h, (up_b, 0), (up_rb, 0)), plain(BF16, h, (down_b, 0), (down_rb, 0))]
    )
    up_r2, down_r2 = over_x(up_s2), over_x(down_s2)
    (in_one,) = after((in_one,), up_s2)
    in_both, g_a, g_as = call(
        functools.partial(attend_back, True, natural), (me_nat,),
        (q_one, k_one, v_one, att_one, da_one, lse_one, docs, n_far, w_one, go_one, in_one), [both_open] + qkv_out,
        "attend_back_own", 0, back_scratch, mib=14,
    )
    g_ra = over_dp(g_as, 0)
    g_rb, block_one = after((g_rb, block_one), g_a)
    g_b2, g_bs2 = adds("reduce_other_one", split(q, g_b, g_rb))
    g_rb2 = over_dp(g_bs2, 1)
    (in_both,) = after((in_both,), g_bs2)
    in_both = swap_cores(in_both)

    input_start, input_low = call(
        last_kernel, (s1, c1), (Far(tokens), Far(hidden_grad), in_both, both_gains),
        [far(tokens.shape, F32), sds((SEQ // 2, d), BF16)], "norm_back", 0,
        [keep_low, keep_low, keep_wide, sems(4 * NBLK)], mib=14,
    )
    up_r2, down_r2, g_rb2 = after((up_r2, down_r2, g_rb2), input_low)
    up_3, up_s3, down_3, down_s3, g_bx = adds(
        "reduce_mlp_two", split(q, up_a, up_ra, up_r2) + split(q, down_a, down_ra, down_r2) + [plain(BF16, q, (g_b2, 0), (g_rb2, 0))],
        leave=True,
    )
    up_r3, down_r3 = over_dp(up_s3, 1), over_dp(down_s3, 0)
    g_rx = over_x(g_bx)
    (input_low,) = after((input_low,), g_bx)
    input_one = over_x(input_low)
    (g_ra,) = after((g_ra,), g_bx)
    g_a2, g_as2 = adds("reduce_own_one", split(q, g_a, g_ra))
    g_ra2 = over_dp(g_as2, 1)
    last = q // 2
    up_r3, down_r3 = after((up_r3, down_r3), g_as2)
    mlp_4, mlp_s4 = adds(
        "reduce_mlp_three", [
            side_by_side(dtype, last, start, (up_3, up_r3), (down_3, down_r3)) for dtype, start in ((F32, 0), (BF16, last))
        ]
    )
    mlp_r4 = over_dp(mlp_s4, natural[2])
    block_both = jnp.concatenate(after((block_low, block_one), mlp_s4))
    block_both = swap_cores(jnp.stack([block_both, block_both]))
    (block_out,) = call(
        place_kernel, (s1,), (block_both,), [sds(tokens.shape, BF16)], "place", 0,
        in_specs=[VREF], out_specs=[pl.BlockSpec((SEQ // 2, d), lambda i, *_: (i, 0))], grid=(4,),
    )
    g_ra2, g_rx = after((g_ra2, g_rx), block_out)
    g_4, g_s4 = adds("reduce_own_two", split(last, g_a2, g_ra2, g_rx))
    g_r4 = over_dp(g_s4, natural[2])
    input_grad, input_one = after((input_start, input_one), g_s4)
    input_grad = fill(input_grad, input_one)
    mlp_r4, g_r4 = after((mlp_r4, g_r4), input_grad)
    mlp_5 = mlp_4 + mlp_r4.astype(F32)

    def other_steps(total):
        for bit in natural[3:]:
            count = total.shape[0] // 2
            got = over_dp(total[count:].astype(BF16), bit)
            total = total[:count] + got.astype(F32)
        return total[0]

    mlp_part, g_part = other_steps(mlp_5), other_steps(g_4 + g_r4.astype(F32))
    up_part, down_part = mlp_part[:, :units], mlp_part[:, units:]
    qkv_flat, out_part = g_part[:, : 3 * width], g_part[:, 3 * width :]
    start = me * piece
    w_rows = lax.dynamic_slice_in_dim(qkv_weight, start, piece, 0).reshape(piece, 3 * width).astype(F32)
    up_rows = lax.dynamic_slice_in_dim(up_weight, start, piece, 0).astype(F32)
    gains = jnp.stack([jnp.sum(w_rows * qkv_flat, 1), jnp.sum(up_rows * up_part, 1)])
    others = [lax.ppermute(gains, "tensor", [(i, i ^ m) for i in range(n_tensor)]) for m in (1, 2, 3)]
    gains = (gains + others[0]) + (others[1] + others[2])
    gains = gains / lax.dynamic_slice_in_dim(jnp.stack([attn_gain, mlp_gain]), start, piece, 1)
    qkv_part = qkv_flat.reshape(piece, 3, width)
    return (block_out, input_grad, gains[0], qkv_part, out_part.T, gains[1], up_part, down_part.T)


def solution(mesh):
    in_specs = (
        P("dp", None),
        P("dp"),
        P(),
        P(None, None, "tensor"),
        P("tensor", None),
        P(),
        P(None, "tensor"),
        P("tensor", None),
        P("dp", None),
    )
    out_specs = (
        P("dp", None),
        P("dp", None),
        P("dp"),
        P("dp", None, "tensor"),
        P("tensor", "dp"),
        P("dp"),
        P("dp", "tensor"),
        P("tensor", "dp"),
    )
    body = functools.partial(on_device, n_dp=mesh.shape["dp"], n_tensor=mesh.shape["tensor"])
    return jax.shard_map(body, mesh=mesh, in_specs=in_specs, out_specs=out_specs, check_vma=False)
```

```python
import functools
import math

import jax
import jax.numpy as jnp
from jax import lax
from jax.experimental import pallas as pl
from jax.experimental.pallas import tpu as pltpu
from jax.sharding import PartitionSpec as P

HEAD = 64
SEQ = 1024
BLK = 256
NBLK = SEQ // BLK
EPS = 1e-05
VMEM_BYTES = 14 * 1024 * 1024
F32 = jnp.float32
BF16 = jnp.bfloat16
C0 = math.sqrt(2.0 / math.pi)
C1 = 0.044715
NEG = -1e30

NN = (((1,), (0,)), ((), ()))
NT = (((1,), (1,)), ((), ()))
TN = (((0,), (0,)), ((), ()))


def mm(a, b, dims):
    return lax.dot_general(a, b, dims, preferred_element_type=F32)


def normed(rows):
    centered = rows - jnp.mean(rows, -1, keepdims=True)
    inverse = lax.rsqrt(jnp.mean(centered * centered, -1, keepdims=True) + EPS)
    return centered * inverse, inverse


def norm_back(grad_rows, unit, inverse, gain):
    scaled = grad_rows * gain
    first = jnp.mean(scaled, -1, keepdims=True)
    second = jnp.mean(scaled * unit, -1, keepdims=True)
    return inverse * (scaled - first - unit * second)


def head_mask(rows, width, h):
    lane = lax.broadcasted_iota(jnp.int32, (rows, width), 1)
    return (lane >= h * HEAD) & (lane < (h + 1) * HEAD)


def mapped(index, order):
    bits = len(order)
    return sum(((index >> b) & 1) << (bits - 1 - i) for i, b in enumerate(order))


def put_pieces(all_ref, me, grad, order, base=0, lane=0):
    rows = all_ref.shape[1]
    width = grad.shape[1]
    for p in range(grad.shape[0] // rows):
        place = mapped(p + base // rows, order) ^ me
        all_ref[place, :, lane : lane + width] = grad[p * rows : (p + 1) * rows].astype(BF16)


def block(i):
    return slice(i * BLK, (i + 1) * BLK)


def send_out(pairs, sems, base=0):
    copies = [pltpu.make_async_copy(src, dst, sems.at[base + i]) for i, (src, dst) in enumerate(pairs)]
    for one in copies:
        one.start()
    return copies


def wait_all(copies):
    for one in copies:
        one.wait()


def pieces_out(all_ref, refs):
    count = refs[0].shape[0]
    return [(all_ref.at[i * count : (i + 1) * count], ref) for i, ref in enumerate(refs)]


def quarters_in(whole_ref, color, pieces):
    rows = pieces[0].shape[0]
    at = [2 * color, 2 * color + 1, 2 * (1 - color), 2 * (1 - color) + 1]
    return [(ref, whole_ref.at[pl.ds(pl.multiple_of(i * rows, 16), rows)]) for i, ref in zip(at, pieces)]


def forward_scores(q_ref, k_ref, qb, h):
    width = q_ref.shape[1]
    rows = slice(qb * BLK, (qb + 1) * BLK)
    queries = q_ref[rows] * jnp.asarray(0.125, BF16)
    q_h = jnp.where(head_mask(BLK, width, h), queries, jnp.zeros_like(queries))
    return mm(q_h, k_ref[: (qb + 1) * BLK], NT)


def forward_allowed(docs_ref, qb):
    base, end = qb * BLK, (qb + 1) * BLK
    column = jnp.transpose(jnp.broadcast_to(docs_ref[0, :, base:end], (128, BLK)))
    docs_q = jnp.concatenate([column] * (end // 128), 1)
    at_row = lax.broadcasted_iota(jnp.int32, (BLK, end), 0) + base
    at_col = lax.broadcasted_iota(jnp.int32, (BLK, end), 1)
    return (docs_q == docs_ref[0, :, :end]) & (at_col <= at_row)


def forward_attention(q_ref, k_ref, v_ref, docs_ref, lse_ref, att_ref, ahead=2):
    width = q_ref.shape[1]
    heads = width // HEAD
    items = [(qb, h) for qb in range(NBLK) for h in range(heads)]
    pending = [forward_scores(q_ref, k_ref, *items[i]) for i in range(ahead)]
    for i, (qb, h) in enumerate(items):
        rows = slice(qb * BLK, (qb + 1) * BLK)
        if i + ahead < len(items):
            pending.append(forward_scores(q_ref, k_ref, *items[i + ahead]))
        if h == 0:
            allowed = forward_allowed(docs_ref, qb)
            total = jnp.zeros((BLK, width), F32)
        s = jnp.where(allowed, pending.pop(0), NEG)
        row_max = jnp.max(s, -1, keepdims=True)
        e = jnp.exp(s - row_max)
        row_sum = jnp.sum(e, -1, keepdims=True)
        out = mm(e.astype(BF16), v_ref[: (qb + 1) * BLK], NN)
        total = jnp.where(head_mask(BLK, width, h), out / row_sum, total)
        lse = row_max + jnp.log(row_sum)
        lse_ref[h : h + 1, rows] = jnp.transpose(jnp.broadcast_to(lse, (BLK, 128)))[:1]
        if h == heads - 1:
            att_ref[rows] = total.astype(BF16)


def over_blocks(body):
    rows = 2 * BLK

    def step(i, carry):
        body(pl.ds(pl.multiple_of(i * rows, rows), rows))
        return carry

    lax.fori_loop(0, SEQ // rows, step, 0)


def project(n_ref, w_ref, refs):
    width = refs[0].shape[1]
    for i, ref in enumerate(refs):
        ref[...] = mm(n_ref[...], w_ref[i * width : (i + 1) * width], NT).astype(BF16)


def pick_kernel(color_ref, *refs):
    count = (len(refs) - 1) // 3
    sems = refs[-1]
    pairs = []
    for i in range(count):
        src = refs[i]
        rows = src.shape[0] // 4
        for j in range(2):
            at = pl.ds(pl.multiple_of((2 * color_ref[0] + j) * rows, 16), rows)
            pairs.append((src.at[at], refs[count + 2 * i + j]))
    wait_all(send_out(pairs, sems))


def first_kernel(
    s_ref, x_ref, gain_ref, w_ref, docs_ref,
    n_ref, att_ref, n_out, q_out, k_out, v_out, att_out, lse_ref, x_vmem, q_ref, k_ref, v_ref, sems,
):
    mine = pl.ds(pl.multiple_of(s_ref[0] * SEQ, SEQ), SEQ)
    wait_all(send_out([(x_ref.at[mine], x_vmem)], sems, 5))
    for i in range(NBLK):
        unit, _ = normed(x_vmem[block(i)].astype(F32))
        n_ref[block(i)] = (unit * gain_ref[0:1]).astype(BF16)
    project(n_ref, w_ref, (q_ref, k_ref, v_ref))
    copies = send_out([(n_ref, n_out), (q_ref, q_out), (k_ref, k_out), (v_ref, v_out)], sems)
    forward_attention(q_ref, k_ref, v_ref, docs_ref, lse_ref, att_ref)
    wait_all(copies + send_out([(att_ref, att_out)], sems, 4))


def second_kernel(
    color_ref, n_ref, wa_ref, wb_ref, wc_ref, wd_ref, wo_any, docs_ref, att_one_ref, wo_one_ref,
    w_out, q_out, k_out, v_out, att_out, lse_ref, sum_ref,
    w_ref, wo_ref, q_ref, k_ref, v_ref, att_ref, sems,
):
    color = color_ref[0]
    loads = send_out(quarters_in(w_ref, color, (wa_ref, wb_ref, wc_ref, wd_ref)), sems, 6)
    loads_wo = send_out([(wo_any, wo_ref)], sems, 10)
    wait_all(loads)
    project(n_ref, w_ref, (q_ref, k_ref, v_ref))
    wait_all(loads_wo)
    copies = send_out([(w_ref, w_out), (q_ref, q_out), (k_ref, k_out), (v_ref, v_out)], sems)
    forward_attention(q_ref, k_ref, v_ref, docs_ref, lse_ref, att_ref)
    copies += send_out([(att_ref, att_out)], sems, 5)
    for i in range(NBLK):
        total = mm(att_one_ref[block(i)], wo_one_ref[...], NN) + mm(att_ref[block(i)], wo_ref[...], NN)
        sum_ref[block(i)] = total.astype(BF16)
    wait_all(copies)


def gelu_pair(u):
    square = u * u
    th = jnp.tanh(u * (C0 + (C0 * C1) * square))
    half = 0.5 * u
    act = half + half * th
    slope = 0.5 + 0.5 * th + half * (1.0 - th * th) * (C0 + (3.0 * C0 * C1) * square)
    return act, slope


def mlp_rows(rows, in_ref, cot, up_ref, down_ref, act_ref, back_in_ref, ready=None):
    act, slope = gelu_pair(mm(in_ref[rows], up_ref[...], NN))
    if ready is not None:
        ready()
    act = act.astype(BF16)
    act_ref[rows] = act
    back_in = (mm(cot, down_ref[...], NT) * slope).astype(BF16)
    back_in_ref[rows] = back_in
    return mm(act, down_ref[...], NN), mm(back_in, up_ref[...], NT)


def grad_pieces(order, me_ref, left_ref, right_ref, all_ref):
    wide = left_ref.shape[1] // 2

    def one_half(j, carry):
        lanes = pl.ds(pl.multiple_of(j * wide, 128), wide)
        put_pieces(all_ref, me_ref[0], mm(left_ref[:, lanes], right_ref[...], TN), order, j * wide)
        return carry

    lax.fori_loop(0, 2, one_half, 0)


def mlp_first_kernel(
    orders, s_ref, me_down_ref, me_up_ref, x_any, cot_any, up_any, down_any, a_ref, b_ref, gain_ref,
    hidden_any, in_any, out_any, back_any, down_keep, down_send, up_keep, up_send,
    x_ref, cot_ref, up_ref, down_ref, hidden_ref, in_ref, out_ref, back_ref, act_ref, back_in_ref, down_all, up_all,
    sems,
):
    loads = []
    for i in range(NBLK):
        at = pl.ds(pl.multiple_of(s_ref[0] * SEQ + i * BLK, BLK), BLK)
        loads.append(send_out([(x_any.at[at], x_ref.at[block(i)])], sems, i))
    mine = pl.ds(pl.multiple_of(s_ref[0] * SEQ, SEQ), SEQ)
    loads_more = send_out([(up_any, up_ref), (cot_any.at[mine], cot_ref), (down_any, down_ref)], sems, NBLK)
    for i in range(NBLK):
        wait_all(loads[i])
        rows = block(i)
        hidden = x_ref[rows].astype(F32) + (a_ref[rows].astype(F32) + b_ref[rows].astype(F32))
        hidden_ref[rows] = hidden.astype(BF16)
        unit, _ = normed(hidden)
        in_ref[rows] = (unit * gain_ref[1:2]).astype(BF16)
    copies = send_out([(hidden_ref, hidden_any), (in_ref, in_any)], sems, NBLK + 8)
    wait_all(loads_more)

    def one_block(rows):
        out, back = mlp_rows(rows, in_ref, cot_ref[rows], up_ref, down_ref, act_ref, back_in_ref)
        out_ref[rows] = out.astype(BF16)
        back_ref[rows] = back.astype(BF16)

    over_blocks(one_block)
    copies += send_out([(out_ref, out_any), (back_ref, back_any)], sems, NBLK + 10)
    grad_pieces(orders[0], me_down_ref, cot_ref, act_ref, down_all)
    copies += send_out(pieces_out(down_all, (down_keep, down_send)), sems, NBLK + 4)
    grad_pieces(orders[1], me_up_ref, in_ref, back_in_ref, up_all)
    wait_all(copies + send_out(pieces_out(up_all, (up_keep, up_send)), sems, NBLK + 6))


def mlp_second_kernel(
    orders, s_ref, c_ref, me_down_ref, me_up_ref, color_ref, in_any, out_one_any, back_one_any, cot_any,
    ua_ref, ub_ref, uc_ref, ud_ref, da_ref, db_ref, dc_ref, dd_ref,
    out_keep, out_send, both_ref, down_keep, down_send, up_keep, up_send,
    in_ref, out_one_ref, back_one_ref, cot_ref, up_ref, down_ref, out_ref, act_ref, back_in_ref, down_all, up_all, sems,
):
    color = color_ref[0]
    mine = pl.ds(pl.multiple_of(s_ref[0] * SEQ, SEQ), SEQ)
    loads = send_out(quarters_in(up_ref, color, (ua_ref, ub_ref, uc_ref, ud_ref)), sems)
    loads += send_out([(cot_any.at[mine], cot_ref)], sems, 4)
    loads += send_out([(in_any, in_ref)], sems, 16)
    late = [(out_one_any, out_one_ref, 17), (back_one_any, back_one_ref, 18)]
    loads_down = send_out(quarters_in(down_ref, color, (da_ref, db_ref, dc_ref, dd_ref)), sems, 5)
    for src, dst, i in late:
        pltpu.make_async_copy(src, dst, sems.at[i]).start()
    wait_all(loads)

    def one_block(rows):
        def down_ready():
            @pl.when(rows.start == 0)
            def _():
                wait_all(loads_down)

        out, back = mlp_rows(rows, in_ref, cot_ref[rows], up_ref, down_ref, act_ref, back_in_ref, down_ready)

        @pl.when(rows.start == 0)
        def _():
            for src, dst, i in late:
                pltpu.make_async_copy(src, dst, sems.at[i]).wait()

        out_ref[rows] = (out_one_ref[rows].astype(F32) + out).astype(BF16)
        back = (back_one_ref[rows].astype(F32) + back).astype(BF16)
        both_ref[0, rows] = back
        both_ref[1, rows] = back

    over_blocks(one_block)
    half = SEQ // 2
    parts = [pl.ds(pl.multiple_of(c * half, half), half) for c in (c_ref[0], 1 - c_ref[0])]
    copies = send_out([(out_ref.at[parts[0]], out_keep), (out_ref.at[parts[1]], out_send)], sems, 14)
    grad_pieces(orders[0], me_down_ref, cot_ref, act_ref, down_all)
    copies += send_out(pieces_out(down_all, (down_keep, down_send)), sems, 10)
    grad_pieces(orders[1], me_up_ref, in_ref, back_in_ref, up_all)
    wait_all(copies + send_out(pieces_out(up_all, (up_keep, up_send)), sems, 12))


def middle_kernel(
    order, s_ref, me_ref, hidden_any, cot_any, wo_one_any, wo_two_any, att_one_any, att_two_any, both_ref, gain_ref,
    grad_any, da_one_ref, da_two_ref, go_one_any, go_two_any,
    hidden_ref, cot_ref, wo_one_ref, wo_two_ref, att_one_ref, att_two_ref, grad_ref, low_ref, go_one, go_two, sems,
):
    at = [pl.ds(pl.multiple_of(s_ref[0] * SEQ + i * BLK, BLK), BLK) for i in range(NBLK)]
    loads = []
    for i in range(NBLK):
        rows = block(i)
        pairs = [
            (hidden_any.at[rows], hidden_ref.at[rows]),
            (cot_any.at[at[i]], cot_ref.at[rows]),
        ]
        loads.append(send_out(pairs, sems, 3 * i))
        if i == 0:
            loads_wo = send_out([(wo_one_any, wo_one_ref), (wo_two_any, wo_two_ref)], sems, 3 * NBLK)
    loads_att = send_out([(att_one_any, att_one_ref), (att_two_any, att_two_ref)], sems, 3 * NBLK + 2)
    copies = []
    for i in range(NBLK):
        rows = block(i)
        wait_all(loads[i])
        unit, inverse = normed(hidden_ref[rows].astype(F32))
        grad = both_ref[0, rows].astype(F32) + both_ref[1, rows].astype(F32)
        hidden_grad = cot_ref[rows].astype(F32) + norm_back(grad, unit, inverse, gain_ref[1:2])
        grad_ref[rows] = hidden_grad.astype(BF16)
        copies += send_out([(grad_ref.at[rows], grad_any.at[rows])], sems, 3 * NBLK + 4 + i)
        low = hidden_grad.astype(BF16)
        low_ref[rows] = low
        if i == 0:
            wait_all(loads_wo)
        da_one_ref[rows] = mm(low, wo_one_ref[...], NT).astype(BF16)
        da_two_ref[rows] = mm(low, wo_two_ref[...], NT).astype(BF16)
    wait_all(loads_att)
    put_pieces(go_one, me_ref[0], mm(low_ref[...], att_one_ref[...], TN), order)
    put_pieces(go_two, me_ref[0], mm(low_ref[...], att_two_ref[...], TN), order)
    wait_all(copies + send_out([(go_one, go_one_any), (go_two, go_two_any)], sems, 4 * NBLK + 4))


def attend_back(
    add_first, order, me_ref, q_ref, k_ref, v_ref, att_ref, da_ref, lse_ref, docs_ref, n_ref, w_ref, go_ref, *rest
):
    if add_first:
        before_ref, both_ref = rest[:2]
    else:
        (sum_ref,) = rest[:1]
    *grad_refs, dq_ref, dk_ref, dv_ref, ds_ref, all_ref, sems = rest[1 + add_first :]
    width = q_ref.shape[1]
    heads = width // HEAD
    eighth = jnp.asarray(0.125, BF16)
    prod = da_ref[...].astype(F32) * att_ref[...].astype(F32)
    pick_lane = lax.broadcasted_iota(jnp.int32, (8, width), 1)
    pick_row = lax.broadcasted_iota(jnp.int32, (8, width), 0)
    pick = jnp.where((pick_lane >= pick_row * HEAD) & (pick_lane < (pick_row + 1) * HEAD), 1.0, 0.0).astype(BF16)
    high = prod.astype(BF16)
    rest = prod - high.astype(F32)
    middle = rest.astype(BF16)
    inner = mm(pick, high, NT) + mm(pick, middle, NT) + mm(pick, (rest - middle.astype(F32)).astype(BF16), NT)
    for kb in range(NBLK):
        keys = slice(kb * BLK, (kb + 1) * BLK)
        start = kb * BLK
        count = SEQ - start
        column = jnp.transpose(jnp.broadcast_to(docs_ref[0, :, keys], (128, BLK)))
        docs_k = jnp.concatenate([column] * (count // 128), 1)
        at_row = lax.broadcasted_iota(jnp.int32, (BLK, count), 0)
        at_col = lax.broadcasted_iota(jnp.int32, (BLK, count), 1)
        allowed = (docs_k == docs_ref[0, :, start:]) & (at_row <= at_col)
        dk = jnp.zeros((BLK, width), F32)
        dv = jnp.zeros((BLK, width), F32)
        for h in range(heads):
            mask = head_mask(count, width, h)
            q_h = jnp.where(mask, q_ref[start:] * eighth, jnp.zeros((count, width), BF16))
            da_h = jnp.where(mask, da_ref[start:], jnp.zeros((count, width), BF16))
            s = mm(k_ref[keys], q_h, NT) - lse_ref[h : h + 1, start:]
            p = jnp.exp(jnp.where(allowed, s, NEG))
            dp = mm(v_ref[keys], da_h, NT)
            ds = (p * (dp - inner[h : h + 1, start:])).astype(BF16)
            ds_ref[h, keys, start:] = ds
            dv = dv + mm(p.astype(BF16), da_h, NN)
            dk = dk + mm(ds, q_h, NN)
        dk_ref[keys] = dk.astype(BF16)
        dv_ref[keys] = dv.astype(BF16)
    for qb in range(NBLK):
        rows = slice(qb * BLK, (qb + 1) * BLK)
        end = (qb + 1) * BLK
        dq = jnp.zeros((BLK, width), F32)
        for h in range(heads):
            k_h = jnp.where(head_mask(end, width, h), k_ref[:end] * eighth, jnp.zeros((end, width), BF16))
            dq = dq + mm(ds_ref[h, :end, rows], k_h, TN)
        dq_ref[rows] = dq.astype(BF16)
    for qb in range(NBLK):
        rows = slice(qb * BLK, (qb + 1) * BLK)
        total = mm(dq_ref[rows], w_ref[:width], NN)
        total = total + mm(dk_ref[rows], w_ref[width : 2 * width], NN)
        total = total + mm(dv_ref[rows], w_ref[2 * width :], NN)
        if add_first:
            total = (before_ref[rows] + total).astype(BF16)
            both_ref[0, rows] = total
            both_ref[1, rows] = total
        else:
            sum_ref[rows] = total
    n = n_ref[...]
    all_ref[:, :, 3 * width :] = go_ref[...]
    for i, ref in enumerate((dq_ref, dk_ref, dv_ref)):
        put_pieces(all_ref, me_ref[0], mm(n, ref[...], TN), order, 0, i * width)
    wait_all(send_out(pieces_out(all_ref, grad_refs), sems))


def last_kernel(
    s_ref, c_ref, x_any, grad_any, both_ref, gain_ref, out_any, low_ref, x_ref, grad_ref, out_ref, sems,
):
    at = [pl.ds(pl.multiple_of(s_ref[0] * SEQ + i * BLK, BLK), BLK) for i in range(NBLK)]
    loads = []
    for i in range(NBLK):
        rows = block(i)
        pairs = [
            (x_any.at[at[i]], x_ref.at[rows]),
            (grad_any.at[rows], grad_ref.at[rows]),
        ]
        loads.append(send_out(pairs, sems, 3 * i))
    stores = []
    for i in range(NBLK):
        rows = block(i)
        wait_all(loads[i])
        unit, inverse = normed(x_ref[rows].astype(F32))
        grad = both_ref[0, rows].astype(F32) + both_ref[1, rows].astype(F32)
        out = grad_ref[rows].astype(F32) + norm_back(grad, unit, inverse, gain_ref[0:1])
        out_ref[rows] = out
        stores += send_out([(out_ref.at[rows], out_any.at[at[i]])], sems, 3 * NBLK + i)
    half = low_ref.shape[0]
    low_ref[...] = out_ref[pl.ds(pl.multiple_of(c_ref[0] * half, half), half)].astype(BF16)
    wait_all(stores)


def block_kernel(c_ref, hidden_any, a_any, b_any, low_ref, hidden_ref, a_ref, b_ref, sems):
    half = SEQ // 2
    mine = pl.multiple_of(c_ref[0] * half, half)
    loads = []
    for i in range(half // BLK):
        rows = block(i)
        pairs = [(hidden_any.at[pl.ds(mine + i * BLK, BLK)], hidden_ref.at[rows])]
        pairs += [(a_any.at[rows], a_ref.at[rows]), (b_any.at[rows], b_ref.at[rows])]
        loads.append(send_out(pairs, sems, 3 * i))
    for i in range(half // BLK):
        rows = block(i)
        wait_all(loads[i])
        low_ref[rows] = (hidden_ref[rows].astype(F32) + (a_ref[rows].astype(F32) + b_ref[rows].astype(F32))).astype(BF16)


def fill_kernel(s_ref, both_ref, before_ref, out_ref):
    out_ref[...] = both_ref[pl.program_id(0)].astype(out_ref.dtype)


def place_kernel(s_ref, both_ref, out_ref):
    half = out_ref.shape[0]
    step = pl.program_id(0)
    other = jnp.where(step // 2 == s_ref[0], 0, half)
    out_ref[...] = both_ref[step % 2, pl.ds(pl.multiple_of(other, half), half)]


def add_kernel(plan, *refs):
    outs = refs[len(refs) - len(plan) :]
    for out, segments in zip(outs, plan):
        for place, count, lane, width, terms in segments:
            for j in range(count):
                total = None
                for index, first, start in terms:
                    term = refs[index][first + j, :, start : start + width].astype(F32)
                    total = term if total is None else total + term
                out[place + j, :, lane : lane + width] = total.astype(out.dtype)


VREF = pl.BlockSpec(memory_space=pltpu.VMEM)
SREF = pl.BlockSpec(memory_space=pltpu.SMEM)
ANYREF = pl.BlockSpec(memory_space=pl.ANY)


def vm(shape, dtype):
    return pltpu.VMEM(shape, dtype)


def far(shape, dtype):
    return pltpu.HBM(shape, dtype)


def sds(shape, dtype):
    return jax.ShapeDtypeStruct(shape, dtype)


def fast(v):
    return pltpu.with_memory_space_constraint(v, pltpu.VMEM)


class Free:
    def __init__(self, value):
        self.value = value


class Own(Free):
    pass


class Window(Free):
    pass


class Far(Own):
    pass


def call(
    kernel, scalars, args, outs, name, flops, scratch=(), in_specs=None, out_specs=None, grid=None, aliases=None, mib=14
):
    params = pltpu.CompilerParams(vmem_limit_bytes=mib * 1024 * 1024)
    cost = pl.CostEstimate(flops=int(flops), bytes_accessed=0, transcendentals=0)
    if grid is None:
        specs = [ANYREF if isinstance(a, Own) else VREF for a in args]
        args = [placed(a) for a in args]
        out_specs = [
            ANYREF if isinstance(o, Own) or getattr(o, "memory_space", None) == pltpu.HBM else VREF for o in outs
        ]
        outs = [o.value if isinstance(o, Free) else o for o in outs]
        return pl.pallas_call(
            kernel,
            out_shape=outs,
            in_specs=[SREF] * len(scalars) + specs,
            out_specs=out_specs,
            scratch_shapes=list(scratch),
            compiler_params=params,
            cost_estimate=cost,
            name=name,
        )(*scalars, *args)
    return pl.pallas_call(
        kernel,
        out_shape=outs,
        grid_spec=pltpu.PrefetchScalarGridSpec(
            num_scalar_prefetch=len(scalars),
            grid=grid,
            in_specs=[VREF] * len(args) if in_specs is None else in_specs,
            out_specs=out_specs,
            scratch_shapes=list(scratch),
        ),
        input_output_aliases=aliases or {},
        compiler_params=params,
        cost_estimate=cost,
        name=name,
    )(*scalars, *args)


def placed(a):
    if isinstance(a, Far):
        return pltpu.with_memory_space_constraint(a.value, pltpu.HBM)
    return a.value if isinstance(a, Free) else fast(a)


def free(values):
    return [Free(v) for v in values]


def own(values):
    return [Own(v) for v in values]


def apart(values):
    return [Far(v) for v in values]


def sems(count):
    return pltpu.SemaphoreType.DMA((count,))


def after(values, *done):
    kept = lax.optimization_barrier((tuple(values), done))
    return kept[0]


def on_device(
    tokens, documents, attn_gain, qkv_weight, out_weight, mlp_gain, up_weight, down_weight, cotangent, *, n_dp, n_tensor
):
    d = tokens.shape[1]
    width = qkv_weight.shape[2]
    units = up_weight.shape[1]
    heads = width // HEAD
    piece = d // n_dp
    bits = n_dp.bit_length() - 1
    natural = list(range(bits))
    swapped = [1, 0] + natural[2:]
    t = lax.axis_index("tensor").astype(jnp.int32)
    me = lax.axis_index("dp").astype(jnp.int32)
    s, c = t // 2, t % 2
    color = (me ^ (me >> 1)) & 1
    s1, c1, color1 = s.reshape(1), c.reshape(1), color.reshape(1)
    me_nat, me_swap = mapped(me, natural).reshape(1), mapped(me, swapped).reshape(1)

    def over_x(v):
        return lax.ppermute(v, "tensor", [(i, i ^ 2) for i in range(n_tensor)])

    def over_core(v):
        return lax.ppermute(v, "tensor", [(i, i ^ 1) for i in range(n_tensor)])

    def swap_cores(both):
        groups = [[i, i ^ 1] for i in range(0, n_tensor, 2)]
        return lax.all_to_all(both, "tensor", split_axis=0, concat_axis=0, axis_index_groups=groups)

    def over_dp(v, bit):
        return lax.ppermute(v, "dp", [(i, i ^ (1 << bit)) for i in range(n_dp)])

    h, q = n_dp // 2, n_dp // 4

    def pick(weights, name):
        outs = [Window(far((w.shape[0] // 4, w.shape[1]), BF16)) for w in weights for _ in range(2)]
        got = call(
            pick_kernel, (color1,), [Far(w) for w in weights], outs, name, 0,
            [pltpu.SemaphoreType.DMA((len(outs),))],
        )
        return [got[2 * i : 2 * i + 2] for i in range(len(weights))]

    def spread(pair):
        return [*pair, over_dp(pair[0], 0), over_dp(pair[1], 1)]

    w_one = jnp.transpose(qkv_weight, (1, 2, 0)).reshape(3 * width, d)
    wo_one = out_weight
    w_mine, up_mine, down_mine = pick([w_one, up_weight, down_weight], "pick")
    w_halves = [over_x(v) for v in w_mine]
    wo_two = over_x(wo_one)

    docs = documents.astype(F32).reshape(tokens.shape[0] // SEQ, 1, SEQ)
    docs = lax.dynamic_slice_in_dim(docs, s, 1, 0)
    both_gains = jnp.stack([attn_gain, mlp_gain])
    head_far, head_in = far((SEQ, width), BF16), vm((SEQ, width), BF16)
    head_keep = pltpu.VMEM((SEQ, width), BF16)
    keep_low, keep_wide, keep_both = pltpu.VMEM((SEQ, d), BF16), pltpu.VMEM((SEQ, d), F32), pltpu.VMEM((2, SEQ, d), BF16)
    both_open, half_far = vm((2, SEQ, d), BF16), far((SEQ // 2, d), BF16)
    rows_low, rows_wide, rows_open = vm((SEQ, d), BF16), vm((SEQ, d), F32), sds((SEQ, d), BF16)
    lse_out = vm((8, SEQ), F32)
    low_open = sds((BLK, d), BF16)
    long_cost, some_cost = 10**12, 2 * 10**10

    n, att_near, n_far, q_one, k_one, v_one, att_one, lse_one = call(
        first_kernel, (s1,), (Far(tokens), both_gains, w_one, docs),
        [rows_low, head_in, far((SEQ, d), BF16), head_far, head_far, head_far, head_far, lse_out],
        "attend_own", 0,
        [keep_low, head_keep, head_keep, head_keep, sems(6)],
    )
    *up_mine, down_a_mine, down_b_mine = after((*up_mine, *down_mine), n)
    down_mine = [down_a_mine, down_b_mine]
    up_halves = [over_x(v) for v in up_mine]
    down_halves = [over_x(v) for v in down_mine]
    w_pieces = spread(after(w_halves, n))
    w_two, q_two, k_two, v_two, att_two, lse_two, attn_sum = call(
        second_kernel, (color1,), (n, *own(w_pieces), Own(wo_two), docs, att_near, wo_one),
        [far((3 * width, d), BF16)] + [head_far] * 4 + [lse_out, rows_low],
        "attend_other", long_cost,
        [pltpu.VMEM((3 * width, d), BF16), pltpu.VMEM((width, d), BF16)] + [head_keep] * 4
        + [sems(14)], mib=15,
    )
    attn_sum, *up_halves = after((attn_sum, *up_halves), attn_sum)
    attn_recv = over_core(attn_sum)
    up_pieces = spread(up_halves)

    grad_out = far((h, piece, units), BF16)
    keep_up, keep_down = pltpu.VMEM((d, units), BF16), pltpu.VMEM((units, d), BF16)
    keep = [pltpu.VMEM((SEQ, units), BF16), pltpu.VMEM((SEQ, units), BF16)]
    grad_all = [pltpu.VMEM((n_dp, piece, units), BF16)] * 2
    orders = (swapped, natural)
    hidden, mlp_in, out_one, back_one, down_a, down_as, up_a, up_as = call(
        functools.partial(mlp_first_kernel, orders), (s1, me_swap, me_nat),
        (*apart((tokens, cotangent, up_weight, down_weight)), attn_sum, attn_recv, both_gains),
        [far((SEQ, d), BF16)] * 4 + [grad_out] * 4, "mlp_own", 0,
        [keep_low, keep_low, keep_up, keep_down] + [keep_low] * 4 + keep + grad_all + [sems(NBLK + 12)], mib=27,
    )
    down_pieces = spread(after(down_halves, mlp_in))
    up_ra = over_dp(up_as, 0)
    down_ra = over_dp(down_as, 1)
    mlp_keep, mlp_send, back_both, down_b, down_bs, up_b, up_bs = call(
        functools.partial(mlp_second_kernel, orders), (s1, c1, me_swap, me_nat, color1),
        (*apart((mlp_in, out_one, back_one, cotangent)), *own(up_pieces), *own(down_pieces)),
        [half_far, half_far, both_open] + [grad_out] * 4, "mlp_other", some_cost,
        [keep_low] * 4 + [keep_up, keep_down, keep_low] + keep + grad_all + [sems(19)], mib=24,
    )
    mlp_recv = over_core(mlp_send)
    back_both = swap_cores(back_both)
    up_rb = over_dp(up_bs, 0)
    down_rb = over_dp(down_bs, 1)

    half_keep = pltpu.VMEM((SEQ // 2, d), BF16)
    (block_low,) = call(
        block_kernel, (c1,), apart((hidden, after((mlp_keep,), back_both)[0], mlp_recv)), [sds((SEQ // 2, d), BF16)],
        "block_out", 0, [half_keep, half_keep, half_keep, sems(3 * NBLK)],
    )
    block_one = over_x(block_low)
    (back_both,) = after((back_both,), block_low)
    go_out = far((n_dp, piece, width), BF16)
    go_keep = pltpu.VMEM((n_dp, piece, width), BF16)
    hidden_grad, da_one, da_two, go_one, go_two = call(
        functools.partial(middle_kernel, natural), (s1, me_nat),
        (*apart((hidden, cotangent, wo_one, wo_two, att_one, att_two)), back_both, both_gains),
        [far((SEQ, d), BF16), head_in, head_in, go_out, go_out], "middle", some_cost,
        [keep_low, keep_low] + [pltpu.VMEM((width, d), BF16)] * 2
        + [head_keep, head_keep, keep_low, keep_low, go_keep, go_keep, sems(4 * NBLK + 6)], mib=12,
    )

    wide = 4 * width
    qkv_out = [far((h, piece, wide), BF16)] * 2
    back_scratch = [head_keep] * 3 + [pltpu.VMEM((heads, SEQ, SEQ), BF16), pltpu.VMEM((n_dp, piece, wide), BF16)]
    back_scratch += [sems(2)]
    in_one, g_b, g_bs = call(
        functools.partial(attend_back, False, natural), (me_nat,),
        (q_two, k_two, v_two, att_two, da_two, lse_two, docs, n_far, w_two, go_two), [rows_wide, *qkv_out],
        "attend_back_other", 0, back_scratch, mib=14,
    )
    g_rb = over_dp(g_bs, 0)

    def adds(name, results, leave=False):
        args, plan, outs = [], [], []

        def place(array):
            for i, known in enumerate(args):
                if known is array:
                    return i
            args.append(array)
            return len(args) - 1

        for dtype, pieces, rows, lanes, segments in results:
            plan.append([(*seg[:4], [(place(v), first, lane) for v, first, lane in seg[4]]) for seg in segments])
            shape = (pieces, rows, lanes)
            outs.append(Window(far(shape, dtype)) if leave and dtype == BF16 else sds(shape, dtype))
        return call(functools.partial(add_kernel, plan), (), free(args), outs, name, 0)

    def plain(dtype, count, *terms):
        rows, lanes = terms[0][0].shape[1:]
        return (dtype, count, rows, lanes, [(0, count, 0, lanes, [(v, first, 0) for v, first in terms])])

    def split(count, *arrays):
        return [plain(F32, count, *[(v, 0) for v in arrays]), plain(BF16, count, *[(v, count) for v in arrays])]

    def side_by_side(dtype, count, first, *groups):
        lane, segments = 0, []
        for arrays in groups:
            lanes = arrays[0].shape[2]
            segments.append((0, count, lane, lanes, [(v, first, 0) for v in arrays]))
            lane += lanes
        return (dtype, count, piece, lane, segments)

    def fill(start, one):
        both = swap_cores(jnp.stack([one, one]))
        (out,) = call(
            fill_kernel, (s1,), (both, start), [sds(start.shape, start.dtype)], "fill", 0,
            in_specs=[VREF, ANYREF],
            out_specs=[pl.BlockSpec((SEQ // 2, d), lambda i, s_ref, *_: ((1 - s_ref[0]) * 2 + i, 0))],
            grid=(2,), aliases={2: 0},
        )
        return out

    up_ra, up_rb, down_ra, down_rb = after((up_ra, up_rb, down_ra, down_rb), in_one)
    up_s2, down_s2 = adds(
        "reduce_mlp_one", [plain(BF16, h, (up_b, 0), (up_rb, 0)), plain(BF16, h, (down_b, 0), (down_rb, 0))]
    )
    up_r2, down_r2 = over_x(up_s2), over_x(down_s2)
    (in_one,) = after((in_one,), up_s2)
    in_both, g_a, g_as = call(
        functools.partial(attend_back, True, natural), (me_nat,),
        (q_one, k_one, v_one, att_one, da_one, lse_one, docs, n_far, w_one, go_one, in_one), [both_open] + qkv_out,
        "attend_back_own", 0, back_scratch, mib=14,
    )
    g_ra = over_dp(g_as, 0)
    g_rb, block_one = after((g_rb, block_one), g_a)
    g_b2, g_bs2 = adds("reduce_other_one", split(q, g_b, g_rb))
    g_rb2 = over_dp(g_bs2, 1)
    (in_both,) = after((in_both,), g_bs2)
    in_both = swap_cores(in_both)

    input_start, input_low = call(
        last_kernel, (s1, c1), (Far(tokens), Far(hidden_grad), in_both, both_gains),
        [far(tokens.shape, F32), sds((SEQ // 2, d), BF16)], "norm_back", 0,
        [keep_low, keep_low, keep_wide, sems(4 * NBLK)], mib=14,
    )
    up_r2, down_r2, g_rb2 = after((up_r2, down_r2, g_rb2), input_low)
    up_3, up_s3, down_3, down_s3, g_bx = adds(
        "reduce_mlp_two", split(q, up_a, up_ra, up_r2) + split(q, down_a, down_ra, down_r2) + [plain(BF16, q, (g_b2, 0), (g_rb2, 0))],
        leave=True,
    )
    up_r3, down_r3 = over_dp(up_s3, 1), over_dp(down_s3, 0)
    g_rx = over_x(g_bx)
    (input_low,) = after((input_low,), g_bx)
    input_one = over_x(input_low)
    (g_ra,) = after((g_ra,), g_bx)
    g_a2, g_as2 = adds("reduce_own_one", split(q, g_a, g_ra))
    g_ra2 = over_dp(g_as2, 1)
    last = q // 2
    up_r3, down_r3 = after((up_r3, down_r3), g_as2)
    mlp_4, mlp_s4 = adds(
        "reduce_mlp_three", [
            side_by_side(dtype, last, start, (up_3, up_r3), (down_3, down_r3)) for dtype, start in ((F32, 0), (BF16, last))
        ]
    )
    mlp_r4 = over_dp(mlp_s4, natural[2])
    block_both = jnp.concatenate(after((block_low, block_one), mlp_s4))
    block_both = swap_cores(jnp.stack([block_both, block_both]))
    (block_out,) = call(
        place_kernel, (s1,), (block_both,), [sds(tokens.shape, BF16)], "place", 0,
        in_specs=[VREF], out_specs=[pl.BlockSpec((SEQ // 2, d), lambda i, *_: (i, 0))], grid=(4,),
    )
    g_ra2, g_rx = after((g_ra2, g_rx), block_out)
    g_4, g_s4 = adds("reduce_own_two", split(last, g_a2, g_ra2, g_rx))
    g_r4 = over_dp(g_s4, natural[2])
    input_grad, input_one = after((input_start, input_one), g_s4)
    input_grad = fill(input_grad, input_one)
    mlp_r4, g_r4 = after((mlp_r4, g_r4), input_grad)
    mlp_5 = mlp_4 + mlp_r4.astype(F32)

    def other_steps(total):
        for bit in natural[3:]:
            count = total.shape[0] // 2
            got = over_dp(total[count:].astype(BF16), bit)
            total = total[:count] + got.astype(F32)
        return total[0]

    mlp_part, g_part = other_steps(mlp_5), other_steps(g_4 + g_r4.astype(F32))
    up_part, down_part = mlp_part[:, :units], mlp_part[:, units:]
    qkv_flat, out_part = g_part[:, : 3 * width], g_part[:, 3 * width :]
    start = me * piece
    w_rows = lax.dynamic_slice_in_dim(qkv_weight, start, piece, 0).reshape(piece, 3 * width).astype(F32)
    up_rows = lax.dynamic_slice_in_dim(up_weight, start, piece, 0).astype(F32)
    gains = jnp.stack([jnp.sum(w_rows * qkv_flat, 1), jnp.sum(up_rows * up_part, 1)])
    others = [lax.ppermute(gains, "tensor", [(i, i ^ m) for i in range(n_tensor)]) for m in (1, 2, 3)]
    gains = (gains + others[0]) + (others[1] + others[2])
    gains = gains / lax.dynamic_slice_in_dim(jnp.stack([attn_gain, mlp_gain]), start, piece, 1)
    qkv_part = qkv_flat.reshape(piece, 3, width)
    return (block_out, input_grad, gains[0], qkv_part, out_part.T, gains[1], up_part, down_part.T)


def solution(mesh):
    in_specs = (
        P("dp", None),
        P("dp"),
        P(),
        P(None, None, "tensor"),
        P("tensor", None),
        P(),
        P(None, "tensor"),
        P("tensor", None),
        P("dp", None),
    )
    out_specs = (
        P("dp", None),
        P("dp", None),
        P("dp"),
        P("dp", None, "tensor"),
        P("tensor", "dp"),
        P("dp"),
        P("dp", "tensor"),
        P("tensor", "dp"),
    )
    body = functools.partial(on_device, n_dp=mesh.shape["dp"], n_tensor=mesh.shape["tensor"])
    return jax.shard_map(body, mesh=mesh, in_specs=in_specs, out_specs=out_specs, check_vma=False)
```
